32 devices in a mesh: grp: 2 (over x), tp: 8 (over z, y), pd: 2 (over core).
Axes of the slice: x: 2, y: 2, z: 4, core: 2. Of those that a mesh axis runs over, the one named last changes fastest.
Arguments:
- kv_pages: bfloat16 [9984, 2, 16, 128], P(('grp', 'tp', 'pd')), parts along dimension 0, may hold values from -8 to 8
- page_list: int32 [4992], P('grp'), parts along dimension 0, may hold values from -1 to 2047, as said below
- block_tables: int32 [256, 128], P(('grp', 'tp')), parts along dimension 0, may hold values from 0 to 311, as said below
- lengths: int32 [32], P('grp'), parts along dimension 0, may hold values from 1 to 2048
- queries: bfloat16 [256, 2, 1024], P(('grp', 'tp')), parts along dimension 0, may hold values from -8 to 8
- fresh_kv: bfloat16 [256, 2, 2, 128], P(('grp', 'tp')), parts along dimension 0, may hold values from -8 to 8
- stream: bfloat16 [64, 8192], P('grp', ('tp', 'pd')), parts along dimension 0, may hold values from -6 to 6
- out_proj: bfloat16 [8192, 8192], P(('tp', 'pd')), may hold values from -0.0625 to 0.0625
- norm_gain: float32 [8192], replicated, may hold values from 0.5 to 1.5
- gate_weight: bfloat16 [8192, 16384], P(None, ('tp', 'pd')), may hold values from -0.0625 to 0.0625
- up_weight: bfloat16 [8192, 16384], P(None, ('tp', 'pd')), may hold values from -0.0625 to 0.0625
- down_weight: bfloat16 [16384, 8192], P(('tp', 'pd')), may hold values from -0.046875 to 0.046875
Outputs:
- kv_after: bfloat16 [9984, 2, 16, 128], P(('grp', 'tp', 'pd')), parts along dimension 0
- layer_out: bfloat16 [64, 8192], P('grp', ('tp', 'pd')), parts along dimension 0
The draws below stay inside these ranges and needn't reach their ends.
There are 2 independent parts, one for each index of `grp`. The reference program is written for one: setup_inputs(seed, part) draws one part's arguments, and reference() takes and returns one part's arrays. A program takes and returns all parts, laid end to end along the dimension named above; an argument that names none is the same for every part. Nothing has to cross between parts.
Inputs may be any that keep to these rules, and one draw needn't show every extreme that they name: `page_list`: entry t * 312 + i belongs to slot i of prefill member t: -1 if the page stays, else d * 256 + s, sending it to slot 56 + s of decode member d. Every arrival slot of every decode member receives exactly one page, and every prefill member sends exactly 32 pages to every decode member. `block_tables`: entry h * 16 + r lists in token order the slots of row r's pages for KV head h in the pool of decode member h + r // 16; entries past the row's pages are valid slots.
All inputs are finite; a program needn't handle non-finite values.
Results may differ from the reference program's by a relative error of at most 0.006.
Values may be sent and summed in bfloat16 or wider, within the bound.
No kernel may reach another device: no remote copies, remote signals or barrier semaphores. Data moves between devices by JAX's collectives and lax.ppermute only.
A program may use at most 192 MiB of HBM per device.

```python
import math
import jax
import jax.numpy as jnp
from jax import lax

D = 8192
FF = 16384
HD = 128
KVH = 8
GQ = 8
PAGE = 16
STEPS = 2
REQ_DEV = 2
NEWP = 128
RPD = 16
RESP = 4
ROWS = 16
TOK = 32
POOL = 312
N_TP = 8
N_PD = 2


def layout(key):
    key = jax.random.fold_in(key, 101)
    key_rank, key_len, key_res, key_arr, key_src = jax.random.split(key, 5)
    groups = N_TP // KVH
    arrive = REQ_DEV * NEWP
    resident = POOL - arrive
    shuffle = jax.vmap(lambda subkey: jax.random.permutation(subkey, RPD))(jax.random.split(key_rank, groups))
    row_rank = jnp.argsort(shuffle, axis=1).astype(jnp.int32)
    resident_len = jax.random.randint(key_len, (groups, RPD), 1, RESP * PAGE + 1)
    lengths = jnp.where(row_rank < REQ_DEV, NEWP * PAGE, resident_len).reshape(groups * RPD).astype(jnp.int32)
    res_perm = jax.vmap(lambda subkey: jax.random.permutation(subkey, resident))(jax.random.split(key_res, N_TP)).astype(jnp.int32)
    arr_perm = jax.vmap(lambda subkey: jax.random.permutation(subkey, arrive))(jax.random.split(key_arr, N_TP)).astype(jnp.int32)
    member_rank = row_rank[jnp.arange(N_TP) % groups]
    page_ids = jnp.arange(NEWP)
    fresh_index = jnp.minimum(member_rank, REQ_DEV - 1)[:, :, None] * NEWP + page_ids
    fresh_slot = resident + jnp.take_along_axis(arr_perm, fresh_index.reshape(N_TP, -1), axis=1).reshape(N_TP, RPD, NEWP)
    old_index = (jnp.maximum(member_rank - REQ_DEV, 0)[:, :, None] * RESP + page_ids) % resident
    old_slot = jnp.take_along_axis(res_perm, old_index.reshape(N_TP, -1), axis=1).reshape(N_TP, RPD, NEWP)
    tables = jnp.where((member_rank < REQ_DEV)[:, :, None], fresh_slot, old_slot).reshape(N_TP * RPD, NEWP).astype(jnp.int32)
    per_member = NEWP // N_TP
    index = jnp.arange(arrive)
    request = index // (KVH * per_member)
    kv_head = index // per_member % KVH
    offset = index % per_member
    target = kv_head * groups + request // REQ_DEV
    source = jnp.arange(N_TP)[:, None]
    page_no = source * per_member + offset[None, :]
    dest_slot = arr_perm[target[None, :], (request % REQ_DEV)[None, :] * NEWP + page_no]
    encoded = (target[None, :] * arrive + dest_slot).astype(jnp.int32)
    placing = jax.vmap(lambda subkey: jax.random.permutation(subkey, POOL))(jax.random.split(key_src, N_TP))[:, :arrive]
    page_map = jnp.full((N_TP, POOL), -1, jnp.int32).at[source, placing].set(encoded).reshape(N_TP * POOL)
    return (page_map, tables, lengths)


def draw_page_list(key, part):
    return layout(key)[0]


def draw_block_tables(key, part):
    return layout(key)[1]


def draw_lengths(key, part):
    return layout(key)[2]


def draw_kv_pages(key, part):
    key = jax.random.fold_in(key, 1)
    key_a, key_b = jax.random.split(key)
    shape = (POOL * N_TP * N_PD, PAGE, HD)
    keys_part = jax.random.truncated_normal(key_a, -4.0, 4.0, shape)
    values_part = 2.0 * jax.random.truncated_normal(key_b, -3.5, 3.5, shape)
    return jnp.stack([keys_part, values_part], axis=1).astype(jnp.bfloat16)


def draw_fresh_kv(key, part):
    key = jax.random.fold_in(key, 3)
    key_a, key_b = jax.random.split(key)
    shape = (KVH * ROWS, STEPS, HD)
    keys_part = jax.random.truncated_normal(key_a, -4.0, 4.0, shape)
    values_part = 2.0 * jax.random.truncated_normal(key_b, -3.5, 3.5, shape)
    return jnp.stack([keys_part, values_part], axis=2).astype(jnp.bfloat16)


def draw_queries(key, part):
    key = jax.random.fold_in(key, 2)
    shape = (KVH * ROWS, STEPS, GQ, HD)
    values_out = 1.5 * jax.random.truncated_normal(key, -4.0, 4.0, shape)
    return values_out.reshape(KVH * ROWS, STEPS, GQ * HD).astype(jnp.bfloat16)


def block_levels(key, extent, shards, least, largest):
    def one(position, blocks):
        draws = jax.random.uniform(jax.random.fold_in(jax.random.fold_in(key, 6), position), (blocks,), jnp.float32, least / len(shards), largest / len(shards))
        return jnp.repeat(jnp.exp(draws), extent[position] // blocks).reshape((-1,) + (1,) * (len(extent) - position - 1))

    factor_of = one(*shards[0])
    for cut in shards[1:]:
        factor_of = factor_of * one(*cut)
    return factor_of


def centred(own_key, extent, width, reach, cuts=(), kind=jnp.bfloat16):
    level = block_levels(own_key, extent, cuts, -0.22, 0.18) if cuts else 1.0
    array = jax.random.normal(own_key, extent, jnp.float32) * width * level
    return jnp.minimum(jnp.maximum(array, -reach), reach).astype(kind)


def setup_inputs(seed: int = 0, part: int = 0) -> dict:
    seeds = jax.random.split(jax.random.key(seed), 13)
    own_keys = jax.random.split(jax.random.fold_in(seeds[12], part), 13)
    kv_pages = draw_kv_pages(jax.random.fold_in(jax.random.fold_in(seeds[12], part), 71), part)
    page_list = draw_page_list(jax.random.fold_in(jax.random.fold_in(seeds[12], part), 71), part)
    block_tables = draw_block_tables(jax.random.fold_in(jax.random.fold_in(seeds[12], part), 71), part)
    lengths = draw_lengths(jax.random.fold_in(jax.random.fold_in(seeds[12], part), 71), part)
    queries = draw_queries(jax.random.fold_in(jax.random.fold_in(seeds[12], part), 71), part)
    fresh_kv = draw_fresh_kv(jax.random.fold_in(jax.random.fold_in(seeds[12], part), 71), part)
    stream = centred(own_keys[6], (TOK, D), 1.0, 6.0, ((1, 16),))
    out_proj = centred(seeds[7], (D, KVH * GQ * HD), (KVH * GQ * HD) ** -0.5, 0.0625, ((0, 16),))
    norm_gain = jnp.clip(1.0 + 0.1 * jax.random.normal(seeds[8], (D,), jnp.float32), 0.5, 1.5)
    gate_weight = centred(seeds[9], (D, FF), D ** -0.5, 0.0625, ((1, 16),))
    up_weight = centred(seeds[10], (D, FF), D ** -0.5, 0.0625, ((1, 16),))
    down_weight = centred(seeds[11], (FF, D), FF ** -0.5, 0.046875, ((0, 16),))
    return dict(kv_pages=kv_pages, page_list=page_list, block_tables=block_tables, lengths=lengths, queries=queries, fresh_kv=fresh_kv, stream=stream, out_proj=out_proj, norm_gain=norm_gain, gate_weight=gate_weight, up_weight=up_weight, down_weight=down_weight)


def attend(page_pool, tables, row_lengths, query_rows, fresh_rows):
    row_count = tables.shape[0]
    step_count = query_rows.shape[1]
    head_size = fresh_rows.shape[-1]
    picked = page_pool[tables]
    cache_keys = picked[:, :, 0].reshape(row_count, -1, head_size).astype(jnp.float32)
    cache_values = picked[:, :, 1].reshape(row_count, -1, head_size).astype(jnp.float32)
    queries_split = query_rows.reshape(row_count, step_count, -1, head_size).astype(jnp.float32)
    fresh_keys = fresh_rows[:, :, 0].astype(jnp.float32)
    fresh_values = fresh_rows[:, :, 1].astype(jnp.float32)
    score_scale = 1.0 / math.sqrt(head_size)
    cached = jnp.einsum('isjd,ind->isjn', queries_split, cache_keys) * score_scale
    latest = jnp.einsum('isjd,itd->isjt', queries_split, fresh_keys) * score_scale
    positions = jnp.arange(cache_keys.shape[1])
    cache_ok = (positions[None, :] < row_lengths[:, None])[:, None, None, :]
    step_ids = jnp.arange(step_count)
    fresh_ok = (step_ids[None, :] <= step_ids[:, None])[None, :, None, :]
    cached = jnp.where(cache_ok, cached, -jnp.inf)
    latest = jnp.where(fresh_ok, latest, -jnp.inf)
    row_max = jnp.maximum(lax.optimization_barrier(jnp.max(cached, axis=-1)), lax.optimization_barrier(jnp.max(latest, axis=-1)))[..., None]
    prob_cache = jnp.exp(cached - row_max)
    prob_fresh = jnp.exp(latest - row_max)
    denominator = lax.optimization_barrier(jnp.sum(prob_cache, axis=-1)) + lax.optimization_barrier(jnp.sum(prob_fresh, axis=-1))
    rounded_cache = prob_cache.astype(jnp.bfloat16).astype(jnp.float32)
    rounded_fresh = prob_fresh.astype(jnp.bfloat16).astype(jnp.float32)
    numerator = jnp.einsum('isjn,ind->isjd', rounded_cache, cache_values)
    numerator = numerator + jnp.einsum('isjt,itd->isjd', rounded_fresh, fresh_values)
    result = (numerator / denominator[..., None]).astype(jnp.bfloat16)
    return result.reshape(row_count, step_count, -1)

def reference(kv_pages, page_list, block_tables, lengths, queries, fresh_kv, stream, out_proj, norm_gain, gate_weight, up_weight, down_weight):
    groups = N_TP // KVH
    arrive = REQ_DEV * NEWP
    page_pool = kv_pages.reshape(N_TP, N_PD, POOL, 2, PAGE, HD)
    source = page_pool[:, 0].reshape(N_TP * POOL, 2, PAGE, HD)
    target = jnp.where(page_list >= 0, page_list, N_TP * arrive).astype(jnp.int32)
    landed = jnp.zeros((N_TP * arrive, 2, PAGE, HD), kv_pages.dtype).at[target].set(source, mode='drop')
    decode = page_pool[:, 1].at[:, POOL - arrive:].set(landed.reshape(N_TP, arrive, 2, PAGE, HD))
    kv_after = jnp.stack([page_pool[:, 0], decode], axis=1).reshape(kv_pages.shape)
    tables = block_tables.reshape(N_TP, RPD, NEWP)
    row_lengths = jnp.tile(lengths.reshape(groups, RPD), (KVH, 1))
    query_rows = queries.reshape(N_TP, RPD, STEPS, GQ * HD)
    fresh_rows = fresh_kv.reshape(N_TP, RPD, STEPS, 2, HD)
    attended = lax.map(lambda packed: attend(*packed), (decode, tables, row_lengths, query_rows, fresh_rows))
    attention = attended.reshape(KVH, groups, RPD, STEPS, GQ * HD).transpose(3, 1, 2, 0, 4).reshape(STEPS * ROWS, KVH * GQ * HD)
    projected = jnp.dot(attention, out_proj.T, preferred_element_type=jnp.float32)
    residual = (stream.astype(jnp.float32) + projected).astype(jnp.bfloat16)
    wide_rows = residual.astype(jnp.float32)
    normed = (wide_rows * lax.rsqrt(lax.optimization_barrier(jnp.mean(wide_rows * wide_rows, axis=1, keepdims=True)) + 1e-05) * norm_gain.astype(jnp.float32)).astype(jnp.bfloat16)
    gate_act = jnp.dot(normed, gate_weight, preferred_element_type=jnp.float32)
    up_act = jnp.dot(normed, up_weight, preferred_element_type=jnp.float32)
    hidden = (jax.nn.silu(gate_act) * up_act).astype(jnp.bfloat16)
    summed = jnp.dot(hidden, down_weight, preferred_element_type=jnp.float32)
    layer_out = (wide_rows + summed).astype(jnp.bfloat16)
    return (kv_after, layer_out)
```

```python
import functools
import math

import jax
import jax.numpy as jnp
from jax import lax
from jax.experimental import pallas as pl
from jax.experimental.pallas import tpu as pltpu
from jax.sharding import PartitionSpec as P

HD = 128
KVH = 8
GQ = 8
PAGE = 16
REQ_DEV = 2
NEWP = 128
ARRIVE = REQ_DEV * NEWP
MIB = 1024 * 1024
BOTH = ("tp", "pd")

VM = pl.BlockSpec(memory_space=pltpu.VMEM)
SM = pl.BlockSpec(memory_space=pltpu.SMEM)
ANY = pl.BlockSpec(memory_space=pl.ANY)


def pack_kernel(members, place, pages, pool, *refs):
    outs = refs[:members]
    packed, counts, sems = refs[members:]
    member, half = place[0], place[1]
    slots = pool.shape[0]
    per_peer = ARRIVE // members

    @pl.when(half == 0)
    def _():
        @pl.loop(0, members + 1)
        def _(i):
            counts[i] = 0

        @pl.loop(0, slots, unroll=8)
        def _(i):
            entry = pages[member * slots + i]
            target = entry // ARRIVE
            ahead = lax.rem(target - member + members, members)
            row = jnp.where(entry >= 0, ahead, members)
            count = counts[row]
            counts[row] = count + 1
            spot = jnp.where(entry >= 0, row * per_peer + count, ARRIVE)
            packed[spot] = pool[i]

        copies = [
            pltpu.make_async_copy(packed.at[pl.ds(k * per_peer, per_peer)], outs[k], sems.at[k])
            for k in range(members)
        ]
        for copy in copies:
            copy.start()
        for copy in copies:
            copy.wait()


def pack(place, pages, pool):
    members = lax.axis_size("tp")
    per_peer = ARRIVE // members
    shape = jax.ShapeDtypeStruct((per_peer, *pool.shape[1:]), pool.dtype)
    return pl.pallas_call(
        functools.partial(pack_kernel, members),
        out_shape=[shape] * members,
        in_specs=[SM, SM, VM],
        out_specs=[ANY] * members,
        scratch_shapes=[
            pltpu.VMEM((ARRIVE + 1, *pool.shape[1:]), pool.dtype),
            pltpu.SMEM((members + 1,), jnp.int32),
            pltpu.SemaphoreType.DMA((members,)),
        ],
        compiler_params=pltpu.CompilerParams(vmem_limit_bytes=16 * MIB),
        name="pack_pages",
    )(place, pages, pool)


def attend_kernel(members, place, landing, old_pool, bias, query, new_k, new_v, *refs):
    arrived = refs[:members]
    kv_out, att_out = refs[members : members + 2]
    pool, scores, sems = refs[members + 2 :]
    half = place[1]
    slots = pool.shape[0]
    resident = slots - ARRIVE
    per_peer = ARRIVE // members
    rows = bias.shape[0]
    count = query.shape[0]
    steps = count // (rows * GQ)

    @pl.when(half == 0)
    def _():
        copy = pltpu.make_async_copy(old_pool, kv_out, sems.at[0])
        copy.start()
        att_out[...] = jnp.zeros_like(att_out)
        copy.wait()

    @pl.when(half == 1)
    def _():
        copy = pltpu.make_async_copy(
            old_pool.at[pl.ds(0, resident)], pool.at[pl.ds(0, resident)], sems.at[0]
        )
        copy.start()
        for k in range(members):

            @pl.loop(0, per_peer, unroll=math.gcd(per_peer, 8))
            def _(c):
                pool[resident + landing[k * per_peer + c]] = arrived[k][c]

        copy.wait()
        copy_out = pltpu.make_async_copy(pool, kv_out, sems.at[1])
        copy_out.start()

        scale = 1.0 / math.sqrt(HD)
        q = query[...]
        nt = (((1,), (1,)), ((), ()))
        group = 24
        width = group * PAGE
        lanes = 128
        fresh = lax.dot_general(q, new_k[...], nt, preferred_element_type=jnp.float32) * scale
        q_id = lax.broadcasted_iota(jnp.int32, fresh.shape, 0)
        t_id = lax.broadcasted_iota(jnp.int32, fresh.shape, 1)
        allowed = (q_id % rows == t_id // steps) & (t_id % steps <= (q_id // rows) % steps)
        fresh = jnp.where(allowed, fresh, -jnp.inf)
        peak = fresh
        for c in range(slots // group):
            keys = pool[c * group : (c + 1) * group, 0].reshape(width, HD)
            s = lax.dot_general(q, keys, nt, preferred_element_type=jnp.float32) * scale
            b = bias[:, c * width : (c + 1) * width]
            s = (s.reshape(count // rows, rows, width) + b[None]).reshape(count, width)
            scores[:, c * width : (c + 1) * width] = s
            for i in range(width // lanes):
                peak = jnp.maximum(peak, s[:, i * lanes : (i + 1) * lanes])
        top = jnp.max(peak, axis=1, keepdims=True)
        p = jnp.exp(fresh - top)
        total = p
        acc = jnp.dot(p.astype(jnp.bfloat16), new_v[...], preferred_element_type=jnp.float32)
        for c in range(slots // group):
            p = jnp.exp(scores[:, c * width : (c + 1) * width] - top)
            for i in range(width // lanes):
                total = total + p[:, i * lanes : (i + 1) * lanes]
            values = pool[c * group : (c + 1) * group, 1].reshape(width, HD)
            acc = acc + jnp.dot(p.astype(jnp.bfloat16), values, preferred_element_type=jnp.float32)
        out = (acc / jnp.sum(total, axis=1, keepdims=True)).astype(jnp.bfloat16)
        tokens = rows * steps
        for j in range(GQ):
            att_out[:, j * HD : (j + 1) * HD] = out[j * tokens : (j + 1) * tokens]
        copy_out.wait()


def place_and_attend(place, landing, old_pool, bias, query, new_k, new_v, arrived):
    members = len(arrived)
    slots = old_pool.shape[0]
    rows = bias.shape[0]
    count = query.shape[0]
    tokens = count // GQ
    return pl.pallas_call(
        functools.partial(attend_kernel, members),
        out_shape=[
            jax.ShapeDtypeStruct(old_pool.shape, old_pool.dtype),
            jax.ShapeDtypeStruct((tokens, GQ * HD), jnp.bfloat16),
        ],
        in_specs=[SM, SM, ANY, VM, VM, VM, VM] + [VM] * members,
        out_specs=[ANY, VM],
        scratch_shapes=[
            pltpu.VMEM(old_pool.shape, old_pool.dtype),
            pltpu.VMEM((count, slots * PAGE), jnp.float32),
            pltpu.SemaphoreType.DMA((2,)),
        ],
        compiler_params=pltpu.CompilerParams(vmem_limit_bytes=28 * MIB),
        name="place_attend",
    )(place, landing, old_pool, bias, query, new_k, new_v, *arrived)


def table_bias(tables, row_lengths, slots):
    pages = jnp.arange(tables.shape[1])
    whole_pages = row_lengths // PAGE
    hit = tables[:, :, None] == jnp.arange(slots)[None, None, :]
    whole = jnp.sum(
        (hit & (pages[None, :, None] < whole_pages[:, None, None])).astype(jnp.float32), axis=1
    )
    part = jnp.sum(
        (hit & (pages[None, :, None] == whole_pages[:, None, None])).astype(jnp.float32), axis=1
    )
    inside = (jnp.arange(PAGE)[None, :] < (row_lengths % PAGE)[:, None]).astype(jnp.float32)
    times = whole[:, :, None] + part[:, :, None] * inside[:, None, :]
    return jnp.log(times).reshape(tables.shape[0], slots * PAGE)


def landing_slots(slots_from, member, per_peer):
    wanted = (slots_from >= 0) & (slots_from // ARRIVE == member)
    ahead = jnp.cumsum(wanted.astype(jnp.int32), axis=1) - 1
    pick = wanted[:, None, :] & (ahead[:, None, :] == jnp.arange(per_peer)[None, :, None])
    return jnp.sum(jnp.where(pick, (slots_from % ARRIVE)[:, None, :], 0), axis=2)


def project_kernel(members, groups, place, weight, stream, here, there, res_out):
    member, half = place[0], place[1]
    width = GQ * HD
    tokens = here.shape[1]

    def run(source):
        sums = [stream[g * tokens : (g + 1) * tokens].astype(jnp.float32) for g in range(groups)]
        if groups > 1:
            res_f32 = jnp.stack(sums)
        else:
            res_f32 = sums[0]
        for k in range(members):
            owner = lax.rem(member - k + members, members)
            head = pl.multiple_of(owner // groups * width, width)
            part = lax.dot_general(
                source[k],
                weight[:, pl.ds(head, width)],
                (((1,), (1,)), ((), ())),
                preferred_element_type=jnp.float32,
            )
            if groups > 1:
                mine = lax.broadcasted_iota(jnp.int32, res_f32.shape, 0) == lax.rem(owner, groups)
                res_f32 = res_f32 + jnp.where(mine, part[None], 0.0)
            else:
                res_f32 = res_f32 + part
        res_out[...] = res_f32.reshape(res_out.shape).astype(res_out.dtype)

    @pl.when(half == 1)
    def _():
        run(here)

    @pl.when(half == 0)
    def _():
        run(there)


def project(place, weight, stream, here, there, groups):
    members = here.shape[0]
    return pl.pallas_call(
        functools.partial(project_kernel, members, groups),
        out_shape=jax.ShapeDtypeStruct(stream.shape, jnp.bfloat16),
        in_specs=[SM, VM, VM, VM, VM],
        out_specs=VM,
        compiler_params=pltpu.CompilerParams(vmem_limit_bytes=24 * MIB),
        name="out_projection",
    )(place, weight, stream, here, there)


def ffn_kernel(place, mine, sibling, gain, gate, up, down, own_out, other_out, *scratch):
    gate_buf, up_buf, down_buf, normed, gate_sem, up_sem, down_sem = scratch
    half = place[1]
    members, tokens, width = mine.shape
    features = gate.shape[0]
    hidden_count = gate.shape[1]
    blocks = 2 * members
    order = [(t, p) for p in range(2) for t in range(members)]

    def rows_of(t, p):
        which = half if p == 0 else 1 - half
        return pl.ds(pl.multiple_of((t * 2 + which) * width, width), width)

    up_copies, gate_copies, down_copies = [], [], []
    for i, (t, p) in enumerate(order):
        rows = rows_of(t, p)
        gate_copies.append(pltpu.make_async_copy(gate.at[rows], gate_buf.at[rows], gate_sem.at[i]))
        up_copies.append(pltpu.make_async_copy(up.at[rows], up_buf.at[rows], up_sem.at[i]))
        gate_copies[-1].start()
        up_copies[-1].start()
    for t in range(members):
        cols = pl.ds(t * 2 * width, 2 * width)
        down_copies.append(
            pltpu.make_async_copy(down.at[:, cols], down_buf.at[:, cols], down_sem.at[t])
        )
        down_copies[-1].start()

    square = jnp.zeros((tokens, width), jnp.float32)
    for block in (mine, sibling):
        for t in range(members):
            x = block[t].astype(jnp.float32)
            square = square + x * x
    factor = lax.rsqrt(jnp.sum(square, axis=1, keepdims=True) / features + 1e-05)
    gate_act = jnp.zeros((tokens, hidden_count), jnp.float32)
    up_act = jnp.zeros((tokens, hidden_count), jnp.float32)
    for i, (t, p) in enumerate(order):
        rows = rows_of(t, p)
        x = (mine if p == 0 else sibling)[t].astype(jnp.float32)
        which = half if p == 0 else 1 - half
        g = gain[pl.ds(t * 2 + which, 1), :]
        n = (x * factor * g).astype(jnp.bfloat16)
        gate_copies[i].wait()
        gate_act = gate_act + jnp.dot(n, gate_buf[rows, :], preferred_element_type=jnp.float32)
        up_copies[i].wait()
        up_act = up_act + jnp.dot(n, up_buf[rows, :], preferred_element_type=jnp.float32)
    hidden = (gate_act / (1.0 + jnp.exp(-gate_act)) * up_act).astype(jnp.bfloat16)
    for t in range(members):
        down_copies[t].wait()
        part = jnp.dot(
            hidden,
            down_buf[:, 2 * t * width : 2 * (t + 1) * width],
            preferred_element_type=jnp.float32,
        )
        first, second = part[:, :width], part[:, width:]
        own_out[t] = jnp.where(half == 0, first, second)
        other_out[t] = jnp.where(half == 0, second, first).astype(jnp.bfloat16)


def feed_forward(place, mine, sibling, gain, gate, up, down):
    members, tokens, width = mine.shape
    blocks = 2 * members
    return pl.pallas_call(
        ffn_kernel,
        out_shape=[
            jax.ShapeDtypeStruct(mine.shape, jnp.float32),
            jax.ShapeDtypeStruct(mine.shape, jnp.bfloat16),
        ],
        in_specs=[SM, VM, VM, VM, ANY, ANY, ANY],
        out_specs=[VM, VM],
        scratch_shapes=[
            pltpu.VMEM(gate.shape, gate.dtype),
            pltpu.VMEM(up.shape, up.dtype),
            pltpu.VMEM(down.shape, down.dtype),
            pltpu.VMEM((8, 128), jnp.float32),
            pltpu.SemaphoreType.DMA((blocks,)),
            pltpu.SemaphoreType.DMA((blocks,)),
            pltpu.SemaphoreType.DMA((members,)),
        ],
        compiler_params=pltpu.CompilerParams(vmem_limit_bytes=56 * MIB),
        name="feed_forward",
    )(place, mine, sibling, gain.reshape(blocks, width), gate, up, down)


def local(
    kv_pages,
    page_list,
    block_tables,
    lengths,
    queries,
    fresh_kv,
    stream,
    out_proj,
    norm_gain,
    gate_weight,
    up_weight,
    down_weight,
):
    members = lax.axis_size("tp")
    member = lax.axis_index("tp")
    half = lax.axis_index("pd")
    place = jnp.stack([member, half]).astype(jnp.int32)
    slots = kv_pages.shape[0]
    per_peer = ARRIVE // members
    groups = members // KVH
    rows = block_tables.shape[0]
    steps = queries.shape[1]
    tokens = rows * steps

    def ahead(x, k, from_half, to_half):
        route = [
            (2 * t + from_half, 2 * ((t + k) % members) + to_half) for t in range(members)
        ]
        return lax.ppermute(x, BOTH, route)

    def swap(x):
        return lax.ppermute(x, "pd", [(0, 1), (1, 0)])

    outgoing = pack(place, page_list, kv_pages)
    arrived = [ahead(outgoing[k], k, 0, 1) for k in range(members)]

    behind = (member - jnp.arange(members)) % members
    landing = landing_slots(page_list.reshape(members, slots)[behind], member, per_peer)
    row_lengths = lax.dynamic_slice_in_dim(lengths, member % groups * rows, rows)
    bias = table_bias(block_tables, row_lengths, slots)
    query = queries.reshape(rows, steps, GQ, HD).transpose(2, 1, 0, 3).reshape(GQ * tokens, HD)
    padding = ((0, -tokens % 128), (0, 0))
    new_k = jnp.pad(fresh_kv[:, :, 0].reshape(tokens, HD), padding)
    new_v = jnp.pad(fresh_kv[:, :, 1].reshape(tokens, HD), padding)

    kv_after, attended = place_and_attend(
        place, landing.reshape(-1), kv_pages, bias, query, new_k, new_v, arrived
    )

    pieces = [attended] + [ahead(attended, k, 1, 1) for k in range(1, members)]
    here = jnp.stack(pieces)
    there = lax.ppermute(here, "pd", [(1, 0)])

    inner = stream.reshape(steps, groups, rows, -1).transpose(1, 0, 2, 3).reshape(stream.shape)
    residual = project(place, out_proj, inner, here, there, groups)

    spread = jnp.broadcast_to(residual[None], (members, *residual.shape))
    mine = lax.all_to_all(spread, "tp", split_axis=0, concat_axis=0)
    sibling = swap(mine)
    own, other = feed_forward(
        place, mine, sibling, norm_gain, gate_weight, up_weight, down_weight
    )
    summed = (own + swap(other).astype(jnp.float32)).astype(jnp.bfloat16)
    shares = lax.all_to_all(summed, "tp", split_axis=0, concat_axis=0)
    layer = residual.astype(jnp.float32) + jnp.sum(shares.astype(jnp.float32), axis=0)
    layer_out = (
        layer.astype(jnp.bfloat16)
        .reshape(groups, steps, rows, -1)
        .transpose(1, 0, 2, 3)
        .reshape(stream.shape)
    )
    return (kv_after, layer_out)


def solution(mesh):
    return jax.shard_map(
        local,
        mesh=mesh,
        in_specs=(
            P(("grp", "tp", "pd"), None, None, None),
            P("grp"),
            P(("grp", "tp"), None),
            P("grp"),
            P(("grp", "tp"), None, None),
            P(("grp", "tp"), None, None, None),
            P("grp", ("tp", "pd")),
            P(("tp", "pd"), None),
            P(),
            P(None, ("tp", "pd")),
            P(None, ("tp", "pd")),
            P(("tp", "pd"), None),
        ),
        out_specs=(P(("grp", "tp", "pd"), None, None, None), P("grp", ("tp", "pd"))),
        check_vma=False,
    )
```

```python
import functools
import math

import jax
import jax.numpy as jnp
from jax import lax
from jax.experimental import pallas as pl
from jax.experimental.pallas import tpu as pltpu
from jax.sharding import PartitionSpec as P

HD = 128
KVH = 8
GQ = 8
PAGE = 16
REQ_DEV = 2
NEWP = 128
ARRIVE = REQ_DEV * NEWP
MIB = 1024 * 1024
BOTH = ("tp", "pd")

VM = pl.BlockSpec(memory_space=pltpu.VMEM)
SM = pl.BlockSpec(memory_space=pltpu.SMEM)
ANY = pl.BlockSpec(memory_space=pl.ANY)
HBM = pl.BlockSpec(memory_space=pltpu.HBM)


def in_vmem(x):
    return pltpu.with_memory_space_constraint(x, pltpu.VMEM)


def in_hbm(x):
    return pltpu.with_memory_space_constraint(x, pltpu.HBM)


def pack_kernel(members, place, pages, pool, *refs):
    outs = refs[:members]
    packed, held, own, counts, sems, load_sems = refs[members:]
    member, half = place[0], place[1]
    slots = pool.shape[0]
    per_peer = ARRIVE // members
    parts = 4
    step = slots // parts

    @pl.when(half == 0)
    def _():
        own_copy = pltpu.make_async_copy(pages, own, load_sems.at[parts])
        own_copy.start()
        loads = []
        for i in range(parts):
            window = pl.ds(i * step, step)
            loads.append(
                pltpu.make_async_copy(pool.at[window], held.at[window], load_sems.at[i])
            )
            loads[-1].start()
        own_copy.wait()
        start = member * slots

        if members <= 8:
            carry = (jnp.int32(0), jnp.int32(0))
            for i in range(parts):
                loads[i].wait()

                def body(j, words, base=i * step):
                    low, high = words
                    entry = own[start + base + j]
                    ahead = lax.rem((entry >> 8) - member + members, members)
                    leaves = entry >= 0
                    shift = (ahead & 3) * 8
                    is_low = ahead < 4
                    count = (jnp.where(is_low, low, high) >> shift) & 255
                    one = jnp.where(leaves, jnp.int32(1) << shift, 0)
                    packed[jnp.where(leaves, ahead * per_peer + count, ARRIVE)] = held[base + j]
                    return (
                        low + jnp.where(is_low, one, 0),
                        high + jnp.where(is_low, 0, one),
                    )

                carry = lax.fori_loop(0, step, body, carry, unroll=6)
        else:
            for i in range(parts):
                loads[i].wait()

            @pl.loop(0, members + 1)
            def _(i):
                counts[i] = 0

            @pl.loop(0, slots)
            def _(i):
                entry = own[start + i]
                ahead = lax.rem((entry >> 8) - member + members, members)
                row = jnp.where(entry >= 0, ahead, members)
                count = counts[row]
                counts[row] = count + 1
                packed[jnp.where(entry >= 0, row * per_peer + count, ARRIVE)] = held[i]

        copies = [
            pltpu.make_async_copy(packed.at[pl.ds(k * per_peer, per_peer)], outs[k], sems.at[k])
            for k in range(members)
        ]
        for copy in copies:
            copy.start()
        for copy in copies:
            copy.wait()


def pack(place, pages, pool):
    members = lax.axis_size("tp")
    per_peer = ARRIVE // members
    shape = jax.ShapeDtypeStruct((per_peer, *pool.shape[1:]), pool.dtype)
    return pl.pallas_call(
        functools.partial(pack_kernel, members),
        out_shape=[shape] * members,
        in_specs=[SM, HBM, HBM],
        out_specs=[ANY] * members,
        scratch_shapes=[
            pltpu.VMEM((ARRIVE + 1, *pool.shape[1:]), pool.dtype),
            pltpu.VMEM(pool.shape, pool.dtype),
            pltpu.SMEM(pages.shape, jnp.int32),
            pltpu.SMEM((members + 1,), jnp.int32),
            pltpu.SemaphoreType.DMA((members,)),
            pltpu.SemaphoreType.DMA((5,)),
        ],
        compiler_params=pltpu.CompilerParams(vmem_limit_bytes=61 * MIB),
        name="pack_pages",
    )(place, in_hbm(pages), in_hbm(pool))


def hold_kernel(after, *refs):
    count = (len(refs) - 2) // 2
    sources, copies_out = refs[:count], refs[count : 2 * count]
    mark, sems = refs[2 * count :]
    copies = [
        pltpu.make_async_copy(sources[i], copies_out[i], sems.at[i]) for i in range(count)
    ]
    for copy in copies:
        copy.start()
    mark[...] = jnp.zeros_like(mark)
    for copy in copies:
        copy.wait()


def hold(after, weights):
    moved = sum(w.size * w.dtype.itemsize for w in weights)
    return pl.pallas_call(
        hold_kernel,
        out_shape=[pltpu.VMEM(w.shape, w.dtype) for w in weights]
        + [jax.ShapeDtypeStruct((8, 128), jnp.float32)],
        in_specs=[ANY] + [HBM] * len(weights),
        out_specs=[VM] * (len(weights) + 1),
        scratch_shapes=[pltpu.SemaphoreType.DMA((len(weights),))],
        compiler_params=pltpu.CompilerParams(vmem_limit_bytes=2 * MIB),
        cost_estimate=pl.CostEstimate(flops=0, bytes_accessed=moved, transcendentals=0),
        name="hold_weights",
    )(after, *[in_hbm(w) for w in weights])


def attend_kernel(members, place, landing, mark, old_pool, bias, query, new_k, new_v, *refs):
    arrived = refs[:members]
    kv_out, att_low, att_high = refs[members : members + 3]
    pool, scores, sems = refs[members + 3 :]
    half = place[1]
    slots = pool.shape[0]
    resident = slots - ARRIVE
    per_peer = ARRIVE // members
    rows = bias.shape[0]
    count = query.shape[0]
    steps = count // (rows * GQ)

    @pl.when(half == 0)
    def _():
        copy = pltpu.make_async_copy(old_pool, kv_out, sems.at[0])
        copy.start()
        att_low[...] = jnp.zeros_like(att_low)
        att_high[...] = jnp.zeros_like(att_high)
        copy.wait()

    @pl.when(half == 1)
    def _():
        copy = pltpu.make_async_copy(
            old_pool.at[pl.ds(0, resident)], pool.at[pl.ds(0, resident)], sems.at[0]
        )
        copy.start()
        for k in range(members):

            @pl.loop(0, per_peer, unroll=math.gcd(per_peer, 8))
            def _(c):
                pool[resident + landing[k * per_peer + c]] = arrived[k][c]

        copy.wait()
        copy_out = pltpu.make_async_copy(pool, kv_out, sems.at[1])
        copy_out.start()

        scale = 1.0 / math.sqrt(HD)
        q = query[...]
        nt = (((1,), (1,)), ((), ()))
        group = 24
        width = group * PAGE
        lanes = 128
        fresh = lax.dot_general(q, new_k[...], nt, preferred_element_type=jnp.float32) * scale
        q_id = lax.broadcasted_iota(jnp.int32, fresh.shape, 0)
        t_id = lax.broadcasted_iota(jnp.int32, fresh.shape, 1)
        allowed = (q_id % rows == t_id // steps) & (t_id % steps <= (q_id // rows) % steps)
        fresh = jnp.where(allowed, fresh, -jnp.inf)
        peak = fresh
        for c in range(slots // group):
            keys = pool[c * group : (c + 1) * group, 0].reshape(width, HD)
            s = lax.dot_general(q, keys, nt, preferred_element_type=jnp.float32) * scale
            b = bias[:, c * width : (c + 1) * width]
            s = (s.reshape(count // rows, rows, width) + b[None]).reshape(count, width)
            scores[:, c * width : (c + 1) * width] = s
            for i in range(width // lanes):
                peak = jnp.maximum(peak, s[:, i * lanes : (i + 1) * lanes])
        top = jnp.max(peak, axis=1, keepdims=True)
        p = jnp.exp(fresh - top)
        total = p
        acc = jnp.dot(p.astype(jnp.bfloat16), new_v[...], preferred_element_type=jnp.float32)
        for c in range(slots // group):
            p = jnp.exp(scores[:, c * width : (c + 1) * width] - top)
            for i in range(width // lanes):
                total = total + p[:, i * lanes : (i + 1) * lanes]
            values = pool[c * group : (c + 1) * group, 1].reshape(width, HD)
            acc = acc + jnp.dot(p.astype(jnp.bfloat16), values, preferred_element_type=jnp.float32)
        out = (acc / jnp.sum(total, axis=1, keepdims=True)).astype(jnp.bfloat16)
        tokens = rows * steps
        for j in range(GQ // 2):
            att_low[:, j * HD : (j + 1) * HD] = out[j * tokens : (j + 1) * tokens]
            other = j + GQ // 2
            att_high[:, j * HD : (j + 1) * HD] = out[other * tokens : (other + 1) * tokens]
        copy_out.wait()


def place_and_attend(place, landing, mark, old_pool, bias, query, new_k, new_v, arrived):
    members = len(arrived)
    slots = old_pool.shape[0]
    rows = bias.shape[0]
    count = query.shape[0]
    tokens = count // GQ
    return pl.pallas_call(
        functools.partial(attend_kernel, members),
        out_shape=[
            jax.ShapeDtypeStruct(old_pool.shape, old_pool.dtype),
            jax.ShapeDtypeStruct((tokens, GQ * HD // 2), jnp.bfloat16),
            jax.ShapeDtypeStruct((tokens, GQ * HD // 2), jnp.bfloat16),
        ],
        in_specs=[SM, SM, ANY, HBM, VM, VM, VM, VM] + [VM] * members,
        out_specs=[HBM, VM, VM],
        scratch_shapes=[
            pltpu.VMEM(old_pool.shape, old_pool.dtype),
            pltpu.VMEM((count, slots * PAGE), jnp.float32),
            pltpu.SemaphoreType.DMA((2,)),
        ],
        compiler_params=pltpu.CompilerParams(vmem_limit_bytes=9 * MIB),
        name="place_attend",
    )(place, landing, mark, in_hbm(old_pool), bias, query, new_k, new_v, *arrived)


def table_bias(tables, row_lengths, slots):
    pages = jnp.arange(tables.shape[1])
    whole_pages = row_lengths // PAGE
    hit = tables[:, :, None] == jnp.arange(slots)[None, None, :]
    whole = jnp.sum(
        (hit & (pages[None, :, None] < whole_pages[:, None, None])).astype(jnp.float32), axis=1
    )
    part = jnp.sum(
        (hit & (pages[None, :, None] == whole_pages[:, None, None])).astype(jnp.float32), axis=1
    )
    inside = (jnp.arange(PAGE)[None, :] < (row_lengths % PAGE)[:, None]).astype(jnp.float32)
    times = whole[:, :, None] + part[:, :, None] * inside[:, None, :]
    return jnp.log(times).reshape(tables.shape[0], slots * PAGE)


def landing_slots(slots_from, member, per_peer):
    wanted = (slots_from >= 0) & (slots_from // ARRIVE == member)
    ahead = jnp.cumsum(wanted.astype(jnp.int32), axis=1) - 1
    pick = wanted[:, None, :] & (ahead[:, None, :] == jnp.arange(per_peer)[None, :, None])
    return jnp.sum(jnp.where(pick, (slots_from % ARRIVE)[:, None, :], 0), axis=2)


def project_kernel(groups, place, weight, stream, mine, sibling, res_out):
    half = place[1]
    members, tokens, width = mine.shape
    sums = [stream[g * tokens : (g + 1) * tokens].astype(jnp.float32) for g in range(groups)]
    for h in range(KVH):
        for g in range(groups):
            m = h * groups + g
            first = jnp.where(half == 0, mine[m], sibling[m])
            second = jnp.where(half == 0, sibling[m], mine[m])
            sums[g] = sums[g] + lax.dot_general(
                jnp.concatenate([first, second], axis=1),
                weight[:, 2 * h * width : 2 * (h + 1) * width],
                (((1,), (1,)), ((), ())),
                preferred_element_type=jnp.float32,
            )
    for g in range(groups):
        res_out[g * tokens : (g + 1) * tokens] = sums[g].astype(res_out.dtype)


def project(place, weight, stream, mine, sibling, groups):
    return pl.pallas_call(
        functools.partial(project_kernel, groups),
        out_shape=jax.ShapeDtypeStruct(stream.shape, jnp.bfloat16),
        in_specs=[SM, VM, VM, VM, VM],
        out_specs=VM,
        compiler_params=pltpu.CompilerParams(vmem_limit_bytes=4 * MIB),
        name="out_projection",
    )(place, in_vmem(weight), stream, mine, sibling)


def ffn_kernel(place, mine, sibling, gain, gate, up, down, own_out, other_out, *scratch):
    up_buf, down_buf, normed, gated, hidden, up_sem, down_sem = scratch
    half = place[1]
    members, tokens, width = mine.shape
    features, hidden_count = gate.shape
    tile = min(256, hidden_count)
    tiles = [slice(f * tile, (f + 1) * tile) for f in range(hidden_count // tile)]
    up_copies, down_copies = [], []
    for f, cols in enumerate(tiles):
        up_copies.append(
            pltpu.make_async_copy(up.at[:, cols], up_buf.at[:, cols], up_sem.at[f])
        )
        up_copies[-1].start()
    for t in range(members):
        cols = pl.ds(t * 2 * width, 2 * width)
        down_copies.append(
            pltpu.make_async_copy(down.at[:, cols], down_buf.at[:, cols], down_sem.at[t])
        )
        down_copies[-1].start()

    square = jnp.zeros((tokens, width), jnp.float32)
    for block in (mine, sibling):
        for t in range(members):
            x = block[t].astype(jnp.float32)
            square = square + x * x
    factor = lax.rsqrt(jnp.sum(square, axis=1, keepdims=True) / features + 1e-05)
    for t in range(members):
        first = jnp.where(half == 0, mine[t], sibling[t])
        second = jnp.where(half == 0, sibling[t], mine[t])
        x = jnp.concatenate([first, second], axis=1).astype(jnp.float32)
        n = x * factor * gain[t : t + 1, :]
        normed[:, 2 * t * width : 2 * (t + 1) * width] = n.astype(jnp.bfloat16)
    for cols in tiles:
        act = jnp.dot(normed[...], gate[:, cols], preferred_element_type=jnp.float32)
        gated[:, cols] = act / (1.0 + jnp.exp(-act))
    for f, cols in enumerate(tiles):
        up_copies[f].wait()
        act = jnp.dot(normed[...], up_buf[:, cols], preferred_element_type=jnp.float32)
        hidden[:, cols] = (gated[:, cols] * act).astype(jnp.bfloat16)
    for t in range(members):
        down_copies[t].wait()
        part = jnp.dot(
            hidden[...],
            down_buf[:, 2 * t * width : 2 * (t + 1) * width],
            preferred_element_type=jnp.float32,
        )
        first, second = part[:, :width], part[:, width:]
        own_out[t] = jnp.where(half == 0, first, second)
        other_out[t] = jnp.where(half == 0, second, first).astype(jnp.bfloat16)


def feed_forward(place, mine, sibling, gain, gate, up, down):
    members, tokens, width = mine.shape
    blocks = 2 * members
    hidden_count = gate.shape[1]
    return pl.pallas_call(
        ffn_kernel,
        out_shape=[
            jax.ShapeDtypeStruct(mine.shape, jnp.float32),
            jax.ShapeDtypeStruct(mine.shape, jnp.bfloat16),
        ],
        in_specs=[SM, VM, VM, VM, VM, HBM, HBM],
        out_specs=[VM, VM],
        scratch_shapes=[
            pltpu.VMEM(up.shape, up.dtype),
            pltpu.VMEM(down.shape, down.dtype),
            pltpu.VMEM((tokens, blocks * width), jnp.bfloat16),
            pltpu.VMEM((tokens, hidden_count), jnp.float32),
            pltpu.VMEM((tokens, hidden_count), jnp.bfloat16),
            pltpu.SemaphoreType.DMA((-(-hidden_count // 256),)),
            pltpu.SemaphoreType.DMA((members,)),
        ],
        compiler_params=pltpu.CompilerParams(vmem_limit_bytes=36 * MIB),
        name="feed_forward",
    )(
        place,
        mine,
        sibling,
        gain.reshape(members, 2 * width),
        in_vmem(gate),
        in_hbm(up),
        in_hbm(down),
    )


def local(
    kv_pages,
    page_list,
    block_tables,
    lengths,
    queries,
    fresh_kv,
    stream,
    out_proj,
    norm_gain,
    gate_weight,
    up_weight,
    down_weight,
):
    members = lax.axis_size("tp")
    member = lax.axis_index("tp")
    half = lax.axis_index("pd")
    place = jnp.stack([member, half]).astype(jnp.int32)
    slots = kv_pages.shape[0]
    per_peer = ARRIVE // members
    groups = members // KVH
    rows = block_tables.shape[0]
    steps = queries.shape[1]
    tokens = rows * steps

    def ahead(x, k, from_half, to_half):
        route = [
            (2 * t + from_half, 2 * ((t + k) % members) + to_half) for t in range(members)
        ]
        return lax.ppermute(x, BOTH, route)

    def swap(x):
        return lax.ppermute(x, "pd", [(0, 1), (1, 0)])

    outgoing = pack(place, page_list, kv_pages)
    arrived = [None] * members
    for k in sorted(range(members), key=lambda k: abs(k - members // 2)):
        arrived[k] = ahead(outgoing[k], k, 0, 1)

    out_proj, mark = hold(outgoing[0], (out_proj,))

    behind = (member - jnp.arange(members)) % members
    landing = landing_slots(page_list.reshape(members, slots)[behind], member, per_peer)
    row_lengths = lax.dynamic_slice_in_dim(lengths, member % groups * rows, rows)
    bias = table_bias(block_tables, row_lengths, slots)
    query = queries.reshape(rows, steps, GQ, HD).transpose(2, 1, 0, 3).reshape(GQ * tokens, HD)
    padding = ((0, -tokens % 128), (0, 0))
    new_k = jnp.pad(fresh_kv[:, :, 0].reshape(tokens, HD), padding)
    new_v = jnp.pad(fresh_kv[:, :, 1].reshape(tokens, HD), padding)

    kv_after, att_low, att_high = place_and_attend(
        place, landing.reshape(-1), mark, kv_pages, bias, query, new_k, new_v, arrived
    )

    def everywhere(x):
        spread = jnp.broadcast_to(x[None], (members, *x.shape))
        mine = lax.all_to_all(spread, "tp", split_axis=0, concat_axis=0)
        return mine, swap(mine)

    att_mine = jnp.where(half == 1, att_high, lax.ppermute(att_low, "pd", [(1, 0)]))
    here, there = everywhere(att_mine)

    inner = stream.reshape(steps, groups, rows, -1).transpose(1, 0, 2, 3).reshape(stream.shape)
    residual = project(place, out_proj, inner, here, there, groups)

    mine, sibling = everywhere(residual)
    own, other = feed_forward(
        place, mine, sibling, norm_gain, gate_weight, up_weight, down_weight
    )
    summed = (own + swap(other).astype(jnp.float32)).astype(jnp.bfloat16)
    shares = lax.all_to_all(summed, "tp", split_axis=0, concat_axis=0)
    layer = residual.astype(jnp.float32) + jnp.sum(shares.astype(jnp.float32), axis=0)
    layer_out = (
        layer.astype(jnp.bfloat16)
        .reshape(groups, steps, rows, -1)
        .transpose(1, 0, 2, 3)
        .reshape(stream.shape)
    )
    return (kv_after, layer_out)


def solution(mesh):
    return jax.shard_map(
        local,
        mesh=mesh,
        in_specs=(
            P(("grp", "tp", "pd"), None, None, None),
            P("grp"),
            P(("grp", "tp"), None),
            P("grp"),
            P(("grp", "tp"), None, None),
            P(("grp", "tp"), None, None, None),
            P("grp", ("tp", "pd")),
            P(("tp", "pd"), None),
            P(),
            P(None, ("tp", "pd")),
            P(None, ("tp", "pd")),
            P(("tp", "pd"), None),
        ),
        out_specs=(P(("grp", "tp", "pd"), None, None, None), P("grp", ("tp", "pd"))),
        check_vma=False,
    )
```

```python
import functools
import math

import jax
import jax.numpy as jnp
from jax import lax
from jax.experimental import pallas as pl
from jax.experimental.pallas import tpu as pltpu
from jax.sharding import PartitionSpec as P

HD = 128
KVH = 8
GQ = 8
PAGE = 16
REQ_DEV = 2
NEWP = 128
ARRIVE = REQ_DEV * NEWP
MIB = 1024 * 1024
BOTH = ("tp", "pd")
SPLIT = 2

VM = pl.BlockSpec(memory_space=pltpu.VMEM)
SM = pl.BlockSpec(memory_space=pltpu.SMEM)
ANY = pl.BlockSpec(memory_space=pl.ANY)
HBM = pl.BlockSpec(memory_space=pltpu.HBM)


def in_vmem(x):
    return pltpu.with_memory_space_constraint(x, pltpu.VMEM)


def in_hbm(x):
    return pltpu.with_memory_space_constraint(x, pltpu.HBM)


def pack_kernel(members, place, pages, pool, *refs):
    outs = refs[:members]
    packed, held, own, counts, sems, load_sems = refs[members:]
    member, half = place[0], place[1]
    slots = pool.shape[0]
    per_peer = ARRIVE // members
    parts = 4
    step = slots // parts

    @pl.when(half == 0)
    def _():
        own_copy = pltpu.make_async_copy(pages, own, load_sems.at[parts])
        own_copy.start()
        loads = []
        for i in range(parts):
            window = pl.ds(i * step, step)
            loads.append(
                pltpu.make_async_copy(pool.at[window], held.at[window], load_sems.at[i])
            )
            loads[-1].start()
        own_copy.wait()
        start = member * slots

        if members <= 8:
            carry = (jnp.int32(0), jnp.int32(0))
            for i in range(parts):
                loads[i].wait()

                def body(j, words, base=i * step):
                    low, high = words
                    entry = own[start + base + j]
                    ahead = lax.rem((entry >> 8) - member + members, members)
                    leaves = entry >= 0
                    shift = (ahead & 3) * 8
                    is_low = ahead < 4
                    count = (jnp.where(is_low, low, high) >> shift) & 255
                    one = jnp.where(leaves, jnp.int32(1) << shift, 0)
                    packed[jnp.where(leaves, ahead * per_peer + count, ARRIVE)] = held[base + j]
                    return (
                        low + jnp.where(is_low, one, 0),
                        high + jnp.where(is_low, 0, one),
                    )

                carry = lax.fori_loop(0, step, body, carry, unroll=6)
        else:
            for i in range(parts):
                loads[i].wait()

            @pl.loop(0, members + 1)
            def _(i):
                counts[i] = 0

            @pl.loop(0, slots)
            def _(i):
                entry = own[start + i]
                ahead = lax.rem((entry >> 8) - member + members, members)
                row = jnp.where(entry >= 0, ahead, members)
                count = counts[row]
                counts[row] = count + 1
                packed[jnp.where(entry >= 0, row * per_peer + count, ARRIVE)] = held[i]

        copies = [
            pltpu.make_async_copy(packed.at[pl.ds(k * per_peer, per_peer)], outs[k], sems.at[k])
            for k in range(members)
        ]
        for copy in copies:
            copy.start()
        for copy in copies:
            copy.wait()


def pack(place, pages, pool):
    members = lax.axis_size("tp")
    per_peer = ARRIVE // members
    shape = jax.ShapeDtypeStruct((per_peer, *pool.shape[1:]), pool.dtype)
    return pl.pallas_call(
        functools.partial(pack_kernel, members),
        out_shape=[shape] * members,
        in_specs=[SM, HBM, HBM],
        out_specs=[ANY] * members,
        scratch_shapes=[
            pltpu.VMEM((ARRIVE + 1, *pool.shape[1:]), pool.dtype),
            pltpu.VMEM(pool.shape, pool.dtype),
            pltpu.SMEM(pages.shape, jnp.int32),
            pltpu.SMEM((members + 1,), jnp.int32),
            pltpu.SemaphoreType.DMA((members,)),
            pltpu.SemaphoreType.DMA((5,)),
        ],
        compiler_params=pltpu.CompilerParams(vmem_limit_bytes=8 * MIB),
        name="pack_pages",
    )(place, in_hbm(pages), in_hbm(pool))


def prepare_kernel(count, parts, place, lens, lens_wide, table, listed, *refs):
    sources = refs[:count]
    held = refs[len(refs) - 5 - parts : -5]
    bias, landing, whole, part, sems = refs[-5:]
    copies = []
    for source in sources:
        done = 0
        while done < source.shape[0]:
            part_out = held[len(copies)]
            window = pl.ds(done, part_out.shape[0])
            copies.append(
                pltpu.make_async_copy(source.at[window], part_out, sems.at[len(copies)])
            )
            copies[-1].start()
            done += part_out.shape[0]

    member = place[0]
    entry = listed[...]
    members, lanes = entry.shape
    per_peer = ARRIVE // members
    wanted = (entry >= 0) & ((entry >> 8) == member)
    before = lax.broadcasted_iota(jnp.int32, (lanes, lanes), 0) < lax.broadcasted_iota(
        jnp.int32, (lanes, lanes), 1
    )
    rank = jnp.dot(
        jnp.where(wanted, 1.0, 0.0).astype(jnp.bfloat16),
        jnp.where(before, 1.0, 0.0).astype(jnp.bfloat16),
        preferred_element_type=jnp.float32,
    ).astype(jnp.int32)
    column = lax.broadcasted_iota(jnp.int32, landing.shape, 1)
    found = jnp.zeros(landing.shape, jnp.int32)
    for c in range(per_peer):
        slot = jnp.sum(jnp.where(wanted & (rank == c), entry & 255, 0), axis=1, keepdims=True)
        found = jnp.where(column == c, slot, found)
    landing[...] = found

    rows = bias.shape[0]
    pages = table.shape[0]
    wide = whole.shape[1]
    page_id = lax.broadcasted_iota(jnp.int32, (pages, wide), 0)
    slot_id = lax.broadcasted_iota(jnp.int32, (pages, wide), 1)
    for r in range(rows):
        full = lens[r] // PAGE
        hit = table[:, r : r + 1] == slot_id
        in_whole = jnp.where(hit & (page_id < full), 1.0, 0.0)
        in_part = jnp.where(hit & (page_id == full), 1.0, 0.0)
        whole[r : r + 1, :] = jnp.sum(in_whole, axis=0, keepdims=True)
        part[r : r + 1, :] = jnp.sum(in_part, axis=0, keepdims=True)
    whole_b = whole[...].astype(jnp.bfloat16)
    part_b = part[...].astype(jnp.bfloat16)
    lane = lax.broadcasted_iota(jnp.int32, (rows, 128), 1)
    inside = (lane % PAGE) < (lens_wide[...] % PAGE)
    per_block = 128 // PAGE
    slot_in = lax.broadcasted_iota(jnp.int32, (wide, 128), 0)
    lane_in = lax.broadcasted_iota(jnp.int32, (wide, 128), 1) // PAGE
    for i in range(bias.shape[1] // 128):
        expand = jnp.where(slot_in == lane_in + i * per_block, 1.0, 0.0).astype(jnp.bfloat16)
        times = jnp.dot(whole_b, expand, preferred_element_type=jnp.float32)
        extra = jnp.dot(part_b, expand, preferred_element_type=jnp.float32)
        bias[:, i * 128 : (i + 1) * 128] = jnp.log(times + jnp.where(inside, extra, 0.0))

    for copy in copies:
        copy.wait()


def prepare(place, lens, tables, listed, slots, weights, first):
    rows, pages = tables.shape
    members = listed.shape[0]
    wide = -(-slots // 128) * 128
    moved = sum(w.size * w.dtype.itemsize for w, _ in weights)
    count = len(weights)
    pieces = [
        pltpu.VMEM((w.shape[0] // n, w.shape[1]), w.dtype) for w, n in weights for _ in range(n)
    ]
    weights = [w for w, _ in weights]
    parts = len(pieces)
    return pl.pallas_call(
        functools.partial(prepare_kernel, count, parts),
        out_shape=pieces
        + [
            jax.ShapeDtypeStruct((rows, slots * PAGE), jnp.float32),
            jax.ShapeDtypeStruct((members, 128), jnp.int32),
        ],
        in_specs=[SM, SM, VM, VM, VM] + [HBM] * count + [ANY] * len(first),
        out_specs=[VM] * (parts + 2),
        scratch_shapes=[
            pltpu.VMEM((rows, wide), jnp.float32),
            pltpu.VMEM((rows, wide), jnp.float32),
            pltpu.SemaphoreType.DMA((parts,)),
        ],
        compiler_params=pltpu.CompilerParams(vmem_limit_bytes=6 * MIB),
        cost_estimate=pl.CostEstimate(flops=0, bytes_accessed=moved, transcendentals=0),
        name="prepare",
    )(
        place,
        lens,
        jnp.broadcast_to(lens[:, None], (rows, 128)),
        tables.T,
        jnp.pad(listed, ((0, 0), (0, wide - slots)), constant_values=-1),
        *[in_hbm(w) for w in weights],
        *first,
    )


def attend_kernel(members, place, landing, old_pool, bias, query, new_k, new_v, *refs):
    arrived = refs[:members]
    kv_out, att_low, att_high = refs[members : members + 3]
    pool, scores, sems = refs[members + 3 :]
    member, half = place[0], place[1]
    slots = pool.shape[0]
    resident = slots - ARRIVE
    per_peer = ARRIVE // members
    rows = bias.shape[0]
    count = query.shape[0]
    steps = count // (rows * GQ)

    @pl.when(half == 0)
    def _():
        copy = pltpu.make_async_copy(old_pool, pool, sems.at[0])
        copy.start()
        att_low[...] = jnp.zeros_like(att_low)
        att_high[...] = jnp.zeros_like(att_high)
        copy.wait()
        copy_out = pltpu.make_async_copy(pool, kv_out, sems.at[1])
        copy_out.start()
        copy_out.wait()

    @pl.when(half == 1)
    def _():
        copy = pltpu.make_async_copy(
            old_pool.at[pl.ds(0, resident)], pool.at[pl.ds(0, resident)], sems.at[0]
        )
        copy.start()
        for k in range(members):
            source = lax.rem(member - k + members, members)

            @pl.loop(0, per_peer, unroll=math.gcd(per_peer, 8))
            def _(c):
                pool[resident + landing[source, c]] = arrived[k][c]

        copy.wait()
        copy_out = pltpu.make_async_copy(pool, kv_out, sems.at[1])
        copy_out.start()

        scale = 1.0 / math.sqrt(HD)
        q = query[...]
        nt = (((1,), (1,)), ((), ()))
        group = 24
        width = group * PAGE
        lanes = 128
        fresh = lax.dot_general(q, new_k[...], nt, preferred_element_type=jnp.float32) * scale
        q_id = lax.broadcasted_iota(jnp.int32, fresh.shape, 0)
        t_id = lax.broadcasted_iota(jnp.int32, fresh.shape, 1)
        allowed = (q_id % rows == t_id // steps) & (t_id % steps <= (q_id // rows) % steps)
        fresh = jnp.where(allowed, fresh, -jnp.inf)
        peak = fresh
        for c in range(slots // group):
            keys = pool[c * group : (c + 1) * group, 0].reshape(width, HD)
            s = lax.dot_general(q, keys, nt, preferred_element_type=jnp.float32) * scale
            b = bias[:, c * width : (c + 1) * width]
            s = (s.reshape(count // rows, rows, width) + b[None]).reshape(count, width)
            scores[:, c * width : (c + 1) * width] = s
            for i in range(width // lanes):
                peak = jnp.maximum(peak, s[:, i * lanes : (i + 1) * lanes])
        top = jnp.max(peak, axis=1, keepdims=True)
        p = jnp.exp(fresh - top)
        total = p
        acc = jnp.dot(p.astype(jnp.bfloat16), new_v[...], preferred_element_type=jnp.float32)
        for c in range(slots // group):
            p = jnp.exp(scores[:, c * width : (c + 1) * width] - top)
            for i in range(width // lanes):
                total = total + p[:, i * lanes : (i + 1) * lanes]
            values = pool[c * group : (c + 1) * group, 1].reshape(width, HD)
            acc = acc + jnp.dot(p.astype(jnp.bfloat16), values, preferred_element_type=jnp.float32)
        out = (acc / jnp.sum(total, axis=1, keepdims=True)).astype(jnp.bfloat16)
        tokens = rows * steps
        for j in range(GQ // 2):
            att_low[:, j * HD : (j + 1) * HD] = out[j * tokens : (j + 1) * tokens]
            other = j + GQ // 2
            att_high[:, j * HD : (j + 1) * HD] = out[other * tokens : (other + 1) * tokens]
        copy_out.wait()


def place_and_attend(place, landing, old_pool, bias, query, new_k, new_v, arrived):
    members = len(arrived)
    slots = old_pool.shape[0]
    rows = bias.shape[0]
    count = query.shape[0]
    tokens = count // GQ
    return pl.pallas_call(
        functools.partial(attend_kernel, members),
        out_shape=[
            jax.ShapeDtypeStruct(old_pool.shape, old_pool.dtype),
            jax.ShapeDtypeStruct((tokens, GQ * HD // 2), jnp.bfloat16),
            jax.ShapeDtypeStruct((tokens, GQ * HD // 2), jnp.bfloat16),
        ],
        in_specs=[SM, SM, HBM, VM, VM, VM, VM] + [VM] * members,
        out_specs=[HBM, VM, VM],
        scratch_shapes=[
            pltpu.VMEM(old_pool.shape, old_pool.dtype),
            pltpu.VMEM((count, slots * PAGE), jnp.float32),
            pltpu.SemaphoreType.DMA((2,)),
        ],
        compiler_params=pltpu.CompilerParams(vmem_limit_bytes=9 * MIB),
        name="place_attend",
    )(place, landing, in_hbm(old_pool), bias, query, new_k, new_v, *arrived)


def project_kernel(groups, place, weight, stream, mine, sibling, res_out):
    half = place[1]
    members, tokens, width = mine.shape
    sums = [stream[g * tokens : (g + 1) * tokens].astype(jnp.float32) for g in range(groups)]
    for h in range(KVH):
        for g in range(groups):
            m = h * groups + g
            first = jnp.where(half == 0, mine[m], sibling[m])
            second = jnp.where(half == 0, sibling[m], mine[m])
            sums[g] = sums[g] + lax.dot_general(
                jnp.concatenate([first, second], axis=1),
                weight[:, 2 * h * width : 2 * (h + 1) * width],
                (((1,), (1,)), ((), ())),
                preferred_element_type=jnp.float32,
            )
    for g in range(groups):
        res_out[g * tokens : (g + 1) * tokens] = sums[g].astype(res_out.dtype)


def project(place, weight, stream, mine, sibling, groups):
    return pl.pallas_call(
        functools.partial(project_kernel, groups),
        out_shape=jax.ShapeDtypeStruct(stream.shape, jnp.bfloat16),
        in_specs=[SM, VM, VM, VM, VM],
        out_specs=VM,
        compiler_params=pltpu.CompilerParams(vmem_limit_bytes=4 * MIB),
        name="out_projection",
    )(place, in_vmem(weight), stream, mine, sibling)


def ffn_kernel(place, mine, sibling, gain, *refs):
    gate, up = refs[:SPLIT], refs[SPLIT : 2 * SPLIT]
    down, own_out, other_out, *scratch = refs[2 * SPLIT :]
    down_buf, normed, hidden, down_sem = scratch
    half = place[1]
    members, tokens, width = mine.shape
    depth, hidden_count = gate[0].shape
    features = depth * SPLIT
    tile = min(256, hidden_count)
    tiles = [slice(f * tile, (f + 1) * tile) for f in range(hidden_count // tile)]
    down_copies = []
    for t in range(members):
        cols = pl.ds(t * 2 * width, 2 * width)
        down_copies.append(
            pltpu.make_async_copy(down.at[:, cols], down_buf.at[:, cols], down_sem.at[t])
        )
        down_copies[-1].start()

    square = jnp.zeros((tokens, width), jnp.float32)
    for block in (mine, sibling):
        for t in range(members):
            x = block[t].astype(jnp.float32)
            square = square + x * x
    factor = lax.rsqrt(jnp.sum(square, axis=1, keepdims=True) / features + 1e-05)
    for t in range(members):
        first = jnp.where(half == 0, mine[t], sibling[t])
        second = jnp.where(half == 0, sibling[t], mine[t])
        x = jnp.concatenate([first, second], axis=1).astype(jnp.float32)
        n = x * factor * gain[t : t + 1, :]
        normed[:, 2 * t * width : 2 * (t + 1) * width] = n.astype(jnp.bfloat16)
    for cols in tiles:
        gate_act = up_act = 0.0
        for i in range(SPLIT):
            x = normed[:, i * depth : (i + 1) * depth]
            gate_act += jnp.dot(x, gate[i][:, cols], preferred_element_type=jnp.float32)
            up_act += jnp.dot(x, up[i][:, cols], preferred_element_type=jnp.float32)
        h = gate_act / (1.0 + jnp.exp(-gate_act)) * up_act
        hidden[:, cols] = h.astype(jnp.bfloat16)
    for t in range(members):
        down_copies[t].wait()
        part = jnp.dot(
            hidden[...],
            down_buf[:, 2 * t * width : 2 * (t + 1) * width],
            preferred_element_type=jnp.float32,
        )
        first, second = part[:, :width], part[:, width:]
        own_out[t] = jnp.where(half == 0, first, second)
        other_out[t] = jnp.where(half == 0, second, first).astype(jnp.bfloat16)


def feed_forward(place, mine, sibling, gain, gate, up, down):
    members, tokens, width = mine.shape
    blocks = 2 * members
    hidden_count = gate[0].shape[1]
    return pl.pallas_call(
        ffn_kernel,
        out_shape=[
            jax.ShapeDtypeStruct(mine.shape, jnp.float32),
            jax.ShapeDtypeStruct(mine.shape, jnp.bfloat16),
        ],
        in_specs=[SM, VM, VM, VM] + [VM] * (2 * SPLIT) + [HBM],
        out_specs=[VM, VM],
        scratch_shapes=[
            pltpu.VMEM(down.shape, down.dtype),
            pltpu.VMEM((tokens, blocks * width), jnp.bfloat16),
            pltpu.VMEM((tokens, hidden_count), jnp.bfloat16),
            pltpu.SemaphoreType.DMA((members,)),
        ],
        compiler_params=pltpu.CompilerParams(vmem_limit_bytes=19 * MIB),
        name="feed_forward",
    )(place, mine, sibling, gain, *map(in_vmem, gate), *map(in_vmem, up), in_hbm(down))


def local(
    kv_pages,
    page_list,
    block_tables,
    lengths,
    queries,
    fresh_kv,
    stream,
    out_proj,
    norm_gain,
    gate_weight,
    up_weight,
    down_weight,
):
    members = lax.axis_size("tp")
    member = lax.axis_index("tp")
    half = lax.axis_index("pd")
    place = jnp.stack([member, half]).astype(jnp.int32)
    slots = kv_pages.shape[0]
    groups = members // KVH
    rows = block_tables.shape[0]
    steps = queries.shape[1]
    tokens = rows * steps

    def ahead(x, k, from_half, to_half):
        route = [
            (2 * t + from_half, 2 * ((t + k) % members) + to_half) for t in range(members)
        ]
        return lax.ppermute(x, BOTH, route)

    def swap(x):
        return lax.ppermute(x, "pd", [(0, 1), (1, 0)])

    outgoing = pack(place, page_list, kv_pages)
    order = sorted(range(members), key=lambda k: abs(k - members // 2))
    arrived = [None] * members
    for k in order[:5]:
        arrived[k] = ahead(outgoing[k], k, 0, 1)

    row_lengths = lax.dynamic_slice_in_dim(lengths, member % groups * rows, rows)
    query = queries.reshape(rows, steps, GQ, HD).transpose(2, 1, 0, 3).reshape(GQ * tokens, HD)
    padding = ((0, -tokens % 128), (0, 0))
    new_k = jnp.pad(fresh_kv[:, :, 0].reshape(tokens, HD), padding)
    new_v = jnp.pad(fresh_kv[:, :, 1].reshape(tokens, HD), padding)
    gain = norm_gain.reshape(members, -1)
    *held, bias, landing = prepare(
        place,
        row_lengths,
        block_tables,
        page_list.reshape(members, slots),
        slots,
        ((out_proj, 1), (gate_weight, SPLIT), (up_weight, SPLIT)),
        (query, new_k, new_v, gain, outgoing[0]),
    )

    rest, landing = lax.optimization_barrier(([outgoing[k] for k in order[5:]], landing))
    for k, block in zip(order[5:], rest):
        arrived[k] = ahead(block, k, 0, 1)

    kv_after, att_low, att_high = place_and_attend(
        place, landing, kv_pages, bias, query, new_k, new_v, arrived
    )

    def everywhere(x):
        spread = jnp.broadcast_to(x[None], (members, *x.shape))
        mine = lax.all_to_all(spread, "tp", split_axis=0, concat_axis=0)
        return mine, swap(mine)

    att_mine = att_high + lax.ppermute(att_low, "pd", [(1, 0)])
    here, there = everywhere(att_mine)

    inner = stream.reshape(steps, groups, rows, -1).transpose(1, 0, 2, 3).reshape(stream.shape)
    residual = project(place, held[0], inner, here, there, groups)

    mine, sibling = everywhere(residual)
    own, other = feed_forward(
        place, mine, sibling, gain, held[1 : 1 + SPLIT], held[1 + SPLIT :], down_weight
    )
    summed = (own + swap(other).astype(jnp.float32)).astype(jnp.bfloat16)
    shares = lax.all_to_all(summed, "tp", split_axis=0, concat_axis=0)
    layer = residual.astype(jnp.float32) + jnp.sum(shares.astype(jnp.float32), axis=0)
    layer_out = (
        layer.astype(jnp.bfloat16)
        .reshape(groups, steps, rows, -1)
        .transpose(1, 0, 2, 3)
        .reshape(stream.shape)
    )
    return (kv_after, layer_out)


def solution(mesh):
    return jax.shard_map(
        local,
        mesh=mesh,
        in_specs=(
            P(("grp", "tp", "pd"), None, None, None),
            P("grp"),
            P(("grp", "tp"), None),
            P("grp"),
            P(("grp", "tp"), None, None),
            P(("grp", "tp"), None, None, None),
            P("grp", ("tp", "pd")),
            P(("tp", "pd"), None),
            P(),
            P(None, ("tp", "pd")),
            P(None, ("tp", "pd")),
            P(("tp", "pd"), None),
        ),
        out_specs=(P(("grp", "tp", "pd"), None, None, None), P("grp", ("tp", "pd"))),
        check_vma=False,
    )
```

```python
import functools
import math

import jax
import jax.numpy as jnp
from jax import lax
from jax.experimental import pallas as pl
from jax.experimental.pallas import tpu as pltpu
from jax.sharding import PartitionSpec as P

HD = 128
KVH = 8
GQ = 8
PAGE = 16
REQ_DEV = 2
NEWP = 128
ARRIVE = REQ_DEV * NEWP
MIB = 1024 * 1024
BOTH = ("tp", "pd")
SPLIT = 2

VM = pl.BlockSpec(memory_space=pltpu.VMEM)
SM = pl.BlockSpec(memory_space=pltpu.SMEM)
ANY = pl.BlockSpec(memory_space=pl.ANY)
HBM = pl.BlockSpec(memory_space=pltpu.HBM)


def in_vmem(x):
    return pltpu.with_memory_space_constraint(x, pltpu.VMEM)


def in_hbm(x):
    return pltpu.with_memory_space_constraint(x, pltpu.HBM)


def pack_kernel(members, place, pages, pool, *refs):
    outs = refs[:members]
    packed, held, own, counts, sems, load_sems = refs[members:]
    member, half = place[0], place[1]
    slots = pool.shape[0]
    per_peer = ARRIVE // members
    parts = 4
    step = slots // parts

    @pl.when(half == 0)
    def _():
        own_copy = pltpu.make_async_copy(pages, own, load_sems.at[parts])
        own_copy.start()
        loads = []
        for i in range(parts):
            window = pl.ds(i * step, step)
            loads.append(
                pltpu.make_async_copy(pool.at[window], held.at[window], load_sems.at[i])
            )
            loads[-1].start()
        own_copy.wait()
        start = member * slots

        if members <= 8:
            carry = (jnp.int32(0), jnp.int32(0))
            for i in range(parts):
                loads[i].wait()

                def body(j, words, base=i * step):
                    low, high = words
                    entry = own[start + base + j]
                    ahead = lax.rem((entry >> 8) - member + members, members)
                    leaves = entry >= 0
                    shift = (ahead & 3) * 8
                    is_low = ahead < 4
                    count = (jnp.where(is_low, low, high) >> shift) & 255
                    one = jnp.where(leaves, jnp.int32(1) << shift, 0)
                    packed[jnp.where(leaves, ahead * per_peer + count, ARRIVE)] = held[base + j]
                    return (
                        low + jnp.where(is_low, one, 0),
                        high + jnp.where(is_low, 0, one),
                    )

                carry = lax.fori_loop(0, step, body, carry, unroll=6)
        else:
            for i in range(parts):
                loads[i].wait()

            @pl.loop(0, members + 1)
            def _(i):
                counts[i] = 0

            @pl.loop(0, slots)
            def _(i):
                entry = own[start + i]
                ahead = lax.rem((entry >> 8) - member + members, members)
                row = jnp.where(entry >= 0, ahead, members)
                count = counts[row]
                counts[row] = count + 1
                packed[jnp.where(entry >= 0, row * per_peer + count, ARRIVE)] = held[i]

        copies = [
            pltpu.make_async_copy(packed.at[pl.ds(k * per_peer, per_peer)], outs[k], sems.at[k])
            for k in range(members)
        ]
        for copy in copies:
            copy.start()
        for copy in copies:
            copy.wait()


def pack(place, pages, pool):
    members = lax.axis_size("tp")
    per_peer = ARRIVE // members
    shape = pltpu.HBM((per_peer, *pool.shape[1:]), pool.dtype)
    return pl.pallas_call(
        functools.partial(pack_kernel, members),
        out_shape=[shape] * members,
        in_specs=[SM, HBM, HBM],
        out_specs=[HBM] * members,
        scratch_shapes=[
            pltpu.VMEM((ARRIVE + 1, *pool.shape[1:]), pool.dtype),
            pltpu.VMEM(pool.shape, pool.dtype),
            pltpu.SMEM(pages.shape, jnp.int32),
            pltpu.SMEM((members + 1,), jnp.int32),
            pltpu.SemaphoreType.DMA((members,)),
            pltpu.SemaphoreType.DMA((5,)),
        ],
        compiler_params=pltpu.CompilerParams(vmem_limit_bytes=8 * MIB),
        name="pack_pages",
    )(place, in_hbm(pages), in_hbm(pool))


def prepare_kernel(count, parts, groups, place, listed, lengths_hbm, table_hbm, *refs):
    sources = refs[:count]
    held = refs[len(refs) - 8 - parts : -8]
    bias, landing, entries, whole, part, lengths, table, sems = refs[-8:]
    small = [
        pltpu.make_async_copy(lengths_hbm, lengths, sems.at[parts]),
        pltpu.make_async_copy(table_hbm, table, sems.at[parts + 1]),
    ]
    for copy in small:
        copy.start()
    copies = []
    for source in sources:
        done = 0
        while done < source.shape[0]:
            part_out = held[len(copies)]
            window = pl.ds(done, part_out.shape[0])
            copies.append(
                pltpu.make_async_copy(source.at[window], part_out, sems.at[len(copies)])
            )
            copies[-1].start()
            done += part_out.shape[0]

    member = place[0]
    entries[...] = jnp.full(entries.shape, -1, jnp.int32)
    entries[:, : listed.shape[1]] = listed[...]
    entry = entries[...]
    members, lanes = entry.shape
    per_peer = ARRIVE // members
    wanted = (entry >= 0) & ((entry >> 8) == member)
    before = lax.broadcasted_iota(jnp.int32, (lanes, lanes), 0) < lax.broadcasted_iota(
        jnp.int32, (lanes, lanes), 1
    )
    rank = jnp.dot(
        jnp.where(wanted, 1.0, 0.0).astype(jnp.bfloat16),
        jnp.where(before, 1.0, 0.0).astype(jnp.bfloat16),
        preferred_element_type=jnp.float32,
    ).astype(jnp.int32)
    column = lax.broadcasted_iota(jnp.int32, landing.shape, 1)
    found = jnp.zeros(landing.shape, jnp.int32)
    for c in range(per_peer):
        slot = jnp.sum(jnp.where(wanted & (rank == c), entry & 255, 0), axis=1, keepdims=True)
        found = jnp.where(column == c, slot, found)
    landing[...] = found

    for copy in small:
        copy.wait()
    rows, pages = table.shape
    wide = whole.shape[1]
    base = lax.rem(member, groups) * rows
    columns = table[...].T
    page_id = lax.broadcasted_iota(jnp.int32, (pages, wide), 0)
    slot_id = lax.broadcasted_iota(jnp.int32, (pages, wide), 1)
    row_id = lax.broadcasted_iota(jnp.int32, (rows, 128), 0)
    over = jnp.zeros((rows, 128), jnp.int32)
    for r in range(rows):
        length = lengths[base + r]
        full = length // PAGE
        over = jnp.where(row_id == r, length - full * PAGE, over)
        hit = columns[:, r : r + 1] == slot_id
        in_whole = jnp.where(hit & (page_id < full), 1.0, 0.0)
        in_part = jnp.where(hit & (page_id == full), 1.0, 0.0)
        whole[r : r + 1, :] = jnp.sum(in_whole, axis=0, keepdims=True)
        part[r : r + 1, :] = jnp.sum(in_part, axis=0, keepdims=True)
    whole_b = whole[...].astype(jnp.bfloat16)
    part_b = part[...].astype(jnp.bfloat16)
    lane = lax.broadcasted_iota(jnp.int32, (rows, 128), 1)
    inside = (lane % PAGE) < over
    per_block = 128 // PAGE
    slot_in = lax.broadcasted_iota(jnp.int32, (wide, 128), 0)
    lane_in = lax.broadcasted_iota(jnp.int32, (wide, 128), 1) // PAGE
    for i in range(bias.shape[1] // 128):
        expand = jnp.where(slot_in == lane_in + i * per_block, 1.0, 0.0).astype(jnp.bfloat16)
        times = jnp.dot(whole_b, expand, preferred_element_type=jnp.float32)
        extra = jnp.dot(part_b, expand, preferred_element_type=jnp.float32)
        bias[:, i * 128 : (i + 1) * 128] = jnp.log(times + jnp.where(inside, extra, 0.0))

    for copy in copies:
        copy.wait()


def prepare(place, lengths, tables, listed, groups, weights, first):
    rows = tables.shape[0]
    members, slots = listed.shape
    wide = -(-slots // 128) * 128
    moved = sum(w.size * w.dtype.itemsize for w, _ in weights)
    pieces = [
        pltpu.VMEM((w.shape[0] // n, w.shape[1]), w.dtype) for w, n in weights for _ in range(n)
    ]
    weights = [w for w, _ in weights]
    count, parts = len(weights), len(pieces)
    return pl.pallas_call(
        functools.partial(prepare_kernel, count, parts, groups),
        out_shape=pieces
        + [
            jax.ShapeDtypeStruct((rows, slots * PAGE), jnp.float32),
            jax.ShapeDtypeStruct((members, 128), jnp.int32),
        ],
        in_specs=[SM, VM] + [HBM] * (2 + count + len(first)),
        out_specs=[VM] * (parts + 2),
        scratch_shapes=[
            pltpu.VMEM((members, wide), jnp.int32),
            pltpu.VMEM((rows, wide), jnp.float32),
            pltpu.VMEM((rows, wide), jnp.float32),
            pltpu.SMEM(lengths.shape, lengths.dtype),
            pltpu.VMEM(tables.shape, tables.dtype),
            pltpu.SemaphoreType.DMA((parts + 2,)),
        ],
        compiler_params=pltpu.CompilerParams(vmem_limit_bytes=6 * MIB),
        cost_estimate=pl.CostEstimate(flops=0, bytes_accessed=moved, transcendentals=0),
        name="prepare",
    )(place, listed, *[in_hbm(x) for x in (lengths, tables, *weights, *first)])


def attend_kernel(members, steps, place, landing, old_pool, bias, new_k, new_v, *refs):
    asked, refs = refs[:steps], refs[steps:]
    arrived = refs[:members]
    kv_out, att_low, att_high = refs[members : members + 3]
    pool, scores, sems = refs[members + 3 :]
    member, half = place[0], place[1]
    slots = pool.shape[0]
    resident = slots - ARRIVE
    per_peer = ARRIVE // members
    rows = bias.shape[0]
    count = rows * steps * GQ

    @pl.when(half == 0)
    def _():
        copy = pltpu.make_async_copy(old_pool, pool, sems.at[0])
        copy.start()
        att_low[...] = jnp.zeros_like(att_low)
        att_high[...] = jnp.zeros_like(att_high)
        copy.wait()
        copy_out = pltpu.make_async_copy(pool, kv_out, sems.at[1])
        copy_out.start()
        copy_out.wait()

    @pl.when(half == 1)
    def _():
        copy = pltpu.make_async_copy(
            old_pool.at[pl.ds(0, resident)], pool.at[pl.ds(0, resident)], sems.at[0]
        )
        copy.start()
        for k in range(members):
            source = lax.rem(member - k + members, members)

            @pl.loop(0, per_peer, unroll=math.gcd(per_peer, 8))
            def _(c):
                pool[resident + landing[source, c]] = arrived[k][c]

        copy.wait()
        copy_out = pltpu.make_async_copy(pool, kv_out, sems.at[1])
        copy_out.start()

        scale = 1.0 / math.sqrt(HD)
        q = jnp.concatenate(
            [ask[:, j * HD : (j + 1) * HD] for j in range(GQ) for ask in asked], axis=0
        )
        nt = (((1,), (1,)), ((), ()))
        group = 24
        width = group * PAGE
        lanes = 128
        fresh = lax.dot_general(q, new_k[...], nt, preferred_element_type=jnp.float32) * scale
        q_id = lax.broadcasted_iota(jnp.int32, fresh.shape, 0)
        t_id = lax.broadcasted_iota(jnp.int32, fresh.shape, 1)
        allowed = (q_id % rows == t_id // steps) & (t_id % steps <= (q_id // rows) % steps)
        fresh = jnp.where(allowed, fresh, -jnp.inf)
        peak = fresh
        for c in range(slots // group):
            keys = pool[c * group : (c + 1) * group, 0].reshape(width, HD)
            s = lax.dot_general(q, keys, nt, preferred_element_type=jnp.float32) * scale
            b = bias[:, c * width : (c + 1) * width]
            s = (s.reshape(count // rows, rows, width) + b[None]).reshape(count, width)
            scores[:, c * width : (c + 1) * width] = s
            for i in range(width // lanes):
                peak = jnp.maximum(peak, s[:, i * lanes : (i + 1) * lanes])
        top = jnp.max(peak, axis=1, keepdims=True)
        p = jnp.exp(fresh - top)
        total = p
        acc = jnp.dot(p.astype(jnp.bfloat16), new_v[...], preferred_element_type=jnp.float32)
        for c in range(slots // group):
            p = jnp.exp(scores[:, c * width : (c + 1) * width] - top)
            for i in range(width // lanes):
                total = total + p[:, i * lanes : (i + 1) * lanes]
            values = pool[c * group : (c + 1) * group, 1].reshape(width, HD)
            acc = acc + jnp.dot(p.astype(jnp.bfloat16), values, preferred_element_type=jnp.float32)
        out = (acc / jnp.sum(total, axis=1, keepdims=True)).astype(jnp.bfloat16)
        tokens = rows * steps
        for j in range(GQ // 2):
            att_low[:, j * HD : (j + 1) * HD] = out[j * tokens : (j + 1) * tokens]
            other = j + GQ // 2
            att_high[:, j * HD : (j + 1) * HD] = out[other * tokens : (other + 1) * tokens]
        copy_out.wait()


def place_and_attend(place, landing, old_pool, bias, new_k, new_v, asked, arrived):
    members = len(arrived)
    slots = old_pool.shape[0]
    rows = bias.shape[0]
    steps = len(asked)
    tokens = rows * steps
    return pl.pallas_call(
        functools.partial(attend_kernel, members, steps),
        out_shape=[
            jax.ShapeDtypeStruct(old_pool.shape, old_pool.dtype),
            jax.ShapeDtypeStruct((tokens, GQ * HD // 2), jnp.bfloat16),
            jax.ShapeDtypeStruct((tokens, GQ * HD // 2), jnp.bfloat16),
        ],
        in_specs=[SM, SM, HBM, VM, VM, VM] + [VM] * (steps + members),
        out_specs=[HBM, VM, VM],
        scratch_shapes=[
            pltpu.VMEM(old_pool.shape, old_pool.dtype),
            pltpu.VMEM((tokens * GQ, slots * PAGE), jnp.float32),
            pltpu.SemaphoreType.DMA((2,)),
        ],
        compiler_params=pltpu.CompilerParams(vmem_limit_bytes=9 * MIB),
        name="place_attend",
    )(place, landing, in_hbm(old_pool), bias, new_k, new_v, *asked, *arrived)


def project_kernel(groups, place, weight, stream, mine, sibling, res_out):
    half = place[1]
    members, tokens, width = mine.shape
    sums = [stream[g * tokens : (g + 1) * tokens].astype(jnp.float32) for g in range(groups)]
    for h in range(KVH):
        for g in range(groups):
            m = h * groups + g
            first = jnp.where(half == 0, mine[m], sibling[m])
            second = jnp.where(half == 0, sibling[m], mine[m])
            sums[g] = sums[g] + lax.dot_general(
                jnp.concatenate([first, second], axis=1),
                weight[:, 2 * h * width : 2 * (h + 1) * width],
                (((1,), (1,)), ((), ())),
                preferred_element_type=jnp.float32,
            )
    for g in range(groups):
        res_out[g * tokens : (g + 1) * tokens] = sums[g].astype(res_out.dtype)


def project(place, weight, stream, mine, sibling, groups):
    return pl.pallas_call(
        functools.partial(project_kernel, groups),
        out_shape=jax.ShapeDtypeStruct(stream.shape, jnp.bfloat16),
        in_specs=[SM, VM, VM, VM, VM],
        out_specs=VM,
        compiler_params=pltpu.CompilerParams(vmem_limit_bytes=4 * MIB),
        name="out_projection",
    )(place, in_vmem(weight), stream, mine, sibling)


def ffn_kernel(place, mine, sibling, gain, *refs):
    gate = refs[:SPLIT]
    up, down, own_out, other_out, *scratch = refs[SPLIT:]
    up_buf, down_buf, normed, gated, hidden, up_sem, down_sem = scratch
    half = place[1]
    members, tokens, width = mine.shape
    depth, hidden_count = gate[0].shape
    features = depth * SPLIT
    chunks = up_sem.shape[0]
    step = features // chunks
    up_copies, down_copies = [], []
    for i in range(chunks):
        window = pl.ds(i * step, step)
        up_copies.append(
            pltpu.make_async_copy(up.at[window], up_buf.at[window], up_sem.at[i])
        )
        up_copies[-1].start()
    for t in range(members):
        cols = pl.ds(t * 2 * width, 2 * width)
        down_copies.append(
            pltpu.make_async_copy(down.at[:, cols], down_buf.at[:, cols], down_sem.at[t])
        )
        down_copies[-1].start()

    square = jnp.zeros((tokens, width), jnp.float32)
    for block in (mine, sibling):
        for t in range(members):
            x = block[t].astype(jnp.float32)
            square = square + x * x
    factor = lax.rsqrt(jnp.sum(square, axis=1, keepdims=True) / features + 1e-05)
    for t in range(members):
        first = jnp.where(half == 0, mine[t], sibling[t])
        second = jnp.where(half == 0, sibling[t], mine[t])
        x = jnp.concatenate([first, second], axis=1).astype(jnp.float32)
        cols = slice(2 * t * width, 2 * (t + 1) * width)
        normed[:, cols] = (x * factor * gain[cols][None, :]).astype(jnp.bfloat16)
    tile = min(256, hidden_count)
    for f in range(hidden_count // tile):
        cols = slice(f * tile, (f + 1) * tile)
        act = 0.0
        for i in range(SPLIT):
            x = normed[:, i * depth : (i + 1) * depth]
            act += jnp.dot(x, gate[i][:, cols], preferred_element_type=jnp.float32)
        gated[:, cols] = act / (1.0 + jnp.exp(-act))
    act = 0.0
    for i in range(chunks):
        up_copies[i].wait()
        rows = slice(i * step, (i + 1) * step)
        act += jnp.dot(normed[:, rows], up_buf[rows, :], preferred_element_type=jnp.float32)
    hidden[...] = (gated[...] * act).astype(jnp.bfloat16)
    for t in range(members):
        down_copies[t].wait()
        part = jnp.dot(
            hidden[...],
            down_buf[:, 2 * t * width : 2 * (t + 1) * width],
            preferred_element_type=jnp.float32,
        )
        first, second = part[:, :width], part[:, width:]
        own_out[t] = jnp.where(half == 0, first, second)
        other_out[t] = jnp.where(half == 0, second, first).astype(jnp.bfloat16)


def feed_forward(place, mine, sibling, gain, gate, up, down):
    tokens = mine.shape[1]
    features, hidden_count = up.shape
    return pl.pallas_call(
        ffn_kernel,
        out_shape=[
            jax.ShapeDtypeStruct(mine.shape, jnp.float32),
            jax.ShapeDtypeStruct(mine.shape, jnp.bfloat16),
        ],
        in_specs=[SM, VM, VM, VM] + [VM] * SPLIT + [HBM, HBM],
        out_specs=[VM, VM],
        scratch_shapes=[
            pltpu.VMEM(up.shape, up.dtype),
            pltpu.VMEM(down.shape, down.dtype),
            pltpu.VMEM((tokens, features), jnp.bfloat16),
            pltpu.VMEM((tokens, hidden_count), jnp.float32),
            pltpu.VMEM((tokens, hidden_count), jnp.bfloat16),
            pltpu.SemaphoreType.DMA((8,)),
            pltpu.SemaphoreType.DMA((mine.shape[0],)),
        ],
        compiler_params=pltpu.CompilerParams(vmem_limit_bytes=36 * MIB),
        name="feed_forward",
    )(place, mine, sibling, gain, *map(in_vmem, gate), in_hbm(up), in_hbm(down))


def local(
    kv_pages,
    page_list,
    block_tables,
    lengths,
    queries,
    fresh_kv,
    stream,
    out_proj,
    norm_gain,
    gate_weight,
    up_weight,
    down_weight,
):
    members = lax.axis_size("tp")
    member = lax.axis_index("tp")
    half = lax.axis_index("pd")
    place = jnp.stack([member, half]).astype(jnp.int32)
    slots = kv_pages.shape[0]
    groups = members // KVH
    rows = block_tables.shape[0]
    steps = queries.shape[1]
    tokens = rows * steps

    def ahead(x, k, from_half, to_half):
        route = [
            (2 * t + from_half, 2 * ((t + k) % members) + to_half) for t in range(members)
        ]
        return lax.ppermute(x, BOTH, route)

    def swap(x):
        return lax.ppermute(x, "pd", [(0, 1), (1, 0)])

    outgoing = pack(place, page_list, kv_pages)
    order = sorted(range(members), key=lambda k: abs(k - members // 2))
    arrived = [None] * members
    for k in order[:5]:
        arrived[k] = ahead(outgoing[k], k, 0, 1)

    *held, bias, landing = prepare(
        place,
        lengths,
        block_tables,
        page_list.reshape(members, slots),
        groups,
        ((out_proj, 1), (gate_weight, SPLIT)),
        (outgoing[0],),
    )

    rest, landing = lax.optimization_barrier(([outgoing[k] for k in order[5:]], landing))
    for k, block in zip(order[5:], rest):
        arrived[k] = ahead(block, k, 0, 1)

    padding = ((0, -tokens % 128), (0, 0))
    new_k = jnp.pad(fresh_kv[:, :, 0].reshape(tokens, HD), padding)
    new_v = jnp.pad(fresh_kv[:, :, 1].reshape(tokens, HD), padding)
    asked = [queries[:, st] for st in range(steps)]
    kv_after, att_low, att_high = place_and_attend(
        place, landing, kv_pages, bias, new_k, new_v, asked, arrived
    )

    def everywhere(x):
        spread = jnp.broadcast_to(x[None], (members, *x.shape))
        mine = lax.all_to_all(spread, "tp", split_axis=0, concat_axis=0)
        return mine, swap(mine)

    att_mine = att_high + lax.ppermute(att_low, "pd", [(1, 0)])
    here, there = everywhere(att_mine)

    inner = stream.reshape(steps, groups, rows, -1).transpose(1, 0, 2, 3).reshape(stream.shape)
    residual = project(place, held[0], inner, here, there, groups)

    mine, sibling = everywhere(residual)
    own, other = feed_forward(
        place, mine, sibling, norm_gain, held[1:], up_weight, down_weight
    )
    summed = (own + swap(other).astype(jnp.float32)).astype(jnp.bfloat16)
    shares = lax.all_to_all(summed, "tp", split_axis=0, concat_axis=0)
    layer = residual.astype(jnp.float32) + jnp.sum(shares.astype(jnp.float32), axis=0)
    layer_out = (
        layer.astype(jnp.bfloat16)
        .reshape(groups, steps, rows, -1)
        .transpose(1, 0, 2, 3)
        .reshape(stream.shape)
    )
    return (kv_after, layer_out)


def solution(mesh):
    return jax.shard_map(
        local,
        mesh=mesh,
        in_specs=(
            P(("grp", "tp", "pd"), None, None, None),
            P("grp"),
            P(("grp", "tp"), None),
            P("grp"),
            P(("grp", "tp"), None, None),
            P(("grp", "tp"), None, None, None),
            P("grp", ("tp", "pd")),
            P(("tp", "pd"), None),
            P(),
            P(None, ("tp", "pd")),
            P(None, ("tp", "pd")),
            P(("tp", "pd"), None),
        ),
        out_specs=(P(("grp", "tp", "pd"), None, None, None), P("grp", ("tp", "pd"))),
        check_vma=False,
    )
```

```python
import functools
import math

import jax
import jax.numpy as jnp
from jax import lax
from jax.experimental import pallas as pl
from jax.experimental.pallas import tpu as pltpu
from jax.sharding import PartitionSpec as P

HD = 128
KVH = 8
GQ = 8
PAGE = 16
REQ_DEV = 2
NEWP = 128
ARRIVE = REQ_DEV * NEWP
MIB = 1024 * 1024
BOTH = ("tp", "pd")
SPLIT = 2

VM = pl.BlockSpec(memory_space=pltpu.VMEM)
SM = pl.BlockSpec(memory_space=pltpu.SMEM)
ANY = pl.BlockSpec(memory_space=pl.ANY)
HBM = pl.BlockSpec(memory_space=pltpu.HBM)


def in_vmem(x):
    return pltpu.with_memory_space_constraint(x, pltpu.VMEM)


def in_hbm(x):
    return pltpu.with_memory_space_constraint(x, pltpu.HBM)


def pack_kernel(members, place, pages, pool, *refs):
    count = members - 1
    outs, kept = refs[:count], refs[count]
    packed, held, own, counts, sems, load_sems, keep_sems = refs[count + 1 :]
    member, half = place[0], place[1]
    slots = pool.shape[0]
    per_peer = ARRIVE // members
    parts = 4
    step = slots // parts

    @pl.when(half == 0)
    def _():
        own_copy = pltpu.make_async_copy(pages, own, load_sems.at[parts])
        own_copy.start()
        loads, keeps = [], []
        for i in range(parts):
            window = pl.ds(i * step, step)
            loads.append(
                pltpu.make_async_copy(pool.at[window], held.at[window], load_sems.at[i])
            )
            keeps.append(
                pltpu.make_async_copy(held.at[window], kept.at[window], keep_sems.at[i])
            )
            loads[-1].start()
        own_copy.wait()
        start = member * slots

        if members <= 8:
            carry = (jnp.int32(0), jnp.int32(0))
            for i in range(parts):
                loads[i].wait()

                def body(j, words, base=i * step):
                    low, high = words
                    entry = own[start + base + j]
                    ahead = lax.rem((entry >> 8) - member + members + 1, members)
                    leaves = entry >= 0
                    shift = (ahead & 3) * 8
                    is_low = ahead < 4
                    count = (jnp.where(is_low, low, high) >> shift) & 255
                    one = jnp.where(leaves, jnp.int32(1) << shift, 0)
                    packed[jnp.where(leaves, ahead * per_peer + count, ARRIVE)] = held[base + j]
                    return (
                        low + jnp.where(is_low, one, 0),
                        high + jnp.where(is_low, 0, one),
                    )

                carry = lax.fori_loop(0, step, body, carry, unroll=6)
        else:
            for i in range(parts):
                loads[i].wait()

            @pl.loop(0, members + 1)
            def _(i):
                counts[i] = 0

            @pl.loop(0, slots)
            def _(i):
                entry = own[start + i]
                ahead = lax.rem((entry >> 8) - member + members + 1, members)
                row = jnp.where(entry >= 0, ahead, members)
                count = counts[row]
                counts[row] = count + 1
                packed[jnp.where(entry >= 0, row * per_peer + count, ARRIVE)] = held[i]

        copies = []
        near, own_chunk, *far = outs
        moves = [(near, 0, 0), (near, per_peer, 2), (own_chunk, 0, 1)]
        moves += [(out, 0, 3 + i) for i, out in enumerate(far)]
        for i, (out, first, row) in enumerate(moves):
            copies.append(
                pltpu.make_async_copy(
                    packed.at[pl.ds(row * per_peer, per_peer)],
                    out.at[pl.ds(first, per_peer)],
                    sems.at[i],
                )
            )
            copies[-1].start()
        for keep in keeps:
            keep.start()
        for copy in copies + keeps:
            copy.wait()


def pack(place, pages, pool):
    members = lax.axis_size("tp")
    per_peer = ARRIVE // members
    chunk = pool.shape[1:]
    return pl.pallas_call(
        functools.partial(pack_kernel, members),
        out_shape=[pltpu.HBM((2 * per_peer, *chunk), pool.dtype)]
        + [pltpu.HBM((per_peer, *chunk), pool.dtype)] * (members - 2)
        + [pltpu.HBM(pool.shape, pool.dtype)],
        in_specs=[SM, HBM, HBM],
        out_specs=[HBM] * members,
        scratch_shapes=[
            pltpu.VMEM((ARRIVE + 1, *chunk), pool.dtype),
            pltpu.VMEM(pool.shape, pool.dtype),
            pltpu.SMEM(pages.shape, jnp.int32),
            pltpu.SMEM((members + 1,), jnp.int32),
            pltpu.SemaphoreType.DMA((members,)),
            pltpu.SemaphoreType.DMA((5,)),
            pltpu.SemaphoreType.DMA((4,)),
        ],
        compiler_params=pltpu.CompilerParams(vmem_limit_bytes=8 * MIB),
        name="pack_pages",
    )(place, in_hbm(pages), in_hbm(pool))


def prepare_kernel(count, parts, groups, place, listed, lengths_hbm, table_hbm, *refs):
    sources = refs[:count]
    held = refs[len(refs) - 8 - parts : -8]
    bias, landing, entries, whole, part, lengths, table, sems = refs[-8:]
    small = [
        pltpu.make_async_copy(lengths_hbm, lengths, sems.at[parts]),
        pltpu.make_async_copy(table_hbm, table, sems.at[parts + 1]),
    ]
    for copy in small:
        copy.start()
    copies = []
    for source in sources:
        done = 0
        while done < source.shape[0]:
            part_out = held[len(copies)]
            window = pl.ds(done, part_out.shape[0])
            copies.append(
                pltpu.make_async_copy(source.at[window], part_out, sems.at[len(copies)])
            )
            copies[-1].start()
            done += part_out.shape[0]

    member = place[0]
    entries[...] = jnp.full(entries.shape, -1, jnp.int32)
    entries[:, : listed.shape[1]] = listed[...]
    entry = entries[...]
    members, lanes = entry.shape
    per_peer = ARRIVE // members
    wanted = (entry >= 0) & ((entry >> 8) == member)
    before = lax.broadcasted_iota(jnp.int32, (lanes, lanes), 0) < lax.broadcasted_iota(
        jnp.int32, (lanes, lanes), 1
    )
    rank = jnp.dot(
        jnp.where(wanted, 1.0, 0.0).astype(jnp.bfloat16),
        jnp.where(before, 1.0, 0.0).astype(jnp.bfloat16),
        preferred_element_type=jnp.float32,
    ).astype(jnp.int32)
    column = lax.broadcasted_iota(jnp.int32, landing.shape, 1)
    found = jnp.zeros(landing.shape, jnp.int32)
    for c in range(per_peer):
        slot = jnp.sum(jnp.where(wanted & (rank == c), entry & 255, 0), axis=1, keepdims=True)
        found = jnp.where(column == c, slot, found)
    landing[...] = found

    for copy in small:
        copy.wait()
    rows, pages = table.shape
    wide = whole.shape[1]
    base = lax.rem(member, groups) * rows
    columns = table[...].T
    page_id = lax.broadcasted_iota(jnp.int32, (pages, wide), 0)
    slot_id = lax.broadcasted_iota(jnp.int32, (pages, wide), 1)
    row_id = lax.broadcasted_iota(jnp.int32, (rows, 128), 0)
    over = jnp.zeros((rows, 128), jnp.int32)
    for r in range(rows):
        length = lengths[base + r]
        full = length // PAGE
        over = jnp.where(row_id == r, length - full * PAGE, over)
        hit = columns[:, r : r + 1] == slot_id
        in_whole = jnp.where(hit & (page_id < full), 1.0, 0.0)
        in_part = jnp.where(hit & (page_id == full), 1.0, 0.0)
        whole[r : r + 1, :] = jnp.sum(in_whole, axis=0, keepdims=True)
        part[r : r + 1, :] = jnp.sum(in_part, axis=0, keepdims=True)
    whole_b = whole[...].astype(jnp.bfloat16)
    part_b = part[...].astype(jnp.bfloat16)
    lane = lax.broadcasted_iota(jnp.int32, (rows, 128), 1)
    inside = (lane % PAGE) < over
    per_block = 128 // PAGE
    slot_in = lax.broadcasted_iota(jnp.int32, (wide, 128), 0)
    lane_in = lax.broadcasted_iota(jnp.int32, (wide, 128), 1) // PAGE
    for i in range(bias.shape[1] // 128):
        expand = jnp.where(slot_in == lane_in + i * per_block, 1.0, 0.0).astype(jnp.bfloat16)
        times = jnp.dot(whole_b, expand, preferred_element_type=jnp.float32)
        extra = jnp.dot(part_b, expand, preferred_element_type=jnp.float32)
        bias[:, i * 128 : (i + 1) * 128] = jnp.log(times + jnp.where(inside, extra, 0.0))

    for copy in copies:
        copy.wait()


def prepare(place, lengths, tables, listed, groups, weights, first):
    rows = tables.shape[0]
    members, slots = listed.shape
    wide = -(-slots // 128) * 128
    moved = sum(w.size * w.dtype.itemsize for w, _ in weights)
    pieces = [
        pltpu.VMEM((w.shape[0] // n, w.shape[1]), w.dtype) for w, n in weights for _ in range(n)
    ]
    weights = [w for w, _ in weights]
    count, parts = len(weights), len(pieces)
    return pl.pallas_call(
        functools.partial(prepare_kernel, count, parts, groups),
        out_shape=pieces
        + [
            jax.ShapeDtypeStruct((rows, slots * PAGE), jnp.float32),
            jax.ShapeDtypeStruct((members, 128), jnp.int32),
        ],
        in_specs=[SM, VM] + [HBM] * (2 + count + len(first)),
        out_specs=[VM] * (parts + 2),
        scratch_shapes=[
            pltpu.VMEM((members, wide), jnp.int32),
            pltpu.VMEM((rows, wide), jnp.float32),
            pltpu.VMEM((rows, wide), jnp.float32),
            pltpu.SMEM(lengths.shape, lengths.dtype),
            pltpu.VMEM(tables.shape, tables.dtype),
            pltpu.SemaphoreType.DMA((parts + 2,)),
        ],
        compiler_params=pltpu.CompilerParams(vmem_limit_bytes=6 * MIB),
        cost_estimate=pl.CostEstimate(flops=0, bytes_accessed=moved, transcendentals=0),
        name="prepare",
    )(place, listed, *[in_hbm(x) for x in (lengths, tables, *weights, *first)])


def attend_kernel(members, steps, chunks, place, landing, old_pool, _, bias, new_k, new_v, *refs):
    asked, refs = refs[:steps], refs[steps:]
    arrived, refs = refs[:-6], refs[-6:]
    kv_out, att_low, att_high, pool, scores, sems = refs
    member, half = place[0], place[1]
    slots = pool.shape[0]
    resident = slots - ARRIVE
    per_peer = ARRIVE // members
    rows = bias.shape[0]
    count = rows * steps * GQ

    @pl.when(half == 0)
    def _():
        att_low[...] = jnp.zeros_like(att_low)
        att_high[...] = jnp.zeros_like(att_high)

    @pl.when(half == 1)
    def _():
        copy = pltpu.make_async_copy(
            old_pool.at[pl.ds(0, resident)], pool.at[pl.ds(0, resident)], sems.at[0]
        )
        copy.start()
        for i, first, k in chunks:
            source = lax.rem(member - k + members, members)

            @pl.loop(0, per_peer, unroll=math.gcd(per_peer, 8))
            def _(c):
                pool[resident + landing[source, c]] = arrived[i][first + c]

        copy.wait()
        copy_out = pltpu.make_async_copy(pool, kv_out, sems.at[1])
        copy_out.start()

        scale = 1.0 / math.sqrt(HD)
        q = jnp.concatenate(
            [ask[:, j * HD : (j + 1) * HD] for j in range(GQ) for ask in asked], axis=0
        )
        nt = (((1,), (1,)), ((), ()))
        group = 24
        width = group * PAGE
        lanes = 128
        fresh = lax.dot_general(q, new_k[...], nt, preferred_element_type=jnp.float32) * scale
        q_id = lax.broadcasted_iota(jnp.int32, fresh.shape, 0)
        t_id = lax.broadcasted_iota(jnp.int32, fresh.shape, 1)
        allowed = (q_id % rows == t_id // steps) & (t_id % steps <= (q_id // rows) % steps)
        fresh = jnp.where(allowed, fresh, -jnp.inf)
        peak = fresh
        for c in range(slots // group):
            keys = pool[c * group : (c + 1) * group, 0].reshape(width, HD)
            s = lax.dot_general(q, keys, nt, preferred_element_type=jnp.float32) * scale
            b = bias[:, c * width : (c + 1) * width]
            s = (s.reshape(count // rows, rows, width) + b[None]).reshape(count, width)
            scores[:, c * width : (c + 1) * width] = s
            for i in range(width // lanes):
                peak = jnp.maximum(peak, s[:, i * lanes : (i + 1) * lanes])
        top = jnp.max(peak, axis=1, keepdims=True)
        p = jnp.exp(fresh - top)
        total = p
        acc = jnp.dot(p.astype(jnp.bfloat16), new_v[...], preferred_element_type=jnp.float32)
        for c in range(slots // group):
            p = jnp.exp(scores[:, c * width : (c + 1) * width] - top)
            for i in range(width // lanes):
                total = total + p[:, i * lanes : (i + 1) * lanes]
            values = pool[c * group : (c + 1) * group, 1].reshape(width, HD)
            acc = acc + jnp.dot(p.astype(jnp.bfloat16), values, preferred_element_type=jnp.float32)
        out = (acc / jnp.sum(total, axis=1, keepdims=True)).astype(jnp.bfloat16)
        tokens = rows * steps
        for j in range(GQ // 2):
            att_low[:, j * HD : (j + 1) * HD] = out[j * tokens : (j + 1) * tokens]
            other = j + GQ // 2
            att_high[:, j * HD : (j + 1) * HD] = out[other * tokens : (other + 1) * tokens]
        copy_out.wait()


def place_and_attend(place, landing, old_pool, kept, bias, new_k, new_v, asked, arrived, chunks):
    members = landing.shape[0]
    slots = old_pool.shape[0]
    rows = bias.shape[0]
    steps = len(asked)
    tokens = rows * steps
    return pl.pallas_call(
        functools.partial(attend_kernel, members, steps, chunks),
        out_shape=[
            jax.ShapeDtypeStruct(old_pool.shape, old_pool.dtype),
            jax.ShapeDtypeStruct((tokens, GQ * HD // 2), jnp.bfloat16),
            jax.ShapeDtypeStruct((tokens, GQ * HD // 2), jnp.bfloat16),
        ],
        in_specs=[SM, SM, HBM, HBM, VM, VM, VM] + [VM] * (steps + len(arrived)),
        out_specs=[HBM, VM, VM],
        scratch_shapes=[
            pltpu.VMEM(old_pool.shape, old_pool.dtype),
            pltpu.VMEM((tokens * GQ, slots * PAGE), jnp.float32),
            pltpu.SemaphoreType.DMA((2,)),
        ],
        compiler_params=pltpu.CompilerParams(vmem_limit_bytes=9 * MIB),
        input_output_aliases={3: 0},
        name="place_attend",
    )(
        place,
        landing,
        in_hbm(old_pool),
        in_hbm(kept),
        bias,
        new_k,
        new_v,
        *asked,
        *arrived,
    )


def project_kernel(groups, place, weight, stream, mine, sibling, res_out):
    half = place[1]
    members, tokens, width = mine.shape
    sums = [stream[g * tokens : (g + 1) * tokens].astype(jnp.float32) for g in range(groups)]
    for h in range(KVH):
        for g in range(groups):
            m = h * groups + g
            first = jnp.where(half == 0, mine[m], sibling[m])
            second = jnp.where(half == 0, sibling[m], mine[m])
            sums[g] = sums[g] + lax.dot_general(
                jnp.concatenate([first, second], axis=1),
                weight[:, 2 * h * width : 2 * (h + 1) * width],
                (((1,), (1,)), ((), ())),
                preferred_element_type=jnp.float32,
            )
    for g in range(groups):
        res_out[g * tokens : (g + 1) * tokens] = sums[g].astype(res_out.dtype)


def project(place, weight, stream, mine, sibling, groups):
    return pl.pallas_call(
        functools.partial(project_kernel, groups),
        out_shape=jax.ShapeDtypeStruct(stream.shape, jnp.bfloat16),
        in_specs=[SM, VM, VM, VM, VM],
        out_specs=VM,
        compiler_params=pltpu.CompilerParams(vmem_limit_bytes=4 * MIB),
        name="out_projection",
    )(place, in_vmem(weight), stream, mine, sibling)


def ffn_kernel(place, mine, sibling, gain, *refs):
    gate, up = refs[:SPLIT], refs[SPLIT : 2 * SPLIT]
    down, own_out, other_out, down_buf, normed, hidden, down_sem = refs[2 * SPLIT :]
    half = place[1]
    members, tokens, width = mine.shape
    depth, hidden_count = gate[0].shape
    features = depth * SPLIT
    down_copies = []
    for t in range(members):
        cols = pl.ds(t * 2 * width, 2 * width)
        down_copies.append(
            pltpu.make_async_copy(down.at[:, cols], down_buf.at[:, cols], down_sem.at[t])
        )
        down_copies[-1].start()

    square = jnp.zeros((tokens, width), jnp.float32)
    for block in (mine, sibling):
        for t in range(members):
            x = block[t].astype(jnp.float32)
            square = square + x * x
    factor = lax.rsqrt(jnp.sum(square, axis=1, keepdims=True) / features + 1e-05)
    for t in range(members):
        first = jnp.where(half == 0, mine[t], sibling[t])
        second = jnp.where(half == 0, sibling[t], mine[t])
        x = jnp.concatenate([first, second], axis=1).astype(jnp.float32)
        cols = slice(2 * t * width, 2 * (t + 1) * width)
        normed[:, cols] = (x * factor * gain[cols][None, :]).astype(jnp.bfloat16)
    tile = min(256, hidden_count)
    for f in range(hidden_count // tile):
        cols = slice(f * tile, (f + 1) * tile)
        gate_act = up_act = 0.0
        for i in range(SPLIT):
            x = normed[:, i * depth : (i + 1) * depth]
            gate_act += jnp.dot(x, gate[i][:, cols], preferred_element_type=jnp.float32)
            up_act += jnp.dot(x, up[i][:, cols], preferred_element_type=jnp.float32)
        h = gate_act / (1.0 + jnp.exp(-gate_act)) * up_act
        hidden[:, cols] = h.astype(jnp.bfloat16)
    for t in range(members):
        down_copies[t].wait()
        part = jnp.dot(
            hidden[...],
            down_buf[:, 2 * t * width : 2 * (t + 1) * width],
            preferred_element_type=jnp.float32,
        )
        first, second = part[:, :width], part[:, width:]
        own_out[t] = jnp.where(half == 0, first, second)
        other_out[t] = jnp.where(half == 0, second, first).astype(jnp.bfloat16)


def feed_forward(place, mine, sibling, gain, gate, up, down):
    tokens = mine.shape[1]
    hidden_count, features = down.shape
    return pl.pallas_call(
        ffn_kernel,
        out_shape=[
            jax.ShapeDtypeStruct(mine.shape, jnp.float32),
            jax.ShapeDtypeStruct(mine.shape, jnp.bfloat16),
        ],
        in_specs=[SM, VM, VM, VM] + [VM] * (2 * SPLIT) + [HBM],
        out_specs=[VM, VM],
        scratch_shapes=[
            pltpu.VMEM(down.shape, down.dtype),
            pltpu.VMEM((tokens, features), jnp.bfloat16),
            pltpu.VMEM((tokens, hidden_count), jnp.bfloat16),
            pltpu.SemaphoreType.DMA((mine.shape[0],)),
        ],
        compiler_params=pltpu.CompilerParams(vmem_limit_bytes=19 * MIB),
        name="feed_forward",
    )(place, mine, sibling, gain, *map(in_vmem, (*gate, *up)), in_hbm(down))


def local(
    kv_pages,
    page_list,
    block_tables,
    lengths,
    queries,
    fresh_kv,
    stream,
    out_proj,
    norm_gain,
    gate_weight,
    up_weight,
    down_weight,
):
    members = lax.axis_size("tp")
    member = lax.axis_index("tp")
    half = lax.axis_index("pd")
    place = jnp.stack([member, half]).astype(jnp.int32)
    slots = kv_pages.shape[0]
    per_peer = ARRIVE // members
    groups = members // KVH
    rows = block_tables.shape[0]
    steps = queries.shape[1]
    tokens = rows * steps

    def send(x, *hops):
        route = [
            (2 * t + start, 2 * ((t + k) % members) + end)
            for start, k, end in hops
            for t in range(members)
        ]
        return lax.ppermute(x, BOTH, route)

    def swap(x):
        return lax.ppermute(x, "pd", [(0, 1), (1, 0)])

    near, own_chunk, *far, kept = pack(place, page_list, kv_pages)
    far = dict(zip(range(2, members - 1), far))
    crossed = lax.ppermute(near, "pd", [(0, 1)])
    behind, ahead = crossed[:per_peer], crossed[per_peer:]
    hosts = (2, members - 2)
    middle = sorted(set(far) - set(hosts), key=lambda k: abs(k - members // 2))
    arrived = {k: send(far[k], (0, k, 1)) for k in middle}
    for host, k, block in zip(hosts, (1, -1), (ahead, behind)):
        block = jnp.where(half == 0, far[host], block)
        arrived[host] = send(block, (0, host, 1), (1, k, 0))

    *held, bias, landing = prepare(
        place,
        lengths,
        block_tables,
        page_list.reshape(members, slots),
        groups,
        ((out_proj, 1), (gate_weight, SPLIT), (up_weight, SPLIT)),
        (near,),
    )

    arrived, landing = lax.optimization_barrier((arrived, landing))
    last = lax.ppermute(
        jnp.concatenate([own_chunk] + [arrived[host] for host in hosts]), "pd", [(0, 1)]
    )
    arrays = [last] + [arrived[k] for k in sorted(arrived)]
    chunks = [(0, 0, 0), (0, per_peer, 1), (0, 2 * per_peer, members - 1)]
    chunks += [(i + 1, 0, k) for i, k in enumerate(sorted(arrived))]
    padding = ((0, -tokens % 128), (0, 0))
    new_k = jnp.pad(fresh_kv[:, :, 0].reshape(tokens, HD), padding)
    new_v = jnp.pad(fresh_kv[:, :, 1].reshape(tokens, HD), padding)
    asked = [queries[:, st] for st in range(steps)]
    kv_after, att_low, att_high = place_and_attend(
        place, landing, kv_pages, kept, bias, new_k, new_v, asked, arrays, chunks
    )

    def everywhere(x):
        spread = jnp.broadcast_to(x[None], (members, *x.shape))
        mine = lax.all_to_all(spread, "tp", split_axis=0, concat_axis=0)
        return mine, swap(mine)

    att_mine = att_high + lax.ppermute(att_low, "pd", [(1, 0)])
    here, there = everywhere(att_mine)

    inner = stream.reshape(steps, groups, rows, -1).transpose(1, 0, 2, 3).reshape(stream.shape)
    residual = project(place, held[0], inner, here, there, groups)

    mine, sibling = everywhere(residual)
    own, other = feed_forward(
        place, mine, sibling, norm_gain, held[1 : 1 + SPLIT], held[1 + SPLIT :], down_weight
    )
    summed = (own + swap(other).astype(jnp.float32)).astype(jnp.bfloat16)
    shares = lax.all_to_all(summed, "tp", split_axis=0, concat_axis=0)
    layer = residual.astype(jnp.float32) + jnp.sum(shares.astype(jnp.float32), axis=0)
    layer_out = (
        layer.astype(jnp.bfloat16)
        .reshape(groups, steps, rows, -1)
        .transpose(1, 0, 2, 3)
        .reshape(stream.shape)
    )
    return (kv_after, layer_out)


def solution(mesh):
    return jax.shard_map(
        local,
        mesh=mesh,
        in_specs=(
            P(("grp", "tp", "pd"), None, None, None),
            P("grp"),
            P(("grp", "tp"), None),
            P("grp"),
            P(("grp", "tp"), None, None),
            P(("grp", "tp"), None, None, None),
            P("grp", ("tp", "pd")),
            P(("tp", "pd"), None),
            P(),
            P(None, ("tp", "pd")),
            P(None, ("tp", "pd")),
            P(("tp", "pd"), None),
        ),
        out_specs=(P(("grp", "tp", "pd"), None, None, None), P("grp", ("tp", "pd"))),
        check_vma=False,
    )
```

```python
import functools
import math

import jax
import jax.numpy as jnp
from jax import lax
from jax.experimental import pallas as pl
from jax.experimental.pallas import tpu as pltpu
from jax.sharding import PartitionSpec as P

HD = 128
KVH = 8
GQ = 8
PAGE = 16
REQ_DEV = 2
NEWP = 128
ARRIVE = REQ_DEV * NEWP
MIB = 1024 * 1024
BOTH = ("tp", "pd")
SPLIT = 4

VM = pl.BlockSpec(memory_space=pltpu.VMEM)
SM = pl.BlockSpec(memory_space=pltpu.SMEM)
ANY = pl.BlockSpec(memory_space=pl.ANY)
HBM = pl.BlockSpec(memory_space=pltpu.HBM)


def in_vmem(x):
    return pltpu.with_memory_space_constraint(x, pltpu.VMEM)


def in_hbm(x):
    return pltpu.with_memory_space_constraint(x, pltpu.HBM)


def pack_kernel(members, place, pages, pool, *refs):
    count = members - 1
    outs = refs[:count]
    packed, held, own, counts, sems, load_sems = refs[count:]
    member, half = place[0], place[1]
    slots = pool.shape[0]
    per_peer = ARRIVE // members
    parts = 4
    step = slots // parts

    @pl.when(half == 0)
    def _():
        own_copy = pltpu.make_async_copy(pages, own, load_sems.at[parts])
        own_copy.start()
        loads = []
        for i in range(parts):
            window = pl.ds(i * step, step)
            loads.append(
                pltpu.make_async_copy(pool.at[window], held.at[window], load_sems.at[i])
            )
            loads[-1].start()
        own_copy.wait()
        start = member * slots

        if members <= 8:
            carry = (jnp.int32(0), jnp.int32(0))
            for i in range(parts):
                loads[i].wait()

                def body(j, words, base=i * step):
                    low, high = words
                    entry = own[start + base + j]
                    ahead = lax.rem((entry >> 8) - member + members + 1, members)
                    leaves = entry >= 0
                    shift = (ahead & 3) * 8
                    is_low = ahead < 4
                    count = (jnp.where(is_low, low, high) >> shift) & 255
                    one = jnp.where(leaves, jnp.int32(1) << shift, 0)
                    packed[jnp.where(leaves, ahead * per_peer + count, ARRIVE)] = held[base + j]
                    return (
                        low + jnp.where(is_low, one, 0),
                        high + jnp.where(is_low, 0, one),
                    )

                carry = lax.fori_loop(0, step, body, carry, unroll=6)
        else:
            for i in range(parts):
                loads[i].wait()

            @pl.loop(0, members + 1)
            def _(i):
                counts[i] = 0

            @pl.loop(0, slots)
            def _(i):
                entry = own[start + i]
                ahead = lax.rem((entry >> 8) - member + members + 1, members)
                row = jnp.where(entry >= 0, ahead, members)
                count = counts[row]
                counts[row] = count + 1
                packed[jnp.where(entry >= 0, row * per_peer + count, ARRIVE)] = held[i]

        copies = []
        near, own_chunk, *far = outs
        moves = [(near, 0, 0), (near, per_peer, 2), (own_chunk, 0, 1)]
        moves += [(out, 0, 3 + i) for i, out in enumerate(far)]
        for i, (out, first, row) in enumerate(moves):
            copies.append(
                pltpu.make_async_copy(
                    packed.at[pl.ds(row * per_peer, per_peer)],
                    out.at[pl.ds(first, per_peer)],
                    sems.at[i],
                )
            )
            copies[-1].start()
        for copy in copies:
            copy.wait()


def pack(place, pages, pool):
    members = lax.axis_size("tp")
    per_peer = ARRIVE // members
    chunk = pool.shape[1:]
    return pl.pallas_call(
        functools.partial(pack_kernel, members),
        out_shape=[pltpu.HBM((2 * per_peer, *chunk), pool.dtype)]
        + [pltpu.HBM((per_peer, *chunk), pool.dtype)] * (members - 2),
        in_specs=[SM, HBM, HBM],
        out_specs=[HBM] * (members - 1),
        scratch_shapes=[
            pltpu.VMEM((ARRIVE + 1, *chunk), pool.dtype),
            pltpu.VMEM(pool.shape, pool.dtype),
            pltpu.SMEM(pages.shape, jnp.int32),
            pltpu.SMEM((members + 1,), jnp.int32),
            pltpu.SemaphoreType.DMA((members,)),
            pltpu.SemaphoreType.DMA((5,)),
        ],
        compiler_params=pltpu.CompilerParams(vmem_limit_bytes=8 * MIB),
        name="pack_pages",
    )(place, in_hbm(pages), in_hbm(pool))


def prepare_kernel(count, parts, groups, place, listed, lengths_hbm, table_hbm, *refs):
    sources = refs[:count]
    held = refs[len(refs) - 8 - parts : -8]
    bias, landing, entries, whole, part, lengths, table, sems = refs[-8:]
    small = [
        pltpu.make_async_copy(lengths_hbm, lengths, sems.at[parts]),
        pltpu.make_async_copy(table_hbm, table, sems.at[parts + 1]),
    ]
    for copy in small:
        copy.start()
    copies = []
    for source in sources:
        done = 0
        while done < source.shape[0]:
            part_out = held[len(copies)]
            window = pl.ds(done, part_out.shape[0])
            copies.append(
                pltpu.make_async_copy(source.at[window], part_out, sems.at[len(copies)])
            )
            copies[-1].start()
            done += part_out.shape[0]

    member = place[0]
    entries[...] = jnp.full(entries.shape, -1, jnp.int32)
    entries[:, : listed.shape[1]] = listed[...]
    entry = entries[...]
    members, lanes = entry.shape
    per_peer = ARRIVE // members
    wanted = (entry >= 0) & ((entry >> 8) == member)
    before = lax.broadcasted_iota(jnp.int32, (lanes, lanes), 0) < lax.broadcasted_iota(
        jnp.int32, (lanes, lanes), 1
    )
    rank = jnp.dot(
        jnp.where(wanted, 1.0, 0.0).astype(jnp.bfloat16),
        jnp.where(before, 1.0, 0.0).astype(jnp.bfloat16),
        preferred_element_type=jnp.float32,
    ).astype(jnp.int32)
    column = lax.broadcasted_iota(jnp.int32, landing.shape, 1)
    found = jnp.zeros(landing.shape, jnp.int32)
    for c in range(per_peer):
        slot = jnp.sum(jnp.where(wanted & (rank == c), entry & 255, 0), axis=1, keepdims=True)
        found = jnp.where(column == c, slot, found)
    landing[...] = found

    for copy in small:
        copy.wait()
    rows, pages = table.shape
    wide = whole.shape[1]
    base = lax.rem(member, groups) * rows
    columns = table[...].T
    page_id = lax.broadcasted_iota(jnp.int32, (pages, wide), 0)
    slot_id = lax.broadcasted_iota(jnp.int32, (pages, wide), 1)
    row_id = lax.broadcasted_iota(jnp.int32, (rows, 128), 0)
    over = jnp.zeros((rows, 128), jnp.int32)
    for r in range(rows):
        length = lengths[base + r]
        full = length // PAGE
        over = jnp.where(row_id == r, length - full * PAGE, over)
        hit = columns[:, r : r + 1] == slot_id
        in_whole = jnp.where(hit & (page_id < full), 1.0, 0.0)
        in_part = jnp.where(hit & (page_id == full), 1.0, 0.0)
        whole[r : r + 1, :] = jnp.sum(in_whole, axis=0, keepdims=True)
        part[r : r + 1, :] = jnp.sum(in_part, axis=0, keepdims=True)
    whole_b = whole[...].astype(jnp.bfloat16)
    part_b = part[...].astype(jnp.bfloat16)
    lane = lax.broadcasted_iota(jnp.int32, (rows, 128), 1)
    inside = (lane % PAGE) < over
    per_block = 128 // PAGE
    slot_in = lax.broadcasted_iota(jnp.int32, (wide, 128), 0)
    lane_in = lax.broadcasted_iota(jnp.int32, (wide, 128), 1) // PAGE
    for i in range(bias.shape[1] // 128):
        expand = jnp.where(slot_in == lane_in + i * per_block, 1.0, 0.0).astype(jnp.bfloat16)
        times = jnp.dot(whole_b, expand, preferred_element_type=jnp.float32)
        extra = jnp.dot(part_b, expand, preferred_element_type=jnp.float32)
        bias[:, i * 128 : (i + 1) * 128] = jnp.log(times + jnp.where(inside, extra, 0.0))

    for copy in copies:
        copy.wait()


def prepare(place, lengths, tables, listed, groups, weights, first):
    rows = tables.shape[0]
    members, slots = listed.shape
    wide = -(-slots // 128) * 128
    moved = sum(w.size * w.dtype.itemsize for w, _ in weights)
    pieces = [
        pltpu.VMEM((w.shape[0] // n, w.shape[1]), w.dtype) for w, n in weights for _ in range(n)
    ]
    weights = [w for w, _ in weights]
    count, parts = len(weights), len(pieces)
    return pl.pallas_call(
        functools.partial(prepare_kernel, count, parts, groups),
        out_shape=pieces
        + [
            jax.ShapeDtypeStruct((rows, slots * PAGE), jnp.float32),
            jax.ShapeDtypeStruct((members, 128), jnp.int32),
        ],
        in_specs=[SM, VM] + [HBM] * (2 + count + len(first)),
        out_specs=[VM] * (parts + 2),
        scratch_shapes=[
            pltpu.VMEM((members, wide), jnp.int32),
            pltpu.VMEM((rows, wide), jnp.float32),
            pltpu.VMEM((rows, wide), jnp.float32),
            pltpu.SMEM(lengths.shape, lengths.dtype),
            pltpu.VMEM(tables.shape, tables.dtype),
            pltpu.SemaphoreType.DMA((parts + 2,)),
        ],
        compiler_params=pltpu.CompilerParams(vmem_limit_bytes=6 * MIB),
        cost_estimate=pl.CostEstimate(flops=0, bytes_accessed=moved, transcendentals=0),
        name="prepare",
    )(place, listed, *[in_hbm(x) for x in (lengths, tables, *weights, *first)])


def attend_kernel(members, steps, chunks, place, landing, old_pool, bias, new_k, new_v, *refs):
    asked, refs = refs[:steps], refs[steps:]
    arrived, refs = refs[:-6], refs[-6:]
    kv_out, att_low, att_high, pool, scores, sems = refs
    member, half = place[0], place[1]
    slots = pool.shape[0]
    resident = slots - ARRIVE
    per_peer = ARRIVE // members
    rows = bias.shape[0]
    count = rows * steps * GQ

    @pl.when(half == 0)
    def _():
        copy = pltpu.make_async_copy(old_pool, pool, sems.at[0])
        copy.start()
        att_low[...] = jnp.zeros_like(att_low)
        att_high[...] = jnp.zeros_like(att_high)
        copy.wait()
        copy_out = pltpu.make_async_copy(pool, kv_out, sems.at[1])
        copy_out.start()
        copy_out.wait()

    @pl.when(half == 1)
    def _():
        copy = pltpu.make_async_copy(
            old_pool.at[pl.ds(0, resident)], pool.at[pl.ds(0, resident)], sems.at[0]
        )
        copy.start()
        for i, first, k in chunks:
            source = lax.rem(member - k + members, members)

            @pl.loop(0, per_peer, unroll=math.gcd(per_peer, 8))
            def _(c):
                pool[resident + landing[source, c]] = arrived[i][first + c]

        copy.wait()
        copy_out = pltpu.make_async_copy(pool, kv_out, sems.at[1])
        copy_out.start()

        scale = 1.0 / math.sqrt(HD)
        q = jnp.concatenate(
            [ask[:, j * HD : (j + 1) * HD] for j in range(GQ) for ask in asked], axis=0
        )
        nt = (((1,), (1,)), ((), ()))
        group = 24
        width = group * PAGE
        lanes = 128
        fresh = lax.dot_general(q, new_k[...], nt, preferred_element_type=jnp.float32) * scale
        q_id = lax.broadcasted_iota(jnp.int32, fresh.shape, 0)
        t_id = lax.broadcasted_iota(jnp.int32, fresh.shape, 1)
        allowed = (q_id % rows == t_id // steps) & (t_id % steps <= (q_id // rows) % steps)
        fresh = jnp.where(allowed, fresh, -jnp.inf)
        peak = fresh
        for c in range(slots // group):
            keys = pool[c * group : (c + 1) * group, 0].reshape(width, HD)
            s = lax.dot_general(q, keys, nt, preferred_element_type=jnp.float32) * scale
            b = bias[:, c * width : (c + 1) * width]
            s = (s.reshape(count // rows, rows, width) + b[None]).reshape(count, width)
            scores[:, c * width : (c + 1) * width] = s
            for i in range(width // lanes):
                peak = jnp.maximum(peak, s[:, i * lanes : (i + 1) * lanes])
        top = jnp.max(peak, axis=1, keepdims=True)
        p = jnp.exp(fresh - top)
        total = p
        acc = jnp.dot(p.astype(jnp.bfloat16), new_v[...], preferred_element_type=jnp.float32)
        for c in range(slots // group):
            p = jnp.exp(scores[:, c * width : (c + 1) * width] - top)
            for i in range(width // lanes):
                total = total + p[:, i * lanes : (i + 1) * lanes]
            values = pool[c * group : (c + 1) * group, 1].reshape(width, HD)
            acc = acc + jnp.dot(p.astype(jnp.bfloat16), values, preferred_element_type=jnp.float32)
        out = (acc / jnp.sum(total, axis=1, keepdims=True)).astype(jnp.bfloat16)
        tokens = rows * steps
        for j in range(GQ // 2):
            att_low[:, j * HD : (j + 1) * HD] = out[j * tokens : (j + 1) * tokens]
            other = j + GQ // 2
            att_high[:, j * HD : (j + 1) * HD] = out[other * tokens : (other + 1) * tokens]
        copy_out.wait()


def place_and_attend(place, landing, old_pool, bias, new_k, new_v, asked, arrived, chunks):
    members = landing.shape[0]
    slots = old_pool.shape[0]
    rows = bias.shape[0]
    steps = len(asked)
    tokens = rows * steps
    return pl.pallas_call(
        functools.partial(attend_kernel, members, steps, chunks),
        out_shape=[
            jax.ShapeDtypeStruct(old_pool.shape, old_pool.dtype),
            jax.ShapeDtypeStruct((tokens, GQ * HD // 2), jnp.bfloat16),
            jax.ShapeDtypeStruct((tokens, GQ * HD // 2), jnp.bfloat16),
        ],
        in_specs=[SM, SM, HBM, VM, VM, VM] + [VM] * (steps + len(arrived)),
        out_specs=[HBM, VM, VM],
        scratch_shapes=[
            pltpu.VMEM(old_pool.shape, old_pool.dtype),
            pltpu.VMEM((tokens * GQ, slots * PAGE), jnp.float32),
            pltpu.SemaphoreType.DMA((2,)),
        ],
        compiler_params=pltpu.CompilerParams(vmem_limit_bytes=9 * MIB),
        name="place_attend",
    )(
        place,
        landing,
        in_hbm(old_pool),
        bias,
        new_k,
        new_v,
        *asked,
        *arrived,
    )


def project_kernel(groups, place, weight, stream, mine, sibling, res_out):
    half = place[1]
    members, tokens, width = mine.shape
    sums = [stream[g * tokens : (g + 1) * tokens].astype(jnp.float32) for g in range(groups)]
    for h in range(KVH):
        for g in range(groups):
            m = h * groups + g
            first = jnp.where(half == 0, mine[m], sibling[m])
            second = jnp.where(half == 0, sibling[m], mine[m])
            sums[g] = sums[g] + lax.dot_general(
                jnp.concatenate([first, second], axis=1),
                weight[:, 2 * h * width : 2 * (h + 1) * width],
                (((1,), (1,)), ((), ())),
                preferred_element_type=jnp.float32,
            )
    for g in range(groups):
        res_out[g * tokens : (g + 1) * tokens] = sums[g].astype(res_out.dtype)


def project(place, weight, stream, mine, sibling, groups):
    return pl.pallas_call(
        functools.partial(project_kernel, groups),
        out_shape=jax.ShapeDtypeStruct(stream.shape, jnp.bfloat16),
        in_specs=[SM, VM, VM, VM, VM],
        out_specs=VM,
        compiler_params=pltpu.CompilerParams(vmem_limit_bytes=4 * MIB),
        name="out_projection",
    )(place, in_vmem(weight), stream, mine, sibling)


def ffn_kernel(place, mine, sibling, gain, gate, *refs):
    up = refs[:SPLIT]
    down, own_out, other_out, down_buf, normed, hidden, down_sem = refs[SPLIT:]
    half = place[1]
    members, tokens, width = mine.shape
    depth, hidden_count = up[0].shape
    features = depth * SPLIT
    down_copies = []
    for t in range(members):
        cols = pl.ds(t * 2 * width, 2 * width)
        down_copies.append(
            pltpu.make_async_copy(down.at[:, cols], down_buf.at[:, cols], down_sem.at[t])
        )
        down_copies[-1].start()

    square = jnp.zeros((tokens, width), jnp.float32)
    for block in (mine, sibling):
        for t in range(members):
            x = block[t].astype(jnp.float32)
            square = square + x * x
    factor = lax.rsqrt(jnp.sum(square, axis=1, keepdims=True) / features + 1e-05)
    for t in range(members):
        first = jnp.where(half == 0, mine[t], sibling[t])
        second = jnp.where(half == 0, sibling[t], mine[t])
        x = jnp.concatenate([first, second], axis=1).astype(jnp.float32)
        cols = slice(2 * t * width, 2 * (t + 1) * width)
        normed[:, cols] = (x * factor * gain[cols][None, :]).astype(jnp.bfloat16)
    tile = min(256, hidden_count)
    for f in range(hidden_count // tile):
        cols = slice(f * tile, (f + 1) * tile)
        gate_act = jnp.dot(normed[...], gate[:, cols], preferred_element_type=jnp.float32)
        up_act = 0.0
        for i in range(SPLIT):
            x = normed[:, i * depth : (i + 1) * depth]
            up_act += jnp.dot(x, up[i][:, cols], preferred_element_type=jnp.float32)
        h = gate_act / (1.0 + jnp.exp(-gate_act)) * up_act
        hidden[:, cols] = h.astype(jnp.bfloat16)
    for t in range(members):
        down_copies[t].wait()
        part = jnp.dot(
            hidden[...],
            down_buf[:, 2 * t * width : 2 * (t + 1) * width],
            preferred_element_type=jnp.float32,
        )
        first, second = part[:, :width], part[:, width:]
        own_out[t] = jnp.where(half == 0, first, second)
        other_out[t] = jnp.where(half == 0, second, first).astype(jnp.bfloat16)


def feed_forward(place, mine, sibling, gain, gate, up, down):
    tokens = mine.shape[1]
    hidden_count, features = down.shape
    return pl.pallas_call(
        ffn_kernel,
        out_shape=[
            jax.ShapeDtypeStruct(mine.shape, jnp.float32),
            jax.ShapeDtypeStruct(mine.shape, jnp.bfloat16),
        ],
        in_specs=[SM, VM, VM, VM] + [VM] * (1 + SPLIT) + [HBM],
        out_specs=[VM, VM],
        scratch_shapes=[
            pltpu.VMEM(down.shape, down.dtype),
            pltpu.VMEM((tokens, features), jnp.bfloat16),
            pltpu.VMEM((tokens, hidden_count), jnp.bfloat16),
            pltpu.SemaphoreType.DMA((mine.shape[0],)),
        ],
        compiler_params=pltpu.CompilerParams(vmem_limit_bytes=19 * MIB),
        name="feed_forward",
    )(place, mine, sibling, gain, *map(in_vmem, (gate, *up)), in_hbm(down))


def local(
    kv_pages,
    page_list,
    block_tables,
    lengths,
    queries,
    fresh_kv,
    stream,
    out_proj,
    norm_gain,
    gate_weight,
    up_weight,
    down_weight,
):
    members = lax.axis_size("tp")
    member = lax.axis_index("tp")
    half = lax.axis_index("pd")
    place = jnp.stack([member, half]).astype(jnp.int32)
    slots = kv_pages.shape[0]
    per_peer = ARRIVE // members
    groups = members // KVH
    rows = block_tables.shape[0]
    steps = queries.shape[1]
    tokens = rows * steps

    def send(x, *hops):
        route = [
            (2 * t + start, 2 * ((t + k) % members) + end)
            for start, k, end in hops
            for t in range(members)
        ]
        return lax.ppermute(x, BOTH, route)

    def swap(x):
        return lax.ppermute(x, "pd", [(0, 1), (1, 0)])

    near, own_chunk, *far = pack(place, page_list, kv_pages)
    far = dict(zip(range(2, members - 1), far))
    crossed = lax.ppermute(near, "pd", [(0, 1)])
    behind, ahead = crossed[:per_peer], crossed[per_peer:]
    hosts = (2, members - 2)
    middle = sorted(set(far) - set(hosts), key=lambda k: abs(k - members // 2))
    arrived = {k: send(far[k], (0, k, 1)) for k in middle}
    for host, k, block in zip(hosts, (1, -1), (ahead, behind)):
        block = jnp.where(half == 0, far[host], block)
        arrived[host] = send(block, (0, host, 1), (1, k, 0))

    *held, bias, landing = prepare(
        place,
        lengths,
        block_tables,
        page_list.reshape(members, slots),
        groups,
        ((up_weight, SPLIT),),
        (near,),
    )

    arrived, landing = lax.optimization_barrier((arrived, landing))
    last = lax.ppermute(
        jnp.concatenate([own_chunk] + [arrived[host] for host in hosts]), "pd", [(0, 1)]
    )
    arrays = [last] + [arrived[k] for k in sorted(arrived)]
    chunks = [(0, 0, 0), (0, per_peer, 1), (0, 2 * per_peer, members - 1)]
    chunks += [(i + 1, 0, k) for i, k in enumerate(sorted(arrived))]
    padding = ((0, -tokens % 128), (0, 0))
    new_k = jnp.pad(fresh_kv[:, :, 0].reshape(tokens, HD), padding)
    new_v = jnp.pad(fresh_kv[:, :, 1].reshape(tokens, HD), padding)
    asked = [queries[:, st] for st in range(steps)]
    kv_after, att_low, att_high = place_and_attend(
        place, landing, kv_pages, bias, new_k, new_v, asked, arrays, chunks
    )

    def everywhere(x):
        spread = jnp.broadcast_to(x[None], (members, *x.shape))
        mine = lax.all_to_all(spread, "tp", split_axis=0, concat_axis=0)
        return mine, swap(mine)

    att_mine = att_high + lax.ppermute(att_low, "pd", [(1, 0)])
    here, there = everywhere(att_mine)

    inner = stream.reshape(steps, groups, rows, -1).transpose(1, 0, 2, 3).reshape(stream.shape)
    residual = project(place, out_proj, inner, here, there, groups)

    mine, sibling = everywhere(residual)
    own, other = feed_forward(
        place, mine, sibling, norm_gain, gate_weight, held, down_weight
    )
    summed = (own + swap(other).astype(jnp.float32)).astype(jnp.bfloat16)
    shares = lax.all_to_all(summed, "tp", split_axis=0, concat_axis=0)
    layer = residual.astype(jnp.float32) + jnp.sum(shares.astype(jnp.float32), axis=0)
    layer_out = (
        layer.astype(jnp.bfloat16)
        .reshape(groups, steps, rows, -1)
        .transpose(1, 0, 2, 3)
        .reshape(stream.shape)
    )
    return (kv_after, layer_out)


def solution(mesh):
    return jax.shard_map(
        local,
        mesh=mesh,
        in_specs=(
            P(("grp", "tp", "pd"), None, None, None),
            P("grp"),
            P(("grp", "tp"), None),
            P("grp"),
            P(("grp", "tp"), None, None),
            P(("grp", "tp"), None, None, None),
            P("grp", ("tp", "pd")),
            P(("tp", "pd"), None),
            P(),
            P(None, ("tp", "pd")),
            P(None, ("tp", "pd")),
            P(("tp", "pd"), None),
        ),
        out_specs=(P(("grp", "tp", "pd"), None, None, None), P("grp", ("tp", "pd"))),
        check_vma=False,
    )
```

```python
import functools
import math

import jax
import jax.numpy as jnp
from jax import lax
from jax.experimental import pallas as pl
from jax.experimental.pallas import tpu as pltpu
from jax.sharding import PartitionSpec as P

HD = 128
KVH = 8
GQ = 8
PAGE = 16
REQ_DEV = 2
NEWP = 128
ARRIVE = REQ_DEV * NEWP
MIB = 1024 * 1024
BOTH = ("tp", "pd")
SPLIT = 4

VM = pl.BlockSpec(memory_space=pltpu.VMEM)
SM = pl.BlockSpec(memory_space=pltpu.SMEM)
ANY = pl.BlockSpec(memory_space=pl.ANY)
HBM = pl.BlockSpec(memory_space=pltpu.HBM)


def in_vmem(x):
    return pltpu.with_memory_space_constraint(x, pltpu.VMEM)


def in_hbm(x):
    return pltpu.with_memory_space_constraint(x, pltpu.HBM)


def pack_kernel(members, place, pages, pool, *refs):
    count = members - 1
    outs = refs[:count]
    packed, held, own, counts, sems, load_sems = refs[count:]
    member, half = place[0], place[1]
    slots = pool.shape[0]
    per_peer = ARRIVE // members
    parts = 4
    step = slots // parts

    @pl.when(half == 0)
    def _():
        own_copy = pltpu.make_async_copy(pages, own, load_sems.at[parts])
        own_copy.start()
        loads = []
        for i in range(parts):
            window = pl.ds(i * step, step)
            loads.append(
                pltpu.make_async_copy(pool.at[window], held.at[window], load_sems.at[i])
            )
            loads[-1].start()
        own_copy.wait()
        start = member * slots

        if members in (4, 8):
            carry = (jnp.int32(0), jnp.int32(0))
            for i in range(parts):
                loads[i].wait()

                def body(j, words, base=i * step):
                    low, high = words
                    entry = own[start + base + j]
                    ahead = ((entry >> 8) - member + 1) & (members - 1)
                    leaves = entry >= 0
                    shift = (ahead & 3) * 8
                    is_low = ahead < 4
                    count = (jnp.where(is_low, low, high) >> shift) & 255
                    one = jnp.where(leaves, jnp.int32(1) << shift, 0)
                    packed[jnp.where(leaves, ahead * per_peer + count, ARRIVE)] = held[base + j]
                    return (
                        low + jnp.where(is_low, one, 0),
                        high + jnp.where(is_low, 0, one),
                    )

                carry = lax.fori_loop(0, step, body, carry, unroll=13)
        else:
            for i in range(parts):
                loads[i].wait()

            @pl.loop(0, members + 1)
            def _(i):
                counts[i] = 0

            @pl.loop(0, slots)
            def _(i):
                entry = own[start + i]
                ahead = lax.rem((entry >> 8) - member + members + 1, members)
                row = jnp.where(entry >= 0, ahead, members)
                count = counts[row]
                counts[row] = count + 1
                packed[jnp.where(entry >= 0, row * per_peer + count, ARRIVE)] = held[i]

        copies = []
        near, own_chunk, *far = outs
        moves = [(near, 0, 0), (near, per_peer, 2), (own_chunk, 0, 1)]
        moves += [(out, 0, 3 + i) for i, out in enumerate(far)]
        for i, (out, first, row) in enumerate(moves):
            copies.append(
                pltpu.make_async_copy(
                    packed.at[pl.ds(row * per_peer, per_peer)],
                    out.at[pl.ds(first, per_peer)],
                    sems.at[i],
                )
            )
            copies[-1].start()
        for copy in copies:
            copy.wait()


def pack(place, pages, pool):
    members = lax.axis_size("tp")
    per_peer = ARRIVE // members
    chunk = pool.shape[1:]
    return pl.pallas_call(
        functools.partial(pack_kernel, members),
        out_shape=[pltpu.HBM((2 * per_peer, *chunk), pool.dtype)]
        + [pltpu.HBM((per_peer, *chunk), pool.dtype)] * (members - 2),
        in_specs=[SM, HBM, HBM],
        out_specs=[HBM] * (members - 1),
        scratch_shapes=[
            pltpu.VMEM((ARRIVE + 1, *chunk), pool.dtype),
            pltpu.VMEM(pool.shape, pool.dtype),
            pltpu.SMEM(pages.shape, jnp.int32),
            pltpu.SMEM((members + 1,), jnp.int32),
            pltpu.SemaphoreType.DMA((members,)),
            pltpu.SemaphoreType.DMA((5,)),
        ],
        compiler_params=pltpu.CompilerParams(vmem_limit_bytes=8 * MIB),
        name="pack_pages",
    )(place, in_hbm(pages), in_hbm(pool))


def prepare_kernel(count, parts, groups, place, listed, lengths_hbm, table_hbm, *refs):
    sources = refs[:count]
    held = refs[len(refs) - 8 - parts : -8]
    bias, landing, entries, whole, part, lengths, table, sems = refs[-8:]
    small = [
        pltpu.make_async_copy(lengths_hbm, lengths, sems.at[parts]),
        pltpu.make_async_copy(table_hbm, table, sems.at[parts + 1]),
    ]
    for copy in small:
        copy.start()
    copies = []
    for source in sources:
        done = 0
        while done < source.shape[0]:
            part_out = held[len(copies)]
            window = pl.ds(done, part_out.shape[0])
            copies.append(
                pltpu.make_async_copy(source.at[window], part_out, sems.at[len(copies)])
            )
            copies[-1].start()
            done += part_out.shape[0]

    member = place[0]
    entries[...] = jnp.full(entries.shape, -1, jnp.int32)
    entries[:, : listed.shape[1]] = listed[...]
    entry = entries[...]
    members, lanes = entry.shape
    per_peer = ARRIVE // members
    wanted = (entry >= 0) & ((entry >> 8) == member)
    before = lax.broadcasted_iota(jnp.int32, (lanes, lanes), 0) < lax.broadcasted_iota(
        jnp.int32, (lanes, lanes), 1
    )
    rank = jnp.dot(
        jnp.where(wanted, 1.0, 0.0).astype(jnp.bfloat16),
        jnp.where(before, 1.0, 0.0).astype(jnp.bfloat16),
        preferred_element_type=jnp.float32,
    ).astype(jnp.int32)
    column = lax.broadcasted_iota(jnp.int32, landing.shape, 1)
    found = jnp.zeros(landing.shape, jnp.int32)
    for c in range(per_peer):
        slot = jnp.sum(jnp.where(wanted & (rank == c), entry & 255, 0), axis=1, keepdims=True)
        found = jnp.where(column == c, slot, found)
    landing[...] = found

    for copy in small:
        copy.wait()
    rows, pages = table.shape
    wide = whole.shape[1]
    base = lax.rem(member, groups) * rows
    columns = table[...].T
    page_id = lax.broadcasted_iota(jnp.int32, (pages, wide), 0)
    slot_id = lax.broadcasted_iota(jnp.int32, (pages, wide), 1)
    row_id = lax.broadcasted_iota(jnp.int32, (rows, 128), 0)
    over = jnp.zeros((rows, 128), jnp.int32)
    for r in range(rows):
        length = lengths[base + r]
        full = length // PAGE
        over = jnp.where(row_id == r, length - full * PAGE, over)
        hit = columns[:, r : r + 1] == slot_id
        in_whole = jnp.where(hit & (page_id < full), 1.0, 0.0)
        in_part = jnp.where(hit & (page_id == full), 1.0, 0.0)
        whole[r : r + 1, :] = jnp.sum(in_whole, axis=0, keepdims=True)
        part[r : r + 1, :] = jnp.sum(in_part, axis=0, keepdims=True)
    whole_b = whole[...].astype(jnp.bfloat16)
    part_b = part[...].astype(jnp.bfloat16)
    lane = lax.broadcasted_iota(jnp.int32, (rows, 128), 1)
    inside = (lane % PAGE) < over
    per_block = 128 // PAGE
    slot_in = lax.broadcasted_iota(jnp.int32, (wide, 128), 0)
    lane_in = lax.broadcasted_iota(jnp.int32, (wide, 128), 1) // PAGE
    for i in range(bias.shape[1] // 128):
        expand = jnp.where(slot_in == lane_in + i * per_block, 1.0, 0.0).astype(jnp.bfloat16)
        times = jnp.dot(whole_b, expand, preferred_element_type=jnp.float32)
        extra = jnp.dot(part_b, expand, preferred_element_type=jnp.float32)
        bias[:, i * 128 : (i + 1) * 128] = jnp.log(times + jnp.where(inside, extra, 0.0))

    for copy in copies:
        copy.wait()


def prepare(place, lengths, tables, listed, groups, weights, first):
    rows = tables.shape[0]
    members, slots = listed.shape
    wide = -(-slots // 128) * 128
    moved = sum(w.size * w.dtype.itemsize for w, _ in weights)
    pieces = [
        pltpu.VMEM((w.shape[0] // n, w.shape[1]), w.dtype) for w, n in weights for _ in range(n)
    ]
    weights = [w for w, _ in weights]
    count, parts = len(weights), len(pieces)
    return pl.pallas_call(
        functools.partial(prepare_kernel, count, parts, groups),
        out_shape=pieces
        + [
            jax.ShapeDtypeStruct((rows, slots * PAGE), jnp.float32),
            jax.ShapeDtypeStruct((members, 128), jnp.int32),
        ],
        in_specs=[SM, VM] + [HBM] * (2 + count + len(first)),
        out_specs=[VM] * (parts + 2),
        scratch_shapes=[
            pltpu.VMEM((members, wide), jnp.int32),
            pltpu.VMEM((rows, wide), jnp.float32),
            pltpu.VMEM((rows, wide), jnp.float32),
            pltpu.SMEM(lengths.shape, lengths.dtype),
            pltpu.VMEM(tables.shape, tables.dtype),
            pltpu.SemaphoreType.DMA((parts + 2,)),
        ],
        compiler_params=pltpu.CompilerParams(vmem_limit_bytes=6 * MIB),
        cost_estimate=pl.CostEstimate(flops=0, bytes_accessed=moved, transcendentals=0),
        name="prepare",
    )(place, listed, *[in_hbm(x) for x in (lengths, tables, *weights, *first)])


def attend_kernel(members, steps, chunks, place, landing, old_pool, bias, new_k, new_v, *refs):
    asked, refs = refs[:steps], refs[steps:]
    arrived, refs = refs[:-6], refs[-6:]
    kv_out, att_low, att_high, pool, scores, sems = refs
    member, half = place[0], place[1]
    slots = pool.shape[0]
    resident = slots - ARRIVE
    per_peer = ARRIVE // members
    rows = bias.shape[0]
    count = rows * steps * GQ

    @pl.when(half == 0)
    def _():
        copy = pltpu.make_async_copy(old_pool, pool, sems.at[0])
        copy.start()
        att_low[...] = jnp.zeros_like(att_low)
        att_high[...] = jnp.zeros_like(att_high)
        copy.wait()
        copy_out = pltpu.make_async_copy(pool, kv_out, sems.at[1])
        copy_out.start()
        copy_out.wait()

    @pl.when(half == 1)
    def _():
        copy = pltpu.make_async_copy(
            old_pool.at[pl.ds(0, resident)], pool.at[pl.ds(0, resident)], sems.at[0]
        )
        copy.start()
        for i, first, k in chunks:
            source = lax.rem(member - k + members, members)

            @pl.loop(0, per_peer, unroll=math.gcd(per_peer, 8))
            def _(c):
                pool[resident + landing[source, c]] = arrived[i][first + c]

        copy.wait()
        copy_out = pltpu.make_async_copy(pool, kv_out, sems.at[1])
        copy_out.start()

        scale = 1.0 / math.sqrt(HD)
        q = jnp.concatenate(
            [ask[:, j * HD : (j + 1) * HD] for j in range(GQ) for ask in asked], axis=0
        )
        nt = (((1,), (1,)), ((), ()))
        group = 24
        width = group * PAGE
        lanes = 128
        fresh = lax.dot_general(q, new_k[...], nt, preferred_element_type=jnp.float32) * scale
        q_id = lax.broadcasted_iota(jnp.int32, fresh.shape, 0)
        t_id = lax.broadcasted_iota(jnp.int32, fresh.shape, 1)
        allowed = (q_id % rows == t_id // steps) & (t_id % steps <= (q_id // rows) % steps)
        fresh = jnp.where(allowed, fresh, -jnp.inf)
        peak = fresh
        for c in range(slots // group):
            keys = pool[c * group : (c + 1) * group, 0].reshape(width, HD)
            s = lax.dot_general(q, keys, nt, preferred_element_type=jnp.float32) * scale
            b = bias[:, c * width : (c + 1) * width]
            s = (s.reshape(count // rows, rows, width) + b[None]).reshape(count, width)
            scores[:, c * width : (c + 1) * width] = s
            for i in range(width // lanes):
                peak = jnp.maximum(peak, s[:, i * lanes : (i + 1) * lanes])
        top = jnp.max(peak, axis=1, keepdims=True)
        p = jnp.exp(fresh - top)
        total = p
        acc = jnp.dot(p.astype(jnp.bfloat16), new_v[...], preferred_element_type=jnp.float32)
        for c in range(slots // group):
            p = jnp.exp(scores[:, c * width : (c + 1) * width] - top)
            for i in range(width // lanes):
                total = total + p[:, i * lanes : (i + 1) * lanes]
            values = pool[c * group : (c + 1) * group, 1].reshape(width, HD)
            acc = acc + jnp.dot(p.astype(jnp.bfloat16), values, preferred_element_type=jnp.float32)
        out = (acc / jnp.sum(total, axis=1, keepdims=True)).astype(jnp.bfloat16)
        tokens = rows * steps
        for j in range(GQ // 2):
            att_low[:, j * HD : (j + 1) * HD] = out[j * tokens : (j + 1) * tokens]
            other = j + GQ // 2
            att_high[:, j * HD : (j + 1) * HD] = out[other * tokens : (other + 1) * tokens]
        copy_out.wait()


def place_and_attend(place, landing, old_pool, bias, new_k, new_v, asked, arrived, chunks):
    members = landing.shape[0]
    slots = old_pool.shape[0]
    rows = bias.shape[0]
    steps = len(asked)
    tokens = rows * steps
    return pl.pallas_call(
        functools.partial(attend_kernel, members, steps, chunks),
        out_shape=[
            jax.ShapeDtypeStruct(old_pool.shape, old_pool.dtype),
            jax.ShapeDtypeStruct((tokens, GQ * HD // 2), jnp.bfloat16),
            jax.ShapeDtypeStruct((tokens, GQ * HD // 2), jnp.bfloat16),
        ],
        in_specs=[SM, SM, HBM, VM, VM, VM] + [VM] * (steps + len(arrived)),
        out_specs=[HBM, VM, VM],
        scratch_shapes=[
            pltpu.VMEM(old_pool.shape, old_pool.dtype),
            pltpu.VMEM((tokens * GQ, slots * PAGE), jnp.float32),
            pltpu.SemaphoreType.DMA((2,)),
        ],
        compiler_params=pltpu.CompilerParams(vmem_limit_bytes=9 * MIB),
        name="place_attend",
    )(
        place,
        landing,
        in_hbm(old_pool),
        bias,
        new_k,
        new_v,
        *asked,
        *arrived,
    )


def member_bits(members):
    offsets = [0]
    for bit in reversed(range(members.bit_length() - 1)):
        offsets += [o ^ (1 << bit) for o in offsets]
    return offsets


def project_kernel(groups, place, *refs):
    *weight, stream, mine, sibling, res_out = refs
    member, half = place[0], place[1]
    members, tokens, width = mine.shape
    rows = weight[0].shape[0]
    sums = [
        [
            stream[g * tokens : (g + 1) * tokens, i * rows : (i + 1) * rows].astype(jnp.float32)
            for g in range(groups)
        ]
        for i in range(len(weight))
    ]
    for m, offset in enumerate(member_bits(members)):
        owner = member ^ offset
        first = jnp.where(half == 0, mine[m], sibling[m])
        second = jnp.where(half == 0, sibling[m], mine[m])
        x = jnp.concatenate([first, second], axis=1)
        head = pl.ds(pl.multiple_of(owner // groups * 2 * width, 2 * width), 2 * width)
        for i in range(len(weight)):
            part = lax.dot_general(
                x,
                weight[i][:, head],
                (((1,), (1,)), ((), ())),
                preferred_element_type=jnp.float32,
            )
            for g in range(groups):
                if groups > 1:
                    part_g = jnp.where(lax.rem(owner, groups) == g, part, 0.0)
                else:
                    part_g = part
                sums[i][g] = sums[i][g] + part_g
    for i in range(len(weight)):
        for g in range(groups):
            res_out[g * tokens : (g + 1) * tokens, i * rows : (i + 1) * rows] = sums[i][g].astype(
                res_out.dtype
            )


def project(place, weight, stream, mine, sibling, groups):
    return pl.pallas_call(
        functools.partial(project_kernel, groups),
        out_shape=jax.ShapeDtypeStruct(stream.shape, jnp.bfloat16),
        in_specs=[SM] + [VM] * (len(weight) + 3),
        out_specs=VM,
        compiler_params=pltpu.CompilerParams(vmem_limit_bytes=9 * MIB),
        name="out_projection",
    )(place, *map(in_vmem, weight), stream, mine, sibling)


def ffn_kernel(place, mine, sibling, gain, gate, *refs):
    up = refs[:SPLIT]
    down, own_out, other_out, down_buf, normed, hidden, down_sem = refs[SPLIT:]
    half = place[1]
    members, tokens, width = mine.shape
    depth, hidden_count = up[0].shape
    features = depth * SPLIT
    down_copies = []
    for t in range(members):
        cols = pl.ds(t * 2 * width, 2 * width)
        down_copies.append(
            pltpu.make_async_copy(down.at[:, cols], down_buf.at[:, cols], down_sem.at[t])
        )
        down_copies[-1].start()

    square = jnp.zeros((tokens, width), jnp.float32)
    for block in (mine, sibling):
        for t in range(members):
            x = block[t].astype(jnp.float32)
            square = square + x * x
    factor = lax.rsqrt(jnp.sum(square, axis=1, keepdims=True) / features + 1e-05)
    for t, offset in enumerate(member_bits(members)):
        first = jnp.where(half == 0, mine[t], sibling[t])
        second = jnp.where(half == 0, sibling[t], mine[t])
        x = jnp.concatenate([first, second], axis=1).astype(jnp.float32)
        owner = place[0] ^ offset
        cols = pl.ds(pl.multiple_of(owner * 2 * width, 2 * width), 2 * width)
        normed[:, cols] = (x * factor * gain[cols][None, :]).astype(jnp.bfloat16)
    tile = min(256, hidden_count)
    for f in range(hidden_count // tile):
        cols = slice(f * tile, (f + 1) * tile)
        gate_act = jnp.dot(normed[...], gate[:, cols], preferred_element_type=jnp.float32)
        up_act = 0.0
        for i in range(SPLIT):
            x = normed[:, i * depth : (i + 1) * depth]
            up_act += jnp.dot(x, up[i][:, cols], preferred_element_type=jnp.float32)
        h = gate_act / (1.0 + jnp.exp(-gate_act)) * up_act
        hidden[:, cols] = h.astype(jnp.bfloat16)
    for t in range(members):
        down_copies[t].wait()
        part = jnp.dot(
            hidden[...],
            down_buf[:, 2 * t * width : 2 * (t + 1) * width],
            preferred_element_type=jnp.float32,
        )
        first, second = part[:, :width], part[:, width:]
        own_out[t] = jnp.where(half == 0, first, second)
        other_out[t] = jnp.where(half == 0, second, first).astype(jnp.bfloat16)


def feed_forward(place, mine, sibling, gain, gate, up, down):
    tokens = mine.shape[1]
    hidden_count, features = down.shape
    return pl.pallas_call(
        ffn_kernel,
        out_shape=[
            jax.ShapeDtypeStruct(mine.shape, jnp.float32),
            jax.ShapeDtypeStruct(mine.shape, jnp.bfloat16),
        ],
        in_specs=[SM, VM, VM, VM] + [VM] * (1 + SPLIT) + [HBM],
        out_specs=[VM, VM],
        scratch_shapes=[
            pltpu.VMEM(down.shape, down.dtype),
            pltpu.VMEM((tokens, features), jnp.bfloat16),
            pltpu.VMEM((tokens, hidden_count), jnp.bfloat16),
            pltpu.SemaphoreType.DMA((mine.shape[0],)),
        ],
        compiler_params=pltpu.CompilerParams(vmem_limit_bytes=19 * MIB),
        name="feed_forward",
    )(place, mine, sibling, gain, *map(in_vmem, (gate, *up)), in_hbm(down))


def local(
    kv_pages,
    page_list,
    block_tables,
    lengths,
    queries,
    fresh_kv,
    stream,
    out_proj,
    norm_gain,
    gate_weight,
    up_weight,
    down_weight,
):
    members = lax.axis_size("tp")
    member = lax.axis_index("tp")
    half = lax.axis_index("pd")
    place = jnp.stack([member, half]).astype(jnp.int32)
    slots = kv_pages.shape[0]
    per_peer = ARRIVE // members
    groups = members // KVH
    rows = block_tables.shape[0]
    steps = queries.shape[1]
    tokens = rows * steps

    def send(x, *hops):
        route = [
            (2 * t + start, 2 * ((t + k) % members) + end)
            for start, k, end in hops
            for t in range(members)
        ]
        return lax.ppermute(x, BOTH, route)

    def swap(x):
        return lax.ppermute(x, "pd", [(0, 1), (1, 0)])

    near, own_chunk, *far = pack(place, page_list, kv_pages)
    far = dict(zip(range(2, members - 1), far))
    crossed = lax.ppermute(near, "pd", [(0, 1)])
    behind, ahead = crossed[:per_peer], crossed[per_peer:]
    hosts = (2, members - 2)
    middle = sorted(set(far) - set(hosts), key=lambda k: abs(k - members // 2))
    arrived = {k: send(far[k], (0, k, 1)) for k in middle}
    for host, k, block in zip(hosts, (1, -1), (ahead, behind)):
        block = jnp.where(half == 0, far[host], block)
        arrived[host] = send(block, (0, host, 1), (1, k, 0))

    *held, bias, landing = prepare(
        place,
        lengths,
        block_tables,
        page_list.reshape(members, slots),
        groups,
        ((out_proj, 2), (up_weight, SPLIT)),
        (near,),
    )

    arrived, landing = lax.optimization_barrier((arrived, landing))
    last = lax.ppermute(
        jnp.concatenate([own_chunk] + [arrived[host] for host in hosts]), "pd", [(0, 1)]
    )
    arrays = [last] + [arrived[k] for k in sorted(arrived)]
    chunks = [(0, 0, 0), (0, per_peer, 1), (0, 2 * per_peer, members - 1)]
    chunks += [(i + 1, 0, k) for i, k in enumerate(sorted(arrived))]
    padding = ((0, -tokens % 128), (0, 0))
    new_k = jnp.pad(fresh_kv[:, :, 0].reshape(tokens, HD), padding)
    new_v = jnp.pad(fresh_kv[:, :, 1].reshape(tokens, HD), padding)
    asked = [queries[:, st] for st in range(steps)]
    kv_after, att_low, att_high = place_and_attend(
        place, landing, kv_pages, bias, new_k, new_v, asked, arrays, chunks
    )

    def everywhere(x):
        blocks = x[None]
        for bit in reversed(range(members.bit_length() - 1)):
            route = [(t, t ^ (1 << bit)) for t in range(members)]
            blocks = jnp.concatenate([blocks, lax.ppermute(blocks, "tp", route)])
        return blocks, swap(blocks)

    att_mine = att_high + lax.ppermute(att_low, "pd", [(1, 0)])
    here, there = everywhere(att_mine)

    inner = stream.reshape(steps, groups, rows, -1).transpose(1, 0, 2, 3).reshape(stream.shape)
    residual = project(place, held[:2], inner, here, there, groups)

    mine, sibling = everywhere(residual)
    own, other = feed_forward(
        place, mine, sibling, norm_gain, gate_weight, held[2:], down_weight
    )
    summed = (own + swap(other).astype(jnp.float32)).astype(jnp.bfloat16)
    shares = lax.all_to_all(summed, "tp", split_axis=0, concat_axis=0)
    layer = residual.astype(jnp.float32) + jnp.sum(shares.astype(jnp.float32), axis=0)
    layer_out = (
        layer.astype(jnp.bfloat16)
        .reshape(groups, steps, rows, -1)
        .transpose(1, 0, 2, 3)
        .reshape(stream.shape)
    )
    return (kv_after, layer_out)


def solution(mesh):
    return jax.shard_map(
        local,
        mesh=mesh,
        in_specs=(
            P(("grp", "tp", "pd"), None, None, None),
            P("grp"),
            P(("grp", "tp"), None),
            P("grp"),
            P(("grp", "tp"), None, None),
            P(("grp", "tp"), None, None, None),
            P("grp", ("tp", "pd")),
            P(("tp", "pd"), None),
            P(),
            P(None, ("tp", "pd")),
            P(None, ("tp", "pd")),
            P(("tp", "pd"), None),
        ),
        out_specs=(P(("grp", "tp", "pd"), None, None, None), P("grp", ("tp", "pd"))),
        check_vma=False,
    )
```

```python
import functools
import math

import jax
import jax.numpy as jnp
from jax import lax
from jax.experimental import pallas as pl
from jax.experimental.pallas import tpu as pltpu
from jax.sharding import PartitionSpec as P

HD = 128
KVH = 8
GQ = 8
PAGE = 16
REQ_DEV = 2
NEWP = 128
ARRIVE = REQ_DEV * NEWP
MIB = 1024 * 1024
BOTH = ("tp", "pd")
SPLIT = 4

VM = pl.BlockSpec(memory_space=pltpu.VMEM)
SM = pl.BlockSpec(memory_space=pltpu.SMEM)
ANY = pl.BlockSpec(memory_space=pl.ANY)
HBM = pl.BlockSpec(memory_space=pltpu.HBM)


def in_vmem(x):
    return pltpu.with_memory_space_constraint(x, pltpu.VMEM)


def in_hbm(x):
    return pltpu.with_memory_space_constraint(x, pltpu.HBM)


def pack_kernel(members, place, pages, pool, *refs):
    count = members - 1
    outs = refs[:count]
    packed, held, own, counts, sems, load_sems = refs[count:]
    member, half = place[0], place[1]
    slots = pool.shape[0]
    per_peer = ARRIVE // members
    parts = 4
    step = slots // parts

    @pl.when(half == 0)
    def _():
        own_copy = pltpu.make_async_copy(pages, own, load_sems.at[parts])
        own_copy.start()
        loads = []
        for i in range(parts):
            window = pl.ds(i * step, step)
            loads.append(
                pltpu.make_async_copy(pool.at[window], held.at[window], load_sems.at[i])
            )
            loads[-1].start()
        own_copy.wait()
        start = member * slots

        if members in (4, 8):
            carry = (jnp.int32(0), jnp.int32(0))
            for i in range(parts):
                loads[i].wait()

                def body(j, words, base=i * step):
                    low, high = words
                    entry = own[start + base + j]
                    ahead = ((entry >> 8) - member + 1) & (members - 1)
                    leaves = entry >= 0
                    shift = (ahead & 3) * 8
                    is_low = ahead < 4
                    count = (jnp.where(is_low, low, high) >> shift) & 255
                    one = jnp.where(leaves, jnp.int32(1) << shift, 0)
                    packed[jnp.where(leaves, ahead * per_peer + count, ARRIVE)] = held[base + j]
                    return (
                        low + jnp.where(is_low, one, 0),
                        high + jnp.where(is_low, 0, one),
                    )

                carry = lax.fori_loop(0, step, body, carry, unroll=13)
        else:
            for i in range(parts):
                loads[i].wait()

            @pl.loop(0, members + 1)
            def _(i):
                counts[i] = 0

            @pl.loop(0, slots)
            def _(i):
                entry = own[start + i]
                ahead = lax.rem((entry >> 8) - member + members + 1, members)
                row = jnp.where(entry >= 0, ahead, members)
                count = counts[row]
                counts[row] = count + 1
                packed[jnp.where(entry >= 0, row * per_peer + count, ARRIVE)] = held[i]

        copies = []
        near, own_chunk, *far = outs
        moves = [(near, 0, 0), (near, per_peer, 2), (own_chunk, 0, 1)]
        moves += [(out, 0, 3 + i) for i, out in enumerate(far)]
        for i, (out, first, row) in enumerate(moves):
            copies.append(
                pltpu.make_async_copy(
                    packed.at[pl.ds(row * per_peer, per_peer)],
                    out.at[pl.ds(first, per_peer)],
                    sems.at[i],
                )
            )
            copies[-1].start()
        for copy in copies:
            copy.wait()


def pack(place, pages, pool):
    members = lax.axis_size("tp")
    per_peer = ARRIVE // members
    chunk = pool.shape[1:]
    return pl.pallas_call(
        functools.partial(pack_kernel, members),
        out_shape=[pltpu.HBM((2 * per_peer, *chunk), pool.dtype)]
        + [pltpu.HBM((per_peer, *chunk), pool.dtype)] * (members - 2),
        in_specs=[SM, HBM, HBM],
        out_specs=[HBM] * (members - 1),
        scratch_shapes=[
            pltpu.VMEM((ARRIVE + 1, *chunk), pool.dtype),
            pltpu.VMEM(pool.shape, pool.dtype),
            pltpu.SMEM(pages.shape, jnp.int32),
            pltpu.SMEM((members + 1,), jnp.int32),
            pltpu.SemaphoreType.DMA((members,)),
            pltpu.SemaphoreType.DMA((5,)),
        ],
        compiler_params=pltpu.CompilerParams(vmem_limit_bytes=8 * MIB),
        name="pack_pages",
    )(place, in_hbm(pages), in_hbm(pool))


def prepare_kernel(count, parts, groups, place, listed, lengths_hbm, table_hbm, *refs):
    sources = refs[:count]
    held = refs[len(refs) - 8 - parts : -8]
    bias, landing, entries, whole, part, lengths, table, sems = refs[-8:]
    small = [
        pltpu.make_async_copy(lengths_hbm, lengths, sems.at[parts]),
        pltpu.make_async_copy(table_hbm, table, sems.at[parts + 1]),
    ]
    for copy in small:
        copy.start()
    copies = []
    for source in sources:
        done = 0
        while done < source.shape[0]:
            part_out = held[len(copies)]
            window = pl.ds(done, part_out.shape[0])
            copies.append(
                pltpu.make_async_copy(source.at[window], part_out, sems.at[len(copies)])
            )
            copies[-1].start()
            done += part_out.shape[0]

    member = place[0]
    entries[...] = jnp.full(entries.shape, -1, jnp.int32)
    entries[:, : listed.shape[1]] = listed[...]
    entry = entries[...]
    members, lanes = entry.shape
    per_peer = ARRIVE // members
    wanted = (entry >= 0) & ((entry >> 8) == member)
    before = lax.broadcasted_iota(jnp.int32, (lanes, lanes), 0) < lax.broadcasted_iota(
        jnp.int32, (lanes, lanes), 1
    )
    rank = jnp.dot(
        jnp.where(wanted, 1.0, 0.0).astype(jnp.bfloat16),
        jnp.where(before, 1.0, 0.0).astype(jnp.bfloat16),
        preferred_element_type=jnp.float32,
    ).astype(jnp.int32)
    column = lax.broadcasted_iota(jnp.int32, landing.shape, 1)
    found = jnp.zeros(landing.shape, jnp.int32)
    for c in range(per_peer):
        slot = jnp.sum(jnp.where(wanted & (rank == c), entry & 255, 0), axis=1, keepdims=True)
        found = jnp.where(column == c, slot, found)
    landing[...] = found

    for copy in small:
        copy.wait()
    rows, pages = table.shape
    wide = whole.shape[1]
    base = lax.rem(member, groups) * rows
    columns = table[...].T
    page_id = lax.broadcasted_iota(jnp.int32, (pages, wide), 0)
    slot_id = lax.broadcasted_iota(jnp.int32, (pages, wide), 1)
    row_id = lax.broadcasted_iota(jnp.int32, (rows, 128), 0)
    over = jnp.zeros((rows, 128), jnp.int32)
    for r in range(rows):
        length = lengths[base + r]
        full = length // PAGE
        over = jnp.where(row_id == r, length - full * PAGE, over)
        hit = columns[:, r : r + 1] == slot_id
        in_whole = jnp.where(hit & (page_id < full), 1.0, 0.0)
        in_part = jnp.where(hit & (page_id == full), 1.0, 0.0)
        whole[r : r + 1, :] = jnp.sum(in_whole, axis=0, keepdims=True)
        part[r : r + 1, :] = jnp.sum(in_part, axis=0, keepdims=True)
    whole_b = whole[...].astype(jnp.bfloat16)
    part_b = part[...].astype(jnp.bfloat16)
    lane = lax.broadcasted_iota(jnp.int32, (rows, 128), 1)
    inside = (lane % PAGE) < over
    per_block = 128 // PAGE
    slot_in = lax.broadcasted_iota(jnp.int32, (wide, 128), 0)
    lane_in = lax.broadcasted_iota(jnp.int32, (wide, 128), 1) // PAGE
    for i in range(bias.shape[1] // 128):
        expand = jnp.where(slot_in == lane_in + i * per_block, 1.0, 0.0).astype(jnp.bfloat16)
        times = jnp.dot(whole_b, expand, preferred_element_type=jnp.float32)
        extra = jnp.dot(part_b, expand, preferred_element_type=jnp.float32)
        bias[:, i * 128 : (i + 1) * 128] = jnp.log(times + jnp.where(inside, extra, 0.0))

    for copy in copies:
        copy.wait()


def prepare(place, lengths, tables, listed, groups, weights, first):
    rows = tables.shape[0]
    members, slots = listed.shape
    wide = -(-slots // 128) * 128
    moved = sum(w.size * w.dtype.itemsize for w, _ in weights)
    pieces = [
        pltpu.VMEM((w.shape[0] // n, w.shape[1]), w.dtype) for w, n in weights for _ in range(n)
    ]
    weights = [w for w, _ in weights]
    count, parts = len(weights), len(pieces)
    return pl.pallas_call(
        functools.partial(prepare_kernel, count, parts, groups),
        out_shape=pieces
        + [
            jax.ShapeDtypeStruct((rows, slots * PAGE), jnp.float32),
            jax.ShapeDtypeStruct((members, 128), jnp.int32),
        ],
        in_specs=[SM, VM] + [HBM] * (2 + count + len(first)),
        out_specs=[VM] * (parts + 2),
        scratch_shapes=[
            pltpu.VMEM((members, wide), jnp.int32),
            pltpu.VMEM((rows, wide), jnp.float32),
            pltpu.VMEM((rows, wide), jnp.float32),
            pltpu.SMEM(lengths.shape, lengths.dtype),
            pltpu.VMEM(tables.shape, tables.dtype),
            pltpu.SemaphoreType.DMA((parts + 2,)),
        ],
        compiler_params=pltpu.CompilerParams(vmem_limit_bytes=6 * MIB),
        cost_estimate=pl.CostEstimate(flops=0, bytes_accessed=moved, transcendentals=0),
        name="prepare",
    )(place, listed, *[in_hbm(x) for x in (lengths, tables, *weights, *first)])


def attend_kernel(members, steps, chunks, place, landing, old_pool, weight, bias, new_k, new_v, *refs):
    asked, refs = refs[:steps], refs[steps:]
    arrived, refs = refs[:-7], refs[-7:]
    kv_out, att_low, att_high, held, pool, scores, sems = refs
    fetch = pltpu.make_async_copy(weight, held, sems.at[2])
    fetch.start()
    member, half = place[0], place[1]
    slots = pool.shape[0]
    resident = slots - ARRIVE
    per_peer = ARRIVE // members
    rows = bias.shape[0]
    count = rows * steps * GQ

    @pl.when(half == 0)
    def _():
        copy = pltpu.make_async_copy(old_pool, pool, sems.at[0])
        copy.start()
        att_low[...] = jnp.zeros_like(att_low)
        att_high[...] = jnp.zeros_like(att_high)
        copy.wait()
        copy_out = pltpu.make_async_copy(pool, kv_out, sems.at[1])
        copy_out.start()
        copy_out.wait()

    @pl.when(half == 1)
    def _():
        copy = pltpu.make_async_copy(
            old_pool.at[pl.ds(0, resident)], pool.at[pl.ds(0, resident)], sems.at[0]
        )
        copy.start()
        for i, first, k in chunks:
            source = lax.rem(member - k + members, members)

            @pl.loop(0, per_peer, unroll=math.gcd(per_peer, 8))
            def _(c):
                pool[resident + landing[source, c]] = arrived[i][first + c]

        copy.wait()
        copy_out = pltpu.make_async_copy(pool, kv_out, sems.at[1])
        copy_out.start()

        scale = 1.0 / math.sqrt(HD)
        q = jnp.concatenate(
            [ask[:, j * HD : (j + 1) * HD] for j in range(GQ) for ask in asked], axis=0
        )
        nt = (((1,), (1,)), ((), ()))
        group = 24
        width = group * PAGE
        lanes = 128
        fresh = lax.dot_general(q, new_k[...], nt, preferred_element_type=jnp.float32) * scale
        q_id = lax.broadcasted_iota(jnp.int32, fresh.shape, 0)
        t_id = lax.broadcasted_iota(jnp.int32, fresh.shape, 1)
        allowed = (q_id % rows == t_id // steps) & (t_id % steps <= (q_id // rows) % steps)
        fresh = jnp.where(allowed, fresh, -jnp.inf)
        peak = fresh
        for c in range(slots // group):
            keys = pool[c * group : (c + 1) * group, 0].reshape(width, HD)
            s = lax.dot_general(q, keys, nt, preferred_element_type=jnp.float32) * scale
            b = bias[:, c * width : (c + 1) * width]
            s = (s.reshape(count // rows, rows, width) + b[None]).reshape(count, width)
            scores[:, c * width : (c + 1) * width] = s
            for i in range(width // lanes):
                peak = jnp.maximum(peak, s[:, i * lanes : (i + 1) * lanes])
        top = jnp.max(peak, axis=1, keepdims=True)
        p = jnp.exp(fresh - top)
        total = p
        acc = jnp.dot(p.astype(jnp.bfloat16), new_v[...], preferred_element_type=jnp.float32)
        for c in range(slots // group):
            p = jnp.exp(scores[:, c * width : (c + 1) * width] - top)
            for i in range(width // lanes):
                total = total + p[:, i * lanes : (i + 1) * lanes]
            values = pool[c * group : (c + 1) * group, 1].reshape(width, HD)
            acc = acc + jnp.dot(p.astype(jnp.bfloat16), values, preferred_element_type=jnp.float32)
        out = (acc / jnp.sum(total, axis=1, keepdims=True)).astype(jnp.bfloat16)
        tokens = rows * steps
        for j in range(GQ // 2):
            att_low[:, j * HD : (j + 1) * HD] = out[j * tokens : (j + 1) * tokens]
            other = j + GQ // 2
            att_high[:, j * HD : (j + 1) * HD] = out[other * tokens : (other + 1) * tokens]
        copy_out.wait()

    fetch.wait()


def place_and_attend(place, landing, old_pool, weight, bias, new_k, new_v, asked, arrived, chunks):
    members = landing.shape[0]
    slots = old_pool.shape[0]
    rows = bias.shape[0]
    steps = len(asked)
    tokens = rows * steps
    return pl.pallas_call(
        functools.partial(attend_kernel, members, steps, chunks),
        out_shape=[
            jax.ShapeDtypeStruct(old_pool.shape, old_pool.dtype),
            jax.ShapeDtypeStruct((tokens, GQ * HD // 2), jnp.bfloat16),
            jax.ShapeDtypeStruct((tokens, GQ * HD // 2), jnp.bfloat16),
            pltpu.VMEM(weight.shape, weight.dtype),
        ],
        in_specs=[SM, SM, HBM, HBM, VM, VM, VM] + [VM] * (steps + len(arrived)),
        out_specs=[HBM, VM, VM, VM],
        scratch_shapes=[
            pltpu.VMEM(old_pool.shape, old_pool.dtype),
            pltpu.VMEM((tokens * GQ, slots * PAGE), jnp.float32),
            pltpu.SemaphoreType.DMA((3,)),
        ],
        compiler_params=pltpu.CompilerParams(vmem_limit_bytes=9 * MIB),
        name="place_attend",
    )(
        place,
        landing,
        in_hbm(old_pool),
        in_hbm(weight),
        bias,
        new_k,
        new_v,
        *asked,
        *arrived,
    )


def project_kernel(groups, place, weight, stream, mine, sibling, res_out):
    half = place[1]
    members, tokens, width = mine.shape
    sums = [stream[g * tokens : (g + 1) * tokens].astype(jnp.float32) for g in range(groups)]
    for h in range(KVH):
        for g in range(groups):
            m = h * groups + g
            first = jnp.where(half == 0, mine[m], sibling[m])
            second = jnp.where(half == 0, sibling[m], mine[m])
            sums[g] = sums[g] + lax.dot_general(
                jnp.concatenate([first, second], axis=1),
                weight[:, 2 * h * width : 2 * (h + 1) * width],
                (((1,), (1,)), ((), ())),
                preferred_element_type=jnp.float32,
            )
    for g in range(groups):
        res_out[g * tokens : (g + 1) * tokens] = sums[g].astype(res_out.dtype)


def project(place, weight, stream, mine, sibling, groups):
    return pl.pallas_call(
        functools.partial(project_kernel, groups),
        out_shape=jax.ShapeDtypeStruct(stream.shape, jnp.bfloat16),
        in_specs=[SM, VM, VM, VM, VM],
        out_specs=VM,
        compiler_params=pltpu.CompilerParams(vmem_limit_bytes=4 * MIB),
        name="out_projection",
    )(place, in_vmem(weight), stream, mine, sibling)


def ffn_kernel(place, mine, sibling, gain, gate, *refs):
    up = refs[:SPLIT]
    down, own_out, other_out, down_buf, normed, hidden, down_sem = refs[SPLIT:]
    half = place[1]
    members, tokens, width = mine.shape
    depth, hidden_count = up[0].shape
    features = depth * SPLIT
    down_copies = []
    for t in range(members):
        cols = pl.ds(t * 2 * width, 2 * width)
        down_copies.append(
            pltpu.make_async_copy(down.at[:, cols], down_buf.at[:, cols], down_sem.at[t])
        )
        down_copies[-1].start()

    square = jnp.zeros((tokens, width), jnp.float32)
    for block in (mine, sibling):
        for t in range(members):
            x = block[t].astype(jnp.float32)
            square = square + x * x
    factor = lax.rsqrt(jnp.sum(square, axis=1, keepdims=True) / features + 1e-05)
    for t in range(members):
        first = jnp.where(half == 0, mine[t], sibling[t])
        second = jnp.where(half == 0, sibling[t], mine[t])
        x = jnp.concatenate([first, second], axis=1).astype(jnp.float32)
        cols = slice(2 * t * width, 2 * (t + 1) * width)
        normed[:, cols] = (x * factor * gain[cols][None, :]).astype(jnp.bfloat16)
    tile = min(1024, hidden_count)
    for f in range(hidden_count // tile):
        cols = slice(f * tile, (f + 1) * tile)
        gate_act = jnp.dot(normed[...], gate[:, cols], preferred_element_type=jnp.float32)
        up_act = 0.0
        for i in range(SPLIT):
            x = normed[:, i * depth : (i + 1) * depth]
            up_act += jnp.dot(x, up[i][:, cols], preferred_element_type=jnp.float32)
        h = gate_act / (1.0 + jnp.exp(-gate_act)) * up_act
        hidden[:, cols] = h.astype(jnp.bfloat16)
    for t in range(members):
        down_copies[t].wait()
        part = jnp.dot(
            hidden[...],
            down_buf[:, 2 * t * width : 2 * (t + 1) * width],
            preferred_element_type=jnp.float32,
        )
        first, second = part[:, :width], part[:, width:]
        own_out[t] = jnp.where(half == 0, first, second)
        other_out[t] = jnp.where(half == 0, second, first).astype(jnp.bfloat16)


def feed_forward(place, mine, sibling, gain, gate, up, down):
    tokens = mine.shape[1]
    hidden_count, features = down.shape
    return pl.pallas_call(
        ffn_kernel,
        out_shape=[
            jax.ShapeDtypeStruct(mine.shape, jnp.float32),
            jax.ShapeDtypeStruct(mine.shape, jnp.bfloat16),
        ],
        in_specs=[SM, VM, VM, VM] + [VM] * (1 + SPLIT) + [HBM],
        out_specs=[VM, VM],
        scratch_shapes=[
            pltpu.VMEM(down.shape, down.dtype),
            pltpu.VMEM((tokens, features), jnp.bfloat16),
            pltpu.VMEM((tokens, hidden_count), jnp.bfloat16),
            pltpu.SemaphoreType.DMA((mine.shape[0],)),
        ],
        compiler_params=pltpu.CompilerParams(vmem_limit_bytes=19 * MIB),
        name="feed_forward",
    )(place, mine, sibling, gain, *map(in_vmem, (gate, *up)), in_hbm(down))


def local(
    kv_pages,
    page_list,
    block_tables,
    lengths,
    queries,
    fresh_kv,
    stream,
    out_proj,
    norm_gain,
    gate_weight,
    up_weight,
    down_weight,
):
    members = lax.axis_size("tp")
    member = lax.axis_index("tp")
    half = lax.axis_index("pd")
    place = jnp.stack([member, half]).astype(jnp.int32)
    slots = kv_pages.shape[0]
    per_peer = ARRIVE // members
    groups = members // KVH
    rows = block_tables.shape[0]
    steps = queries.shape[1]
    tokens = rows * steps

    def send(x, *hops):
        route = [
            (2 * t + start, 2 * ((t + k) % members) + end)
            for start, k, end in hops
            for t in range(members)
        ]
        return lax.ppermute(x, BOTH, route)

    def swap(x):
        return lax.ppermute(x, "pd", [(0, 1), (1, 0)])

    near, own_chunk, *far = pack(place, page_list, kv_pages)
    far = dict(zip(range(2, members - 1), far))
    crossed = lax.ppermute(near, "pd", [(0, 1)])
    behind, ahead = crossed[:per_peer], crossed[per_peer:]
    hosts = (2, members - 2)
    middle = sorted(set(far) - set(hosts), key=lambda k: abs(k - members // 2))
    arrived = {k: send(far[k], (0, k, 1)) for k in middle}
    for host, k, block in zip(hosts, (1, -1), (ahead, behind)):
        block = jnp.where(half == 0, far[host], block)
        arrived[host] = send(block, (0, host, 1), (1, k, 0))

    *held, bias, landing = prepare(
        place,
        lengths,
        block_tables,
        page_list.reshape(members, slots),
        groups,
        ((up_weight, SPLIT),),
        (near,),
    )

    arrived, landing = lax.optimization_barrier((arrived, landing))
    last = lax.ppermute(
        jnp.concatenate([own_chunk] + [arrived[host] for host in hosts]), "pd", [(0, 1)]
    )
    arrays = [last] + [arrived[k] for k in sorted(arrived)]
    chunks = [(0, 0, 0), (0, per_peer, 1), (0, 2 * per_peer, members - 1)]
    chunks += [(i + 1, 0, k) for i, k in enumerate(sorted(arrived))]
    padding = ((0, -tokens % 128), (0, 0))
    new_k = jnp.pad(fresh_kv[:, :, 0].reshape(tokens, HD), padding)
    new_v = jnp.pad(fresh_kv[:, :, 1].reshape(tokens, HD), padding)
    asked = [queries[:, st] for st in range(steps)]
    kv_after, att_low, att_high, out_proj = place_and_attend(
        place, landing, kv_pages, out_proj, bias, new_k, new_v, asked, arrays, chunks
    )

    def everywhere(x):
        spread = jnp.broadcast_to(x[None], (members, *x.shape))
        mine = lax.all_to_all(spread, "tp", split_axis=0, concat_axis=0)
        return mine, swap(mine)

    att_mine = att_high + lax.ppermute(att_low, "pd", [(1, 0)])
    here, there = everywhere(att_mine)

    inner = stream.reshape(steps, groups, rows, -1).transpose(1, 0, 2, 3).reshape(stream.shape)
    residual = project(place, out_proj, inner, here, there, groups)

    mine, sibling = everywhere(residual)
    own, other = feed_forward(
        place, mine, sibling, norm_gain, gate_weight, held, down_weight
    )
    summed = (own + swap(other).astype(jnp.float32)).astype(jnp.bfloat16)
    shares = lax.all_to_all(summed, "tp", split_axis=0, concat_axis=0)
    layer = residual.astype(jnp.float32) + jnp.sum(shares.astype(jnp.float32), axis=0)
    layer_out = (
        layer.astype(jnp.bfloat16)
        .reshape(groups, steps, rows, -1)
        .transpose(1, 0, 2, 3)
        .reshape(stream.shape)
    )
    return (kv_after, layer_out)


def solution(mesh):
    return jax.shard_map(
        local,
        mesh=mesh,
        in_specs=(
            P(("grp", "tp", "pd"), None, None, None),
            P("grp"),
            P(("grp", "tp"), None),
            P("grp"),
            P(("grp", "tp"), None, None),
            P(("grp", "tp"), None, None, None),
            P("grp", ("tp", "pd")),
            P(("tp", "pd"), None),
            P(),
            P(None, ("tp", "pd")),
            P(None, ("tp", "pd")),
            P(("tp", "pd"), None),
        ),
        out_specs=(P(("grp", "tp", "pd"), None, None, None), P("grp", ("tp", "pd"))),
        check_vma=False,
    )
```

```python
import functools
import math

import jax
import jax.numpy as jnp
from jax import lax
from jax.experimental import pallas as pl
from jax.experimental.pallas import tpu as pltpu
from jax.sharding import PartitionSpec as P

HD = 128
KVH = 8
GQ = 8
PAGE = 16
REQ_DEV = 2
NEWP = 128
ARRIVE = REQ_DEV * NEWP
MIB = 1024 * 1024
BOTH = ("tp", "pd")
SPLIT = 2

VM = pl.BlockSpec(memory_space=pltpu.VMEM)
SM = pl.BlockSpec(memory_space=pltpu.SMEM)
ANY = pl.BlockSpec(memory_space=pl.ANY)
HBM = pl.BlockSpec(memory_space=pltpu.HBM)


def in_vmem(x):
    return pltpu.with_memory_space_constraint(x, pltpu.VMEM)


def in_hbm(x):
    return pltpu.with_memory_space_constraint(x, pltpu.HBM)


def pack_kernel(members, place, pages, pool, *refs):
    count = members - 1
    outs = refs[:count]
    packed, held, own, counts, sems, load_sems = refs[count:]
    member, half = place[0], place[1]
    slots = pool.shape[0]
    per_peer = ARRIVE // members
    parts = 4
    step = slots // parts

    @pl.when(half == 0)
    def _():
        own_copy = pltpu.make_async_copy(pages, own, load_sems.at[parts])
        own_copy.start()
        loads = []
        for i in range(parts):
            window = pl.ds(i * step, step)
            loads.append(
                pltpu.make_async_copy(pool.at[window], held.at[window], load_sems.at[i])
            )
            loads[-1].start()
        own_copy.wait()
        start = member * slots

        if members in (4, 8):
            carry = (jnp.int32(0), jnp.int32(0))
            for i in range(parts):
                loads[i].wait()

                def body(j, words, base=i * step):
                    low, high = words
                    entry = own[start + base + j]
                    ahead = ((entry >> 8) - member + 1) & (members - 1)
                    leaves = entry >= 0
                    shift = (ahead & 3) * 8
                    is_low = ahead < 4
                    count = (jnp.where(is_low, low, high) >> shift) & 255
                    one = jnp.where(leaves, jnp.int32(1) << shift, 0)
                    packed[jnp.where(leaves, ahead * per_peer + count, ARRIVE)] = held[base + j]
                    return (
                        low + jnp.where(is_low, one, 0),
                        high + jnp.where(is_low, 0, one),
                    )

                carry = lax.fori_loop(0, step, body, carry, unroll=13)
        else:
            for i in range(parts):
                loads[i].wait()

            @pl.loop(0, members + 1)
            def _(i):
                counts[i] = 0

            @pl.loop(0, slots)
            def _(i):
                entry = own[start + i]
                ahead = lax.rem((entry >> 8) - member + members + 1, members)
                row = jnp.where(entry >= 0, ahead, members)
                count = counts[row]
                counts[row] = count + 1
                packed[jnp.where(entry >= 0, row * per_peer + count, ARRIVE)] = held[i]

        copies = []
        near, own_chunk, *far = outs
        moves = [(near, 0, 0), (near, per_peer, 2), (own_chunk, 0, 1)]
        moves += [(out, 0, 3 + i) for i, out in enumerate(far)]
        for i, (out, first, row) in enumerate(moves):
            copies.append(
                pltpu.make_async_copy(
                    packed.at[pl.ds(row * per_peer, per_peer)],
                    out.at[pl.ds(first, per_peer)],
                    sems.at[i],
                )
            )
            copies[-1].start()
        for copy in copies:
            copy.wait()


def pack(place, pages, pool):
    members = lax.axis_size("tp")
    per_peer = ARRIVE // members
    chunk = pool.shape[1:]
    return pl.pallas_call(
        functools.partial(pack_kernel, members),
        out_shape=[pltpu.HBM((2 * per_peer, *chunk), pool.dtype)]
        + [pltpu.HBM((per_peer, *chunk), pool.dtype)] * (members - 2),
        in_specs=[SM, HBM, HBM],
        out_specs=[HBM] * (members - 1),
        scratch_shapes=[
            pltpu.VMEM((ARRIVE + 1, *chunk), pool.dtype),
            pltpu.VMEM(pool.shape, pool.dtype),
            pltpu.SMEM(pages.shape, jnp.int32),
            pltpu.SMEM((members + 1,), jnp.int32),
            pltpu.SemaphoreType.DMA((members,)),
            pltpu.SemaphoreType.DMA((5,)),
        ],
        compiler_params=pltpu.CompilerParams(vmem_limit_bytes=8 * MIB),
        name="pack_pages",
    )(place, in_hbm(pages), in_hbm(pool))


def prepare_kernel(count, parts, groups, place, listed, lengths_hbm, table_hbm, *refs):
    sources = refs[:count]
    held = refs[len(refs) - 8 - parts : -8]
    bias, landing, entries, whole, part, lengths, table, sems = refs[-8:]
    small = [
        pltpu.make_async_copy(lengths_hbm, lengths, sems.at[parts]),
        pltpu.make_async_copy(table_hbm, table, sems.at[parts + 1]),
    ]
    for copy in small:
        copy.start()
    copies = []
    for source in sources:
        done = 0
        while done < source.shape[0]:
            part_out = held[len(copies)]
            window = pl.ds(done, part_out.shape[0])
            copies.append(
                pltpu.make_async_copy(source.at[window], part_out, sems.at[len(copies)])
            )
            copies[-1].start()
            done += part_out.shape[0]

    member = place[0]
    entries[...] = jnp.full(entries.shape, -1, jnp.int32)
    entries[:, : listed.shape[1]] = listed[...]
    entry = entries[...]
    members, lanes = entry.shape
    per_peer = ARRIVE // members
    wanted = (entry >= 0) & ((entry >> 8) == member)
    before = lax.broadcasted_iota(jnp.int32, (lanes, lanes), 0) < lax.broadcasted_iota(
        jnp.int32, (lanes, lanes), 1
    )
    rank = jnp.dot(
        jnp.where(wanted, 1.0, 0.0).astype(jnp.bfloat16),
        jnp.where(before, 1.0, 0.0).astype(jnp.bfloat16),
        preferred_element_type=jnp.float32,
    ).astype(jnp.int32)
    column = lax.broadcasted_iota(jnp.int32, landing.shape, 1)
    found = jnp.zeros(landing.shape, jnp.int32)
    distance = member - lax.broadcasted_iota(jnp.int32, entry.shape, 0)
    distance = jnp.where(distance < 0, distance + members, distance)
    is_near = (distance <= 1) | (distance == members - 1)
    slot_lane = lax.broadcasted_iota(jnp.int32, entry.shape, 1) - (listed.shape[1] - ARRIVE)
    near = jnp.zeros(entry.shape, jnp.float32)
    for c in range(per_peer):
        slot = jnp.sum(jnp.where(wanted & (rank == c), entry & 255, 0), axis=1, keepdims=True)
        found = jnp.where(column == c, slot, found)
        near = jnp.where(is_near & (slot == slot_lane), 1.0, near)
    landing[...] = found
    near = jnp.max(near, axis=0, keepdims=True)
    present = jnp.where(place[1] == 0, near, 1.0 - near)

    for copy in small:
        copy.wait()
    rows, pages = table.shape
    wide = whole.shape[1]
    base = lax.rem(member, groups) * rows
    columns = table[...].T
    page_id = lax.broadcasted_iota(jnp.int32, (pages, wide), 0)
    slot_id = lax.broadcasted_iota(jnp.int32, (pages, wide), 1)
    row_id = lax.broadcasted_iota(jnp.int32, (rows, 128), 0)
    over = jnp.zeros((rows, 128), jnp.int32)
    for r in range(rows):
        length = lengths[base + r]
        full = length // PAGE
        over = jnp.where(row_id == r, length - full * PAGE, over)
        hit = columns[:, r : r + 1] == slot_id
        in_whole = jnp.where(hit & (page_id < full), 1.0, 0.0)
        in_part = jnp.where(hit & (page_id == full), 1.0, 0.0)
        whole[r : r + 1, :] = jnp.sum(in_whole, axis=0, keepdims=True)
        part[r : r + 1, :] = jnp.sum(in_part, axis=0, keepdims=True)
    whole_b = (whole[...] * present).astype(jnp.bfloat16)
    part_b = (part[...] * present).astype(jnp.bfloat16)
    lane = lax.broadcasted_iota(jnp.int32, (rows, 128), 1)
    inside = (lane % PAGE) < over
    per_block = 128 // PAGE
    slot_in = lax.broadcasted_iota(jnp.int32, (wide, 128), 0)
    lane_in = lax.broadcasted_iota(jnp.int32, (wide, 128), 1) // PAGE
    for i in range(bias.shape[1] // 128):
        expand = jnp.where(slot_in == lane_in + i * per_block, 1.0, 0.0).astype(jnp.bfloat16)
        times = jnp.dot(whole_b, expand, preferred_element_type=jnp.float32)
        extra = jnp.dot(part_b, expand, preferred_element_type=jnp.float32)
        bias[:, i * 128 : (i + 1) * 128] = jnp.log(times + jnp.where(inside, extra, 0.0))

    for copy in copies:
        copy.wait()


def prepare(place, lengths, tables, listed, groups, weights, first):
    rows = tables.shape[0]
    members, slots = listed.shape
    wide = -(-slots // 128) * 128
    moved = sum(w.size * w.dtype.itemsize for w, _ in weights)
    pieces = [
        pltpu.VMEM((w.shape[0] // n, w.shape[1]), w.dtype) for w, n in weights for _ in range(n)
    ]
    weights = [w for w, _ in weights]
    count, parts = len(weights), len(pieces)
    return pl.pallas_call(
        functools.partial(prepare_kernel, count, parts, groups),
        out_shape=pieces
        + [
            jax.ShapeDtypeStruct((rows, slots * PAGE), jnp.float32),
            jax.ShapeDtypeStruct((members, 128), jnp.int32),
        ],
        in_specs=[SM, VM] + [HBM] * (2 + count + len(first)),
        out_specs=[VM] * (parts + 2),
        scratch_shapes=[
            pltpu.VMEM((members, wide), jnp.int32),
            pltpu.VMEM((rows, wide), jnp.float32),
            pltpu.VMEM((rows, wide), jnp.float32),
            pltpu.SMEM(lengths.shape, lengths.dtype),
            pltpu.VMEM(tables.shape, tables.dtype),
            pltpu.SemaphoreType.DMA((parts + 2,)),
        ],
        compiler_params=pltpu.CompilerParams(vmem_limit_bytes=16 * MIB),
        cost_estimate=pl.CostEstimate(flops=0, bytes_accessed=moved, transcendentals=0),
        name="prepare",
    )(place, listed, *[in_hbm(x) for x in (lengths, tables, *weights, *first)])


def attend_kernel(members, steps, chunks, place, landing, old_pool, bias, new_k, new_v, *refs):
    asked, refs = refs[:steps], refs[steps:]
    arrived, refs = refs[:-6], refs[-6:]
    kv_out, keep, give, pool, scores, sems = refs
    member, half = place[0], place[1]
    slots = pool.shape[0]
    resident = slots - ARRIVE
    per_peer = ARRIVE // members
    rows = bias.shape[0]
    count = rows * steps * GQ
    pool[resident:] = jnp.zeros((ARRIVE, *pool.shape[1:]), pool.dtype)

    def place_pages(which):
        for i, k in chunks[which]:
            source = lax.rem(member - k + members, members)

            @pl.loop(0, per_peer, unroll=math.gcd(per_peer, 8))
            def _(c):
                pool[resident + landing[source, c]] = arrived[i][c]

    @pl.when(half == 0)
    def _():
        pool[:resident] = jnp.zeros((resident, *pool.shape[1:]), pool.dtype)
        place_pages(0)

    @pl.when(half == 1)
    def _():
        copy = pltpu.make_async_copy(
            old_pool.at[pl.ds(0, resident)], pool.at[pl.ds(0, resident)], sems.at[0]
        )
        copy.start()
        place_pages(1)
        copy.wait()
        pltpu.make_async_copy(pool, kv_out, sems.at[1]).start()

    scale = 1.0 / math.sqrt(HD)
    q = jnp.concatenate(
        [ask[:, j * HD : (j + 1) * HD] for j in range(GQ) for ask in asked], axis=0
    )
    nt = (((1,), (1,)), ((), ()))
    group = 24
    width = group * PAGE
    lanes = 128
    fresh = lax.dot_general(q, new_k[...], nt, preferred_element_type=jnp.float32) * scale
    q_id = lax.broadcasted_iota(jnp.int32, fresh.shape, 0)
    t_id = lax.broadcasted_iota(jnp.int32, fresh.shape, 1)
    allowed = (q_id % rows == t_id // steps) & (t_id % steps <= (q_id // rows) % steps)
    fresh = jnp.where(allowed & (half == 1), fresh, -jnp.inf)
    peak = fresh
    for c in range(slots // group):
        keys = pool[c * group : (c + 1) * group, 0].reshape(width, HD)
        s = lax.dot_general(q, keys, nt, preferred_element_type=jnp.float32) * scale
        b = bias[:, c * width : (c + 1) * width]
        s = (s.reshape(count // rows, rows, width) + b[None]).reshape(count, width)
        scores[:, c * width : (c + 1) * width] = s
        for i in range(width // lanes):
            peak = jnp.maximum(peak, s[:, i * lanes : (i + 1) * lanes])
    top = jnp.maximum(jnp.max(peak, axis=1, keepdims=True), -1e30)
    p = jnp.exp(fresh - top)
    total = p
    acc = jnp.dot(p.astype(jnp.bfloat16), new_v[...], preferred_element_type=jnp.float32)
    for c in range(slots // group):
        p = jnp.exp(scores[:, c * width : (c + 1) * width] - top)
        for i in range(width // lanes):
            total = total + p[:, i * lanes : (i + 1) * lanes]
        values = pool[c * group : (c + 1) * group, 1].reshape(width, HD)
        acc = acc + jnp.dot(p.astype(jnp.bfloat16), values, preferred_element_type=jnp.float32)
    total = jnp.sum(total, axis=1, keepdims=True)
    middle = count // 2
    for out, first in ((keep, half == 0), (give, half == 1)):
        out[:, :HD] = jnp.where(first, acc[:middle], acc[middle:])
        out[:, HD : 2 * HD] = jnp.broadcast_to(
            jnp.where(first, top[:middle], top[middle:]), (middle, HD)
        )
        out[:, 2 * HD :] = jnp.broadcast_to(
            jnp.where(first, total[:middle], total[middle:]), (middle, HD)
        )

    @pl.when(half == 1)
    def _():
        pltpu.make_async_copy(pool, kv_out, sems.at[1]).wait()


def place_and_attend(place, landing, old_pool, bias, new_k, new_v, asked, arrived, chunks):
    members = landing.shape[0]
    slots = old_pool.shape[0]
    steps = len(asked)
    count = bias.shape[0] * steps * GQ
    part = jax.ShapeDtypeStruct((count // 2, 3 * HD), jnp.float32)
    return pl.pallas_call(
        functools.partial(attend_kernel, members, steps, chunks),
        out_shape=[jax.ShapeDtypeStruct(old_pool.shape, old_pool.dtype), part, part],
        in_specs=[SM, SM, HBM, VM, VM, VM] + [VM] * (steps + len(arrived)),
        out_specs=[HBM, VM, VM],
        scratch_shapes=[
            pltpu.VMEM(old_pool.shape, old_pool.dtype),
            pltpu.VMEM((count, slots * PAGE), jnp.float32),
            pltpu.SemaphoreType.DMA((2,)),
        ],
        compiler_params=pltpu.CompilerParams(vmem_limit_bytes=9 * MIB),
        name="place_attend",
    )(place, landing, in_hbm(old_pool), bias, new_k, new_v, *asked, *arrived)


def combine_kernel(mine, other, out):
    tokens = out.shape[0]
    for j in range(out.shape[1] // HD):
        rows = slice(j * tokens, (j + 1) * tokens)
        a, b = mine[rows, :], other[rows, :]
        top_a, top_b = a[:, HD : 2 * HD], b[:, HD : 2 * HD]
        top = jnp.maximum(top_a, top_b)
        scale_a, scale_b = jnp.exp(top_a - top), jnp.exp(top_b - top)
        total = a[:, 2 * HD :] * scale_a + b[:, 2 * HD :] * scale_b
        value = (a[:, :HD] * scale_a + b[:, :HD] * scale_b) / total
        out[:, j * HD : (j + 1) * HD] = value.astype(out.dtype)


def combine(mine, other, tokens):
    return pl.pallas_call(
        combine_kernel,
        out_shape=jax.ShapeDtypeStruct((tokens, GQ // 2 * HD), jnp.bfloat16),
        in_specs=[VM, VM],
        out_specs=VM,
        compiler_params=pltpu.CompilerParams(vmem_limit_bytes=2 * MIB),
        name="combine",
    )(mine, other)


def project_kernel(groups, place, weight, stream, mine, sibling, old_pool, _, *refs):
    res_out, kv_out, pool, sems = refs
    half = place[1]

    @pl.when(half == 0)
    def _():
        pltpu.make_async_copy(old_pool, pool, sems.at[0]).start()

    members, tokens, width = mine.shape
    sums = [stream[g * tokens : (g + 1) * tokens].astype(jnp.float32) for g in range(groups)]
    for h in range(KVH):
        if h == KVH // 2:

            @pl.when(half == 0)
            def _():
                pltpu.make_async_copy(old_pool, pool, sems.at[0]).wait()
                pltpu.make_async_copy(pool, kv_out, sems.at[1]).start()

        for g in range(groups):
            m = h * groups + g
            first = jnp.where(half == 0, mine[m], sibling[m])
            second = jnp.where(half == 0, sibling[m], mine[m])
            sums[g] = sums[g] + lax.dot_general(
                jnp.concatenate([first, second], axis=1),
                weight[:, 2 * h * width : 2 * (h + 1) * width],
                (((1,), (1,)), ((), ())),
                preferred_element_type=jnp.float32,
            )
    for g in range(groups):
        res_out[g * tokens : (g + 1) * tokens] = sums[g].astype(res_out.dtype)

    @pl.when(half == 0)
    def _():
        pltpu.make_async_copy(pool, kv_out, sems.at[1]).wait()


def project(place, weight, stream, mine, sibling, old_pool, kv, groups):
    return pl.pallas_call(
        functools.partial(project_kernel, groups),
        out_shape=[
            jax.ShapeDtypeStruct(stream.shape, jnp.bfloat16),
            jax.ShapeDtypeStruct(kv.shape, kv.dtype),
        ],
        in_specs=[SM, VM, VM, VM, VM, HBM, HBM],
        out_specs=[VM, HBM],
        scratch_shapes=[
            pltpu.VMEM(kv.shape, kv.dtype),
            pltpu.SemaphoreType.DMA((2,)),
        ],
        input_output_aliases={6: 1},
        compiler_params=pltpu.CompilerParams(vmem_limit_bytes=6 * MIB),
        name="out_projection",
    )(place, in_vmem(weight), stream, mine, sibling, in_hbm(old_pool), in_hbm(kv))


def ffn_kernel(place, landing, mine, sibling, gain, *refs):
    gate, up, refs = refs[:SPLIT], refs[SPLIT : 2 * SPLIT], refs[2 * SPLIT :]
    down, late, _, own_out, other_out, kv_out = refs[:6]
    down_buf, normed, hidden, down_sem, late_sem = refs[6:]
    member, half = place[0], place[1]
    members, tokens, width = mine.shape
    per_peer = ARRIVE // members
    resident = kv_out.shape[0] - ARRIVE

    def late_copy(i, k, c):
        source = lax.rem(member - k + members, members)
        spot = i * per_peer + c
        return pltpu.make_async_copy(
            late.at[spot], kv_out.at[resident + landing[source, c]], late_sem.at[spot]
        )

    late_chunks = [(0, 0), (1, 1), (2, members - 1)]

    @pl.when(half == 1)
    def _():
        for i, k in late_chunks:

            @pl.loop(0, per_peer)
            def _(c):
                late_copy(i, k, c).start()

    depth, hidden_count = up[0].shape
    features = depth * SPLIT
    down_copies = []
    for t in range(members):
        cols = pl.ds(t * 2 * width, 2 * width)
        down_copies.append(
            pltpu.make_async_copy(down.at[:, cols], down_buf.at[:, cols], down_sem.at[t])
        )
        down_copies[-1].start()

    square = jnp.zeros((tokens, width), jnp.float32)
    for block in (mine, sibling):
        for t in range(members):
            x = block[t].astype(jnp.float32)
            square = square + x * x
    factor = lax.rsqrt(jnp.sum(square, axis=1, keepdims=True) / features + 1e-05)
    for t in range(members):
        first = jnp.where(half == 0, mine[t], sibling[t])
        second = jnp.where(half == 0, sibling[t], mine[t])
        x = jnp.concatenate([first, second], axis=1).astype(jnp.float32)
        cols = slice(2 * t * width, 2 * (t + 1) * width)
        normed[:, cols] = (x * factor * gain[cols][None, :]).astype(jnp.bfloat16)
    tile = min(1024, hidden_count)
    for f in range(hidden_count // tile):
        cols = slice(f * tile, (f + 1) * tile)
        gate_act = up_act = 0.0
        for i in range(SPLIT):
            x = normed[:, i * depth : (i + 1) * depth]
            gate_act += jnp.dot(x, gate[i][:, cols], preferred_element_type=jnp.float32)
            up_act += jnp.dot(x, up[i][:, cols], preferred_element_type=jnp.float32)
        h = gate_act / (1.0 + jnp.exp(-gate_act)) * up_act
        hidden[:, cols] = h.astype(jnp.bfloat16)
    for t in range(members):
        down_copies[t].wait()
        part = jnp.dot(
            hidden[...],
            down_buf[:, 2 * t * width : 2 * (t + 1) * width],
            preferred_element_type=jnp.float32,
        )
        first, second = part[:, :width], part[:, width:]
        own_out[t] = jnp.where(half == 0, first, second)
        other_out[t] = jnp.where(half == 0, second, first).astype(jnp.bfloat16)

    @pl.when(half == 1)
    def _():
        for i, k in late_chunks:

            @pl.loop(0, per_peer)
            def _(c):
                late_copy(i, k, c).wait()


def feed_forward(place, landing, mine, sibling, gain, gate, up, down, late, kv):
    tokens = mine.shape[1]
    hidden_count, features = down.shape
    return pl.pallas_call(
        ffn_kernel,
        out_shape=[
            jax.ShapeDtypeStruct(mine.shape, jnp.float32),
            jax.ShapeDtypeStruct(mine.shape, jnp.bfloat16),
            jax.ShapeDtypeStruct(kv.shape, kv.dtype),
        ],
        in_specs=[SM, SM, VM, VM, VM] + [VM] * (2 * SPLIT) + [HBM] * 3,
        out_specs=[VM, VM, HBM],
        input_output_aliases={5 + 2 * SPLIT + 2: 2},
        scratch_shapes=[
            pltpu.VMEM(down.shape, down.dtype),
            pltpu.VMEM((tokens, features), jnp.bfloat16),
            pltpu.VMEM((tokens, hidden_count), jnp.bfloat16),
            pltpu.SemaphoreType.DMA((mine.shape[0],)),
            pltpu.SemaphoreType.DMA((late.shape[0],)),
        ],
        compiler_params=pltpu.CompilerParams(vmem_limit_bytes=19 * MIB),
        name="feed_forward",
    )(
        place,
        landing,
        mine,
        sibling,
        gain,
        *map(in_vmem, (*gate, *up)),
        *map(in_hbm, (down, late, kv)),
    )


def local(
    kv_pages,
    page_list,
    block_tables,
    lengths,
    queries,
    fresh_kv,
    stream,
    out_proj,
    norm_gain,
    gate_weight,
    up_weight,
    down_weight,
):
    members = lax.axis_size("tp")
    member = lax.axis_index("tp")
    half = lax.axis_index("pd")
    place = jnp.stack([member, half]).astype(jnp.int32)
    slots = kv_pages.shape[0]
    per_peer = ARRIVE // members
    groups = members // KVH
    rows = block_tables.shape[0]
    steps = queries.shape[1]
    tokens = rows * steps

    def send(x, *hops):
        route = [
            (2 * t + start, 2 * ((t + k) % members) + end)
            for start, k, end in hops
            for t in range(members)
        ]
        return lax.ppermute(x, BOTH, route)

    def swap(x):
        return lax.ppermute(x, "pd", [(0, 1), (1, 0)])

    near, own_chunk, *far = pack(place, page_list, kv_pages)
    far = dict(zip(range(2, members - 1), far))
    crossed = lax.ppermute(near, "pd", [(0, 1)])
    behind, ahead = crossed[:per_peer], crossed[per_peer:]
    hosts = (2, members - 2)
    middle = sorted(set(far) - set(hosts), key=lambda k: abs(k - members // 2))
    arrived = {k: send(far[k], (0, k, 1)) for k in middle}
    for host, k, block in zip(hosts, (1, -1), (ahead, behind)):
        block = jnp.where(half == 0, far[host], block)
        arrived[host] = send(block, (0, host, 1), (1, k, 0))

    *held, bias, landing = prepare(
        place,
        lengths,
        block_tables,
        page_list.reshape(members, slots),
        groups,
        ((out_proj, 1), (gate_weight, SPLIT), (up_weight, SPLIT)),
        (near,),
    )

    late = lax.ppermute(
        jnp.concatenate([own_chunk] + [arrived[host] for host in hosts]), "pd", [(0, 1)]
    )
    order = sorted(arrived)
    arrays = [own_chunk] + [arrived[k] for k in order]
    chunks = (
        [(0, 0)] + [(1 + order.index(host), k % members) for host, k in zip(hosts, (1, -1))],
        [(1 + i, k) for i, k in enumerate(order)],
    )
    padding = ((0, -tokens % 128), (0, 0))
    new_k = jnp.pad(fresh_kv[:, :, 0].reshape(tokens, HD), padding)
    new_v = jnp.pad(fresh_kv[:, :, 1].reshape(tokens, HD), padding)
    asked = [queries[:, st] for st in range(steps)]
    kv_part, keep, give = place_and_attend(
        place, landing, kv_pages, bias, new_k, new_v, asked, arrays, chunks
    )

    def everywhere(x):
        spread = jnp.broadcast_to(x[None], (members, *x.shape))
        mine = lax.all_to_all(spread, "tp", split_axis=0, concat_axis=0)
        return mine, swap(mine)

    att_mine = combine(keep, swap(give), tokens)
    here, there = everywhere(att_mine)

    inner = stream.reshape(steps, groups, rows, -1).transpose(1, 0, 2, 3).reshape(stream.shape)
    residual, kv_part = project(
        place, held[0], inner, here, there, kv_pages, kv_part, groups
    )

    mine, sibling = everywhere(residual)
    own, other, kv_after = feed_forward(
        place, landing, mine, sibling, norm_gain, held[1 : 1 + SPLIT], held[1 + SPLIT :], down_weight, late, kv_part
    )
    summed = (own + swap(other).astype(jnp.float32)).astype(jnp.bfloat16)
    shares = lax.all_to_all(summed, "tp", split_axis=0, concat_axis=0)
    layer = residual.astype(jnp.float32) + jnp.sum(shares.astype(jnp.float32), axis=0)
    layer_out = (
        layer.astype(jnp.bfloat16)
        .reshape(groups, steps, rows, -1)
        .transpose(1, 0, 2, 3)
        .reshape(stream.shape)
    )
    return (kv_after, layer_out)


def solution(mesh):
    return jax.shard_map(
        local,
        mesh=mesh,
        in_specs=(
            P(("grp", "tp", "pd"), None, None, None),
            P("grp"),
            P(("grp", "tp"), None),
            P("grp"),
            P(("grp", "tp"), None, None),
            P(("grp", "tp"), None, None, None),
            P("grp", ("tp", "pd")),
            P(("tp", "pd"), None),
            P(),
            P(None, ("tp", "pd")),
            P(None, ("tp", "pd")),
            P(("tp", "pd"), None),
        ),
        out_specs=(P(("grp", "tp", "pd"), None, None, None), P("grp", ("tp", "pd"))),
        check_vma=False,
    )
```

```python
import functools
import math

import jax
import jax.numpy as jnp
from jax import lax
from jax.experimental import pallas as pl
from jax.experimental.pallas import tpu as pltpu
from jax.sharding import PartitionSpec as P

HD = 128
KVH = 8
GQ = 8
PAGE = 16
REQ_DEV = 2
NEWP = 128
ARRIVE = REQ_DEV * NEWP
MIB = 1024 * 1024
BOTH = ("tp", "pd")
SPLIT = 4

VM = pl.BlockSpec(memory_space=pltpu.VMEM)
SM = pl.BlockSpec(memory_space=pltpu.SMEM)
ANY = pl.BlockSpec(memory_space=pl.ANY)
HBM = pl.BlockSpec(memory_space=pltpu.HBM)


def in_vmem(x):
    return pltpu.with_memory_space_constraint(x, pltpu.VMEM)


def in_hbm(x):
    return pltpu.with_memory_space_constraint(x, pltpu.HBM)


def pack_kernel(members, place, pages, pool, *refs):
    count = members - 1
    outs = refs[:count]
    packed, held, own, counts, sems, load_sems = refs[count:]
    member, half = place[0], place[1]
    slots = pool.shape[0]
    per_peer = ARRIVE // members
    parts = 4
    step = slots // parts

    @pl.when(half == 0)
    def _():
        own_copy = pltpu.make_async_copy(pages, own, load_sems.at[parts])
        own_copy.start()
        loads = []
        for i in range(parts):
            window = pl.ds(i * step, step)
            loads.append(
                pltpu.make_async_copy(pool.at[window], held.at[window], load_sems.at[i])
            )
            loads[-1].start()
        own_copy.wait()
        start = member * slots

        if members in (4, 8):
            carry = (jnp.int32(0), jnp.int32(0))
            for i in range(parts):
                loads[i].wait()

                def body(j, words, base=i * step):
                    low, high = words
                    entry = own[start + base + j]
                    ahead = ((entry >> 8) - member + 1) & (members - 1)
                    leaves = entry >= 0
                    shift = (ahead & 3) * 8
                    is_low = ahead < 4
                    count = (jnp.where(is_low, low, high) >> shift) & 255
                    one = jnp.where(leaves, jnp.int32(1) << shift, 0)
                    packed[jnp.where(leaves, ahead * per_peer + count, ARRIVE)] = held[base + j]
                    return (
                        low + jnp.where(is_low, one, 0),
                        high + jnp.where(is_low, 0, one),
                    )

                carry = lax.fori_loop(0, step, body, carry, unroll=13)
        else:
            for i in range(parts):
                loads[i].wait()

            @pl.loop(0, members + 1)
            def _(i):
                counts[i] = 0

            @pl.loop(0, slots)
            def _(i):
                entry = own[start + i]
                ahead = lax.rem((entry >> 8) - member + members + 1, members)
                row = jnp.where(entry >= 0, ahead, members)
                count = counts[row]
                counts[row] = count + 1
                packed[jnp.where(entry >= 0, row * per_peer + count, ARRIVE)] = held[i]

        copies = []
        near, own_chunk, *far = outs
        moves = [(near, 0, 0), (near, per_peer, 2), (own_chunk, 0, 1)]
        moves += [(out, 0, 3 + i) for i, out in enumerate(far)]
        for i, (out, first, row) in enumerate(moves):
            copies.append(
                pltpu.make_async_copy(
                    packed.at[pl.ds(row * per_peer, per_peer)],
                    out.at[pl.ds(first, per_peer)],
                    sems.at[i],
                )
            )
            copies[-1].start()
        for copy in copies:
            copy.wait()


def pack(place, pages, pool):
    members = lax.axis_size("tp")
    per_peer = ARRIVE // members
    chunk = pool.shape[1:]
    return pl.pallas_call(
        functools.partial(pack_kernel, members),
        out_shape=[pltpu.HBM((2 * per_peer, *chunk), pool.dtype)]
        + [pltpu.HBM((per_peer, *chunk), pool.dtype)] * (members - 2),
        in_specs=[SM, HBM, HBM],
        out_specs=[HBM] * (members - 1),
        scratch_shapes=[
            pltpu.VMEM((ARRIVE + 1, *chunk), pool.dtype),
            pltpu.VMEM(pool.shape, pool.dtype),
            pltpu.SMEM(pages.shape, jnp.int32),
            pltpu.SMEM((members + 1,), jnp.int32),
            pltpu.SemaphoreType.DMA((members,)),
            pltpu.SemaphoreType.DMA((5,)),
        ],
        compiler_params=pltpu.CompilerParams(vmem_limit_bytes=8 * MIB),
        name="pack_pages",
    )(place, in_hbm(pages), in_hbm(pool))


def prepare_kernel(count, parts, groups, place, listed, lengths_hbm, table_hbm, *refs):
    sources = refs[:count]
    held = refs[len(refs) - 8 - parts : -8]
    bias, landing, entries, whole, part, lengths, table, sems = refs[-8:]
    small = [
        pltpu.make_async_copy(lengths_hbm, lengths, sems.at[parts]),
        pltpu.make_async_copy(table_hbm, table, sems.at[parts + 1]),
    ]
    for copy in small:
        copy.start()
    copies = []
    for source in sources:
        done = 0
        while done < source.shape[0]:
            part_out = held[len(copies)]
            window = pl.ds(done, part_out.shape[0])
            copies.append(
                pltpu.make_async_copy(source.at[window], part_out, sems.at[len(copies)])
            )
            copies[-1].start()
            done += part_out.shape[0]

    member = place[0]
    entries[...] = jnp.full(entries.shape, -1, jnp.int32)
    entries[:, : listed.shape[1]] = listed[...]
    entry = entries[...]
    members, lanes = entry.shape
    per_peer = ARRIVE // members
    wanted = (entry >= 0) & ((entry >> 8) == member)
    before = lax.broadcasted_iota(jnp.int32, (lanes, lanes), 0) < lax.broadcasted_iota(
        jnp.int32, (lanes, lanes), 1
    )
    rank = jnp.dot(
        jnp.where(wanted, 1.0, 0.0).astype(jnp.bfloat16),
        jnp.where(before, 1.0, 0.0).astype(jnp.bfloat16),
        preferred_element_type=jnp.float32,
    ).astype(jnp.int32)
    column = lax.broadcasted_iota(jnp.int32, landing.shape, 1)
    found = jnp.zeros(landing.shape, jnp.int32)
    distance = member - lax.broadcasted_iota(jnp.int32, entry.shape, 0)
    distance = jnp.where(distance < 0, distance + members, distance)
    is_near = (distance <= 1) | (distance == members - 1)
    slot_lane = lax.broadcasted_iota(jnp.int32, entry.shape, 1) - (listed.shape[1] - ARRIVE)
    near = jnp.zeros(entry.shape, jnp.float32)
    for c in range(per_peer):
        slot = jnp.sum(jnp.where(wanted & (rank == c), entry & 255, 0), axis=1, keepdims=True)
        found = jnp.where(column == c, slot, found)
        near = jnp.where(is_near & (slot == slot_lane), 1.0, near)
    landing[...] = found
    near = jnp.max(near, axis=0, keepdims=True)
    present = jnp.where(place[1] == 0, near, 1.0 - near)

    for copy in small:
        copy.wait()
    rows, pages = table.shape
    wide = whole.shape[1]
    base = lax.rem(member, groups) * rows
    columns = table[...].T
    page_id = lax.broadcasted_iota(jnp.int32, (pages, wide), 0)
    slot_id = lax.broadcasted_iota(jnp.int32, (pages, wide), 1)
    row_id = lax.broadcasted_iota(jnp.int32, (rows, 128), 0)
    over = jnp.zeros((rows, 128), jnp.int32)
    for r in range(rows):
        length = lengths[base + r]
        full = length // PAGE
        over = jnp.where(row_id == r, length - full * PAGE, over)
        hit = columns[:, r : r + 1] == slot_id
        in_whole = jnp.where(hit & (page_id < full), 1.0, 0.0)
        in_part = jnp.where(hit & (page_id == full), 1.0, 0.0)
        whole[r : r + 1, :] = jnp.sum(in_whole, axis=0, keepdims=True)
        part[r : r + 1, :] = jnp.sum(in_part, axis=0, keepdims=True)
    whole_b = (whole[...] * present).astype(jnp.bfloat16)
    part_b = (part[...] * present).astype(jnp.bfloat16)
    lane = lax.broadcasted_iota(jnp.int32, (rows, 128), 1)
    inside = (lane % PAGE) < over
    per_block = 128 // PAGE
    slot_in = lax.broadcasted_iota(jnp.int32, (wide, 128), 0)
    lane_in = lax.broadcasted_iota(jnp.int32, (wide, 128), 1) // PAGE
    for i in range(bias.shape[1] // 128):
        expand = jnp.where(slot_in == lane_in + i * per_block, 1.0, 0.0).astype(jnp.bfloat16)
        times = jnp.dot(whole_b, expand, preferred_element_type=jnp.float32)
        extra = jnp.dot(part_b, expand, preferred_element_type=jnp.float32)
        bias[:, i * 128 : (i + 1) * 128] = jnp.log(times + jnp.where(inside, extra, 0.0))

    for copy in copies:
        copy.wait()


def prepare(place, lengths, tables, listed, groups, weights, first):
    rows = tables.shape[0]
    members, slots = listed.shape
    wide = -(-slots // 128) * 128
    moved = sum(w.size * w.dtype.itemsize for w, _ in weights)
    pieces = [
        pltpu.VMEM((w.shape[0] // n, w.shape[1]), w.dtype) for w, n in weights for _ in range(n)
    ]
    weights = [w for w, _ in weights]
    count, parts = len(weights), len(pieces)
    return pl.pallas_call(
        functools.partial(prepare_kernel, count, parts, groups),
        out_shape=pieces
        + [
            jax.ShapeDtypeStruct((rows, slots * PAGE), jnp.float32),
            jax.ShapeDtypeStruct((members, 128), jnp.int32),
        ],
        in_specs=[SM, VM] + [HBM] * (2 + count + len(first)),
        out_specs=[VM] * (parts + 2),
        scratch_shapes=[
            pltpu.VMEM((members, wide), jnp.int32),
            pltpu.VMEM((rows, wide), jnp.float32),
            pltpu.VMEM((rows, wide), jnp.float32),
            pltpu.SMEM(lengths.shape, lengths.dtype),
            pltpu.VMEM(tables.shape, tables.dtype),
            pltpu.SemaphoreType.DMA((parts + 2,)),
        ],
        compiler_params=pltpu.CompilerParams(vmem_limit_bytes=14 * MIB),
        cost_estimate=pl.CostEstimate(flops=0, bytes_accessed=moved, transcendentals=0),
        name="prepare",
    )(place, listed, *[in_hbm(x) for x in (lengths, tables, *weights, *first)])


def attend_kernel(members, steps, chunks, place, landing, old_pool, bias, new_k, new_v, *refs):
    asked, refs = refs[:steps], refs[steps:]
    arrived, refs = refs[:-7], refs[-7:]
    kv_out, keep, give, late, pool, scores, sems = refs
    member, half = place[0], place[1]
    slots = pool.shape[0]
    resident = slots - ARRIVE
    per_peer = ARRIVE // members
    rows = bias.shape[0]
    count = rows * steps * GQ
    pool[resident:] = jnp.zeros((ARRIVE, *pool.shape[1:]), pool.dtype)

    def place_pages(which):
        for i, k in chunks[which]:
            source = lax.rem(member - k + members, members)

            @pl.loop(0, per_peer, unroll=math.gcd(per_peer, 8))
            def _(c):
                pool[resident + landing[source, c]] = arrived[i][c]

    late_copies = [
        pltpu.make_async_copy(
            arrived[i], late.at[pl.ds(n * per_peer, per_peer)], sems.at[2 + n]
        )
        for n, (i, _) in enumerate(chunks[0])
    ]

    @pl.when(half == 0)
    def _():
        for copy in late_copies:
            copy.start()
        pool[:resident] = jnp.zeros((resident, *pool.shape[1:]), pool.dtype)
        place_pages(0)

    @pl.when(half == 1)
    def _():
        copy = pltpu.make_async_copy(
            old_pool.at[pl.ds(0, resident)], pool.at[pl.ds(0, resident)], sems.at[0]
        )
        copy.start()
        place_pages(1)
        copy.wait()
        pltpu.make_async_copy(pool, kv_out, sems.at[1]).start()

    scale = 1.0 / math.sqrt(HD)
    q = jnp.concatenate(
        [ask[:, j * HD : (j + 1) * HD] for j in range(GQ) for ask in asked], axis=0
    )
    nt = (((1,), (1,)), ((), ()))
    group = 24
    width = group * PAGE
    lanes = 128
    fresh = lax.dot_general(q, new_k[...], nt, preferred_element_type=jnp.float32) * scale
    q_id = lax.broadcasted_iota(jnp.int32, fresh.shape, 0)
    t_id = lax.broadcasted_iota(jnp.int32, fresh.shape, 1)
    allowed = (q_id % rows == t_id // steps) & (t_id % steps <= (q_id // rows) % steps)
    fresh = jnp.where(allowed & (half == 1), fresh, -jnp.inf)
    peak = fresh
    for c in range(slots // group):
        keys = pool[c * group : (c + 1) * group, 0].reshape(width, HD)
        s = lax.dot_general(q, keys, nt, preferred_element_type=jnp.float32) * scale
        b = bias[:, c * width : (c + 1) * width]
        s = (s.reshape(count // rows, rows, width) + b[None]).reshape(count, width)
        scores[:, c * width : (c + 1) * width] = s
        for i in range(width // lanes):
            peak = jnp.maximum(peak, s[:, i * lanes : (i + 1) * lanes])
    top = jnp.maximum(jnp.max(peak, axis=1, keepdims=True), -1e30)
    p = jnp.exp(fresh - top)
    total = p
    acc = jnp.dot(p.astype(jnp.bfloat16), new_v[...], preferred_element_type=jnp.float32)
    for c in range(slots // group):
        p = jnp.exp(scores[:, c * width : (c + 1) * width] - top)
        for i in range(width // lanes):
            total = total + p[:, i * lanes : (i + 1) * lanes]
        values = pool[c * group : (c + 1) * group, 1].reshape(width, HD)
        acc = acc + jnp.dot(p.astype(jnp.bfloat16), values, preferred_element_type=jnp.float32)
    total = jnp.sum(total, axis=1, keepdims=True)
    middle = count // 2
    for out, first in ((keep, half == 0), (give, half == 1)):
        out[:, :HD] = jnp.where(first, acc[:middle], acc[middle:])
        out[:, HD : 2 * HD] = jnp.broadcast_to(
            jnp.where(first, top[:middle], top[middle:]), (middle, HD)
        )
        out[:, 2 * HD :] = jnp.broadcast_to(
            jnp.where(first, total[:middle], total[middle:]), (middle, HD)
        )

    @pl.when(half == 1)
    def _():
        pltpu.make_async_copy(pool, kv_out, sems.at[1]).wait()

    @pl.when(half == 0)
    def _():
        for copy in late_copies:
            copy.wait()


def place_and_attend(place, landing, old_pool, bias, new_k, new_v, asked, arrived, chunks):
    members = landing.shape[0]
    slots = old_pool.shape[0]
    steps = len(asked)
    count = bias.shape[0] * steps * GQ
    part = jax.ShapeDtypeStruct((count // 2, 3 * HD), jnp.float32)
    return pl.pallas_call(
        functools.partial(attend_kernel, members, steps, chunks),
        out_shape=[
            jax.ShapeDtypeStruct(old_pool.shape, old_pool.dtype),
            part,
            part,
            jax.ShapeDtypeStruct((3 * ARRIVE // members, *old_pool.shape[1:]), old_pool.dtype),
        ],
        in_specs=[SM, SM, HBM, VM, VM, VM] + [VM] * (steps + len(arrived)),
        out_specs=[HBM, VM, VM, HBM],
        scratch_shapes=[
            pltpu.VMEM(old_pool.shape, old_pool.dtype),
            pltpu.VMEM((count, slots * PAGE), jnp.float32),
            pltpu.SemaphoreType.DMA((5,)),
        ],
        compiler_params=pltpu.CompilerParams(vmem_limit_bytes=9 * MIB),
        name="place_attend",
    )(place, landing, in_hbm(old_pool), bias, new_k, new_v, *asked, *arrived)


def combine_kernel(mine, other, out):
    tokens = out.shape[0]
    for j in range(out.shape[1] // HD):
        rows = slice(j * tokens, (j + 1) * tokens)
        a, b = mine[rows, :], other[rows, :]
        top_a, top_b = a[:, HD : 2 * HD], b[:, HD : 2 * HD]
        top = jnp.maximum(top_a, top_b)
        scale_a, scale_b = jnp.exp(top_a - top), jnp.exp(top_b - top)
        total = a[:, 2 * HD :] * scale_a + b[:, 2 * HD :] * scale_b
        value = (a[:, :HD] * scale_a + b[:, :HD] * scale_b) / total
        out[:, j * HD : (j + 1) * HD] = value.astype(out.dtype)


def combine(mine, other, tokens):
    return pl.pallas_call(
        combine_kernel,
        out_shape=jax.ShapeDtypeStruct((tokens, GQ // 2 * HD), jnp.bfloat16),
        in_specs=[VM, VM],
        out_specs=VM,
        compiler_params=pltpu.CompilerParams(vmem_limit_bytes=2 * MIB),
        name="combine",
    )(mine, other)


def project_kernel(groups, place, weight, stream, mine, sibling, res_out):
    half = place[1]
    members, tokens, width = mine.shape
    sums = [stream[g * tokens : (g + 1) * tokens].astype(jnp.float32) for g in range(groups)]
    for h in range(KVH):
        for g in range(groups):
            m = h * groups + g
            first = jnp.where(half == 0, mine[m], sibling[m])
            second = jnp.where(half == 0, sibling[m], mine[m])
            sums[g] = sums[g] + lax.dot_general(
                jnp.concatenate([first, second], axis=1),
                weight[:, 2 * h * width : 2 * (h + 1) * width],
                (((1,), (1,)), ((), ())),
                preferred_element_type=jnp.float32,
            )
    for g in range(groups):
        res_out[g * tokens : (g + 1) * tokens] = sums[g].astype(res_out.dtype)


def project(place, weight, stream, mine, sibling, groups):
    return pl.pallas_call(
        functools.partial(project_kernel, groups),
        out_shape=jax.ShapeDtypeStruct(stream.shape, jnp.bfloat16),
        in_specs=[SM, VM, VM, VM, VM],
        out_specs=VM,
        compiler_params=pltpu.CompilerParams(vmem_limit_bytes=4 * MIB),
        name="out_projection",
    )(place, in_vmem(weight), stream, mine, sibling)


def ffn_kernel(place, landing, mine, sibling, gain, gate, *refs):
    up, refs = refs[:SPLIT], refs[SPLIT:]
    down, late, old_pool, _, own_out, other_out, kv_out = refs[:7]
    down_buf, normed, hidden, pool, down_sem, late_sem, pool_sem = refs[7:]
    member, half = place[0], place[1]
    members, tokens, width = mine.shape
    per_peer = ARRIVE // members
    resident = kv_out.shape[0] - ARRIVE

    def late_copy(i, k, c):
        source = lax.rem(member - k + members, members)
        spot = i * per_peer + c
        return pltpu.make_async_copy(
            late.at[spot], kv_out.at[resident + landing[source, c]], late_sem.at[spot]
        )

    late_chunks = [(0, 0), (1, 1), (2, members - 1)]

    pool_in = pltpu.make_async_copy(old_pool, pool, pool_sem.at[0])
    pool_out = pltpu.make_async_copy(pool, kv_out, pool_sem.at[1])

    @pl.when(half == 0)
    def _():
        pool_in.start()

    @pl.when(half == 1)
    def _():
        for i, k in late_chunks:

            @pl.loop(0, per_peer)
            def _(c):
                late_copy(i, k, c).start()

    depth, hidden_count = up[0].shape
    features = depth * SPLIT
    down_copies = []
    for t in range(members):
        cols = pl.ds(t * 2 * width, 2 * width)
        down_copies.append(
            pltpu.make_async_copy(down.at[:, cols], down_buf.at[:, cols], down_sem.at[t])
        )
        down_copies[-1].start()

    square = jnp.zeros((tokens, width), jnp.float32)
    for block in (mine, sibling):
        for t in range(members):
            x = block[t].astype(jnp.float32)
            square = square + x * x
    factor = lax.rsqrt(jnp.sum(square, axis=1, keepdims=True) / features + 1e-05)
    for t in range(members):
        first = jnp.where(half == 0, mine[t], sibling[t])
        second = jnp.where(half == 0, sibling[t], mine[t])
        x = jnp.concatenate([first, second], axis=1).astype(jnp.float32)
        cols = slice(2 * t * width, 2 * (t + 1) * width)
        normed[:, cols] = (x * factor * gain[cols][None, :]).astype(jnp.bfloat16)
    tile = min(1024, hidden_count)
    for f in range(hidden_count // tile):
        cols = slice(f * tile, (f + 1) * tile)
        gate_act = jnp.dot(normed[...], gate[:, cols], preferred_element_type=jnp.float32)
        up_act = 0.0
        for i in range(SPLIT):
            x = normed[:, i * depth : (i + 1) * depth]
            up_act += jnp.dot(x, up[i][:, cols], preferred_element_type=jnp.float32)
        h = gate_act / (1.0 + jnp.exp(-gate_act)) * up_act
        hidden[:, cols] = h.astype(jnp.bfloat16)
    @pl.when(half == 0)
    def _():
        pool_in.wait()
        pool_out.start()

    for t in range(members):
        down_copies[t].wait()
        part = jnp.dot(
            hidden[...],
            down_buf[:, 2 * t * width : 2 * (t + 1) * width],
            preferred_element_type=jnp.float32,
        )
        first, second = part[:, :width], part[:, width:]
        own_out[t] = jnp.where(half == 0, first, second)
        other_out[t] = jnp.where(half == 0, second, first).astype(jnp.bfloat16)

    @pl.when(half == 0)
    def _():
        pool_out.wait()

    @pl.when(half == 1)
    def _():
        for i, k in late_chunks:

            @pl.loop(0, per_peer)
            def _(c):
                late_copy(i, k, c).wait()


def feed_forward(place, landing, mine, sibling, gain, gate, up, down, late, old_pool, kv):
    tokens = mine.shape[1]
    hidden_count, features = down.shape
    return pl.pallas_call(
        ffn_kernel,
        out_shape=[
            jax.ShapeDtypeStruct(mine.shape, jnp.float32),
            jax.ShapeDtypeStruct(mine.shape, jnp.bfloat16),
            jax.ShapeDtypeStruct(kv.shape, kv.dtype),
        ],
        in_specs=[SM, SM, VM, VM, VM] + [VM] * (1 + SPLIT) + [HBM, VM, HBM, HBM],
        out_specs=[VM, VM, HBM],
        input_output_aliases={5 + 1 + SPLIT + 3: 2},
        scratch_shapes=[
            pltpu.VMEM(down.shape, down.dtype),
            pltpu.VMEM((tokens, features), jnp.bfloat16),
            pltpu.VMEM((tokens, hidden_count), jnp.bfloat16),
            pltpu.VMEM(kv.shape, kv.dtype),
            pltpu.SemaphoreType.DMA((mine.shape[0],)),
            pltpu.SemaphoreType.DMA((late.shape[0],)),
            pltpu.SemaphoreType.DMA((2,)),
        ],
        compiler_params=pltpu.CompilerParams(vmem_limit_bytes=21 * MIB),
        name="feed_forward",
    )(
        place,
        landing,
        mine,
        sibling,
        gain,
        *map(in_vmem, (gate, *up)),
        in_hbm(down),
        late,
        in_hbm(old_pool),
        in_hbm(kv),
    )


def local(
    kv_pages,
    page_list,
    block_tables,
    lengths,
    queries,
    fresh_kv,
    stream,
    out_proj,
    norm_gain,
    gate_weight,
    up_weight,
    down_weight,
):
    members = lax.axis_size("tp")
    member = lax.axis_index("tp")
    half = lax.axis_index("pd")
    place = jnp.stack([member, half]).astype(jnp.int32)
    slots = kv_pages.shape[0]
    per_peer = ARRIVE // members
    groups = members // KVH
    rows = block_tables.shape[0]
    steps = queries.shape[1]
    tokens = rows * steps

    def send(x, *hops):
        route = [
            (2 * t + start, 2 * ((t + k) % members) + end)
            for start, k, end in hops
            for t in range(members)
        ]
        return lax.ppermute(x, BOTH, route)

    def swap(x):
        return lax.ppermute(x, "pd", [(0, 1), (1, 0)])

    near, own_chunk, *far = pack(place, page_list, kv_pages)
    far = dict(zip(range(2, members - 1), far))
    crossed = lax.ppermute(near, "pd", [(0, 1)])
    behind, ahead = crossed[:per_peer], crossed[per_peer:]
    hosts = (2, members - 2)
    middle = sorted(set(far) - set(hosts), key=lambda k: abs(k - members // 2))
    arrived = {k: send(far[k], (0, k, 1)) for k in middle}
    for host, k, block in zip(hosts, (1, -1), (ahead, behind)):
        block = jnp.where(half == 0, far[host], block)
        arrived[host] = send(block, (0, host, 1), (1, k, 0))

    *held, bias, landing = prepare(
        place,
        lengths,
        block_tables,
        page_list.reshape(members, slots),
        groups,
        ((out_proj, 1), (up_weight, SPLIT)),
        (near,),
    )

    order = sorted(arrived)
    arrays = [own_chunk] + [arrived[k] for k in order]
    chunks = (
        [(0, 0)] + [(1 + order.index(host), k % members) for host, k in zip(hosts, (1, -1))],
        [(1 + i, k) for i, k in enumerate(order)],
    )
    padding = ((0, -tokens % 128), (0, 0))
    new_k = jnp.pad(fresh_kv[:, :, 0].reshape(tokens, HD), padding)
    new_v = jnp.pad(fresh_kv[:, :, 1].reshape(tokens, HD), padding)
    asked = [queries[:, st] for st in range(steps)]
    kv_part, keep, give, late = place_and_attend(
        place, landing, kv_pages, bias, new_k, new_v, asked, arrays, chunks
    )
    late = lax.ppermute(late, "pd", [(0, 1)])

    def everywhere(x):
        spread = jnp.broadcast_to(x[None], (members, *x.shape))
        mine = lax.all_to_all(spread, "tp", split_axis=0, concat_axis=0)
        return mine, swap(mine)

    att_mine = combine(keep, swap(give), tokens)
    here, there = everywhere(att_mine)

    inner = stream.reshape(steps, groups, rows, -1).transpose(1, 0, 2, 3).reshape(stream.shape)
    residual = project(place, held[0], inner, here, there, groups)

    mine, sibling = everywhere(residual)
    own, other, kv_after = feed_forward(
        place, landing, mine, sibling, norm_gain, gate_weight, held[1:], down_weight, late, kv_pages, kv_part
    )
    summed = (own + swap(other).astype(jnp.float32)).astype(jnp.bfloat16)
    shares = lax.all_to_all(summed, "tp", split_axis=0, concat_axis=0)
    layer = residual.astype(jnp.float32) + jnp.sum(shares.astype(jnp.float32), axis=0)
    layer_out = (
        layer.astype(jnp.bfloat16)
        .reshape(groups, steps, rows, -1)
        .transpose(1, 0, 2, 3)
        .reshape(stream.shape)
    )
    return (kv_after, layer_out)


def solution(mesh):
    return jax.shard_map(
        local,
        mesh=mesh,
        in_specs=(
            P(("grp", "tp", "pd"), None, None, None),
            P("grp"),
            P(("grp", "tp"), None),
            P("grp"),
            P(("grp", "tp"), None, None),
            P(("grp", "tp"), None, None, None),
            P("grp", ("tp", "pd")),
            P(("tp", "pd"), None),
            P(),
            P(None, ("tp", "pd")),
            P(None, ("tp", "pd")),
            P(("tp", "pd"), None),
        ),
        out_specs=(P(("grp", "tp", "pd"), None, None, None), P("grp", ("tp", "pd"))),
        check_vma=False,
    )
```

```python
import functools
import math

import jax
import jax.numpy as jnp
from jax import lax
from jax.experimental import pallas as pl
from jax.experimental.pallas import tpu as pltpu
from jax.sharding import PartitionSpec as P

HD = 128
KVH = 8
GQ = 8
PAGE = 16
REQ_DEV = 2
NEWP = 128
ARRIVE = REQ_DEV * NEWP
MIB = 1024 * 1024
BOTH = ("tp", "pd")
SPLIT = 4

VM = pl.BlockSpec(memory_space=pltpu.VMEM)
SM = pl.BlockSpec(memory_space=pltpu.SMEM)
ANY = pl.BlockSpec(memory_space=pl.ANY)
HBM = pl.BlockSpec(memory_space=pltpu.HBM)


def in_vmem(x):
    return pltpu.with_memory_space_constraint(x, pltpu.VMEM)


def in_hbm(x):
    return pltpu.with_memory_space_constraint(x, pltpu.HBM)


def pack_kernel(members, place, pages, pool, *refs):
    count = members - 1
    outs = refs[:count]
    packed, held, own, counts, sems, load_sems = refs[count:]
    member, half = place[0], place[1]
    slots = pool.shape[0]
    per_peer = ARRIVE // members
    parts = 4
    step = slots // parts

    @pl.when(half == 0)
    def _():
        own_copy = pltpu.make_async_copy(pages, own, load_sems.at[parts])
        own_copy.start()
        loads = []
        for i in range(parts):
            window = pl.ds(i * step, step)
            loads.append(
                pltpu.make_async_copy(pool.at[window], held.at[window], load_sems.at[i])
            )
            loads[-1].start()
        own_copy.wait()
        start = member * slots

        if members in (4, 8):
            carry = (jnp.int32(0), jnp.int32(0))
            for i in range(parts):
                loads[i].wait()

                def body(j, words, base=i * step):
                    low, high = words
                    entry = own[start + base + j]
                    ahead = ((entry >> 8) - member + 1) & (members - 1)
                    leaves = entry >= 0
                    shift = (ahead & 3) * 8
                    is_low = ahead < 4
                    count = (jnp.where(is_low, low, high) >> shift) & 255
                    one = jnp.where(leaves, jnp.int32(1) << shift, 0)
                    packed[jnp.where(leaves, ahead * per_peer + count, ARRIVE)] = held[base + j]
                    return (
                        low + jnp.where(is_low, one, 0),
                        high + jnp.where(is_low, 0, one),
                    )

                carry = lax.fori_loop(0, step, body, carry, unroll=13)
        else:
            for i in range(parts):
                loads[i].wait()

            @pl.loop(0, members + 1)
            def _(i):
                counts[i] = 0

            @pl.loop(0, slots)
            def _(i):
                entry = own[start + i]
                ahead = lax.rem((entry >> 8) - member + members + 1, members)
                row = jnp.where(entry >= 0, ahead, members)
                count = counts[row]
                counts[row] = count + 1
                packed[jnp.where(entry >= 0, row * per_peer + count, ARRIVE)] = held[i]

        copies = []
        near, own_chunk, *far = outs
        moves = [(near, 0, 0), (near, per_peer, 2), (own_chunk, 0, 1)]
        moves += [(out, 0, 3 + i) for i, out in enumerate(far)]
        for i, (out, first, row) in enumerate(moves):
            copies.append(
                pltpu.make_async_copy(
                    packed.at[pl.ds(row * per_peer, per_peer)],
                    out.at[pl.ds(first, per_peer)],
                    sems.at[i],
                )
            )
            copies[-1].start()
        for copy in copies:
            copy.wait()


def pack(place, pages, pool):
    members = lax.axis_size("tp")
    per_peer = ARRIVE // members
    chunk = pool.shape[1:]
    return pl.pallas_call(
        functools.partial(pack_kernel, members),
        out_shape=[pltpu.HBM((2 * per_peer, *chunk), pool.dtype)]
        + [pltpu.HBM((per_peer, *chunk), pool.dtype)] * (members - 2),
        in_specs=[SM, HBM, HBM],
        out_specs=[HBM] * (members - 1),
        scratch_shapes=[
            pltpu.VMEM((ARRIVE + 1, *chunk), pool.dtype),
            pltpu.VMEM(pool.shape, pool.dtype),
            pltpu.SMEM(pages.shape, jnp.int32),
            pltpu.SMEM((members + 1,), jnp.int32),
            pltpu.SemaphoreType.DMA((members,)),
            pltpu.SemaphoreType.DMA((5,)),
        ],
        compiler_params=pltpu.CompilerParams(vmem_limit_bytes=8 * MIB),
        name="pack_pages",
    )(place, in_hbm(pages), in_hbm(pool))


def prepare_kernel(count, parts, groups, place, listed, lengths_hbm, table_hbm, *refs):
    sources = refs[:count]
    held = refs[len(refs) - 8 - parts : -8]
    bias, landing, entries, whole, part, lengths, table, sems = refs[-8:]
    small = [
        pltpu.make_async_copy(lengths_hbm, lengths, sems.at[parts]),
        pltpu.make_async_copy(table_hbm, table, sems.at[parts + 1]),
    ]
    for copy in small:
        copy.start()
    copies = []
    for source in sources:
        done = 0
        while done < source.shape[0]:
            part_out = held[len(copies)]
            window = pl.ds(done, part_out.shape[0])
            copies.append(
                pltpu.make_async_copy(source.at[window], part_out, sems.at[len(copies)])
            )
            copies[-1].start()
            done += part_out.shape[0]

    member = place[0]
    entries[...] = jnp.full(entries.shape, -1, jnp.int32)
    entries[:, : listed.shape[1]] = listed[...]
    entry = entries[...]
    members, lanes = entry.shape
    per_peer = ARRIVE // members
    wanted = (entry >= 0) & ((entry >> 8) == member)
    before = lax.broadcasted_iota(jnp.int32, (lanes, lanes), 0) < lax.broadcasted_iota(
        jnp.int32, (lanes, lanes), 1
    )
    rank = jnp.dot(
        jnp.where(wanted, 1.0, 0.0).astype(jnp.bfloat16),
        jnp.where(before, 1.0, 0.0).astype(jnp.bfloat16),
        preferred_element_type=jnp.float32,
    ).astype(jnp.int32)
    column = lax.broadcasted_iota(jnp.int32, landing.shape, 1)
    found = jnp.zeros(landing.shape, jnp.int32)
    distance = member - lax.broadcasted_iota(jnp.int32, entry.shape, 0)
    distance = jnp.where(distance < 0, distance + members, distance)
    is_near = (distance <= 1) | (distance == members - 1)
    slot_lane = lax.broadcasted_iota(jnp.int32, entry.shape, 1) - (listed.shape[1] - ARRIVE)
    near = jnp.zeros(entry.shape, jnp.float32)
    for c in range(per_peer):
        slot = jnp.sum(jnp.where(wanted & (rank == c), entry & 255, 0), axis=1, keepdims=True)
        found = jnp.where(column == c, slot, found)
        near = jnp.where(is_near & (slot == slot_lane), 1.0, near)
    landing[...] = found
    near = jnp.max(near, axis=0, keepdims=True)
    present = jnp.where(place[1] == 0, near, 1.0 - near)

    for copy in small:
        copy.wait()
    rows, pages = table.shape
    wide = whole.shape[1]
    base = lax.rem(member, groups) * rows
    columns = table[...].T
    page_id = lax.broadcasted_iota(jnp.int32, (pages, wide), 0)
    slot_id = lax.broadcasted_iota(jnp.int32, (pages, wide), 1)
    row_id = lax.broadcasted_iota(jnp.int32, (rows, 128), 0)
    over = jnp.zeros((rows, 128), jnp.int32)
    for r in range(rows):
        length = lengths[base + r]
        full = length // PAGE
        over = jnp.where(row_id == r, length - full * PAGE, over)
        hit = columns[:, r : r + 1] == slot_id
        in_whole = jnp.where(hit & (page_id < full), 1.0, 0.0)
        in_part = jnp.where(hit & (page_id == full), 1.0, 0.0)
        whole[r : r + 1, :] = jnp.sum(in_whole, axis=0, keepdims=True)
        part[r : r + 1, :] = jnp.sum(in_part, axis=0, keepdims=True)
    whole_b = (whole[...] * present).astype(jnp.bfloat16)
    part_b = (part[...] * present).astype(jnp.bfloat16)
    lane = lax.broadcasted_iota(jnp.int32, (rows, 128), 1)
    inside = (lane % PAGE) < over
    per_block = 128 // PAGE
    slot_in = lax.broadcasted_iota(jnp.int32, (wide, 128), 0)
    lane_in = lax.broadcasted_iota(jnp.int32, (wide, 128), 1) // PAGE
    for i in range(bias.shape[1] // 128):
        expand = jnp.where(slot_in == lane_in + i * per_block, 1.0, 0.0).astype(jnp.bfloat16)
        times = jnp.dot(whole_b, expand, preferred_element_type=jnp.float32)
        extra = jnp.dot(part_b, expand, preferred_element_type=jnp.float32)
        bias[:, i * 128 : (i + 1) * 128] = jnp.log(times + jnp.where(inside, extra, 0.0))

    for copy in copies:
        copy.wait()


def prepare(place, lengths, tables, listed, groups, weights, first):
    rows = tables.shape[0]
    members, slots = listed.shape
    wide = -(-slots // 128) * 128
    moved = sum(w.size * w.dtype.itemsize for w, _ in weights)
    pieces = [
        pltpu.VMEM((w.shape[0] // n, w.shape[1]), w.dtype) for w, n in weights for _ in range(n)
    ]
    weights = [w for w, _ in weights]
    count, parts = len(weights), len(pieces)
    return pl.pallas_call(
        functools.partial(prepare_kernel, count, parts, groups),
        out_shape=pieces
        + [
            jax.ShapeDtypeStruct((rows, slots * PAGE), jnp.float32),
            jax.ShapeDtypeStruct((members, 128), jnp.int32),
        ],
        in_specs=[SM, VM] + [HBM] * (2 + count + len(first)),
        out_specs=[VM] * (parts + 2),
        scratch_shapes=[
            pltpu.VMEM((members, wide), jnp.int32),
            pltpu.VMEM((rows, wide), jnp.float32),
            pltpu.VMEM((rows, wide), jnp.float32),
            pltpu.SMEM(lengths.shape, lengths.dtype),
            pltpu.VMEM(tables.shape, tables.dtype),
            pltpu.SemaphoreType.DMA((parts + 2,)),
        ],
        compiler_params=pltpu.CompilerParams(vmem_limit_bytes=13 * MIB),
        cost_estimate=pl.CostEstimate(flops=0, bytes_accessed=moved, transcendentals=0),
        name="prepare",
    )(place, listed, *[in_hbm(x) for x in (lengths, tables, *weights, *first)])


def attend_kernel(members, steps, chunks, place, landing, old_pool, bias, new_k, new_v, *refs):
    asked, refs = refs[:steps], refs[steps:]
    arrived, refs = refs[:-8], refs[-8:]
    kv_out, keep, give, late, pool, spare, scores, sems = refs
    member, half = place[0], place[1]
    slots = pool.shape[0]
    resident = slots - ARRIVE
    per_peer = ARRIVE // members
    rows = bias.shape[0]
    count = rows * steps * GQ
    pool[resident:] = jnp.zeros((ARRIVE, *pool.shape[1:]), pool.dtype)

    def place_pages(which):
        for i, k in chunks[which]:
            source = lax.rem(member - k + members, members)

            @pl.loop(0, per_peer, unroll=math.gcd(per_peer, 8))
            def _(c):
                pool[resident + landing[source, c]] = arrived[i][c]

    spare_in = pltpu.make_async_copy(old_pool, spare, sems.at[0])
    spare_out = pltpu.make_async_copy(spare, kv_out, sems.at[1])

    late_copies = [
        pltpu.make_async_copy(
            arrived[i], late.at[pl.ds(n * per_peer, per_peer)], sems.at[2 + n]
        )
        for n, (i, _) in enumerate(chunks[0])
    ]

    @pl.when(half == 0)
    def _():
        spare_in.start()
        for copy in late_copies:
            copy.start()
        pool[:resident] = jnp.zeros((resident, *pool.shape[1:]), pool.dtype)
        place_pages(0)
        spare_in.wait()
        spare_out.start()

    @pl.when(half == 1)
    def _():
        copy = pltpu.make_async_copy(
            old_pool.at[pl.ds(0, resident)], pool.at[pl.ds(0, resident)], sems.at[0]
        )
        copy.start()
        place_pages(1)
        copy.wait()
        pltpu.make_async_copy(pool, kv_out, sems.at[1]).start()

    scale = 1.0 / math.sqrt(HD)
    q = jnp.concatenate(
        [ask[:, j * HD : (j + 1) * HD] for j in range(GQ) for ask in asked], axis=0
    )
    nt = (((1,), (1,)), ((), ()))
    group = 24
    width = group * PAGE
    lanes = 128
    fresh = lax.dot_general(q, new_k[...], nt, preferred_element_type=jnp.float32) * scale
    q_id = lax.broadcasted_iota(jnp.int32, fresh.shape, 0)
    t_id = lax.broadcasted_iota(jnp.int32, fresh.shape, 1)
    allowed = (q_id % rows == t_id // steps) & (t_id % steps <= (q_id // rows) % steps)
    fresh = jnp.where(allowed & (half == 1), fresh, -jnp.inf)
    peak = fresh
    for c in range(slots // group):
        keys = pool[c * group : (c + 1) * group, 0].reshape(width, HD)
        s = lax.dot_general(q, keys, nt, preferred_element_type=jnp.float32) * scale
        b = bias[:, c * width : (c + 1) * width]
        s = (s.reshape(count // rows, rows, width) + b[None]).reshape(count, width)
        scores[:, c * width : (c + 1) * width] = s
        for i in range(width // lanes):
            peak = jnp.maximum(peak, s[:, i * lanes : (i + 1) * lanes])
    top = jnp.maximum(jnp.max(peak, axis=1, keepdims=True), -1e30)
    p = jnp.exp(fresh - top)
    total = p
    acc = jnp.dot(p.astype(jnp.bfloat16), new_v[...], preferred_element_type=jnp.float32)
    for c in range(slots // group):
        p = jnp.exp(scores[:, c * width : (c + 1) * width] - top)
        for i in range(width // lanes):
            total = total + p[:, i * lanes : (i + 1) * lanes]
        values = pool[c * group : (c + 1) * group, 1].reshape(width, HD)
        acc = acc + jnp.dot(p.astype(jnp.bfloat16), values, preferred_element_type=jnp.float32)
    total = jnp.sum(total, axis=1, keepdims=True)
    middle = count // 2
    for out, first in ((keep, half == 0), (give, half == 1)):
        out[:, :HD] = jnp.where(first, acc[:middle], acc[middle:])
        out[:, HD : 2 * HD] = jnp.broadcast_to(
            jnp.where(first, top[:middle], top[middle:]), (middle, HD)
        )
        out[:, 2 * HD :] = jnp.broadcast_to(
            jnp.where(first, total[:middle], total[middle:]), (middle, HD)
        )

    @pl.when(half == 1)
    def _():
        pltpu.make_async_copy(pool, kv_out, sems.at[1]).wait()

    @pl.when(half == 0)
    def _():
        spare_out.wait()
        for copy in late_copies:
            copy.wait()


def place_and_attend(place, landing, old_pool, bias, new_k, new_v, asked, arrived, chunks):
    members = landing.shape[0]
    slots = old_pool.shape[0]
    steps = len(asked)
    count = bias.shape[0] * steps * GQ
    part = jax.ShapeDtypeStruct((count // 2, 3 * HD), jnp.float32)
    return pl.pallas_call(
        functools.partial(attend_kernel, members, steps, chunks),
        out_shape=[
            jax.ShapeDtypeStruct(old_pool.shape, old_pool.dtype),
            part,
            part,
            jax.ShapeDtypeStruct((3 * ARRIVE // members, *old_pool.shape[1:]), old_pool.dtype),
        ],
        in_specs=[SM, SM, HBM, VM, VM, VM] + [VM] * (steps + len(arrived)),
        out_specs=[HBM, VM, VM, HBM],
        scratch_shapes=[
            pltpu.VMEM(old_pool.shape, old_pool.dtype),
            pltpu.VMEM(old_pool.shape, old_pool.dtype),
            pltpu.VMEM((count, slots * PAGE), jnp.float32),
            pltpu.SemaphoreType.DMA((5,)),
        ],
        compiler_params=pltpu.CompilerParams(vmem_limit_bytes=12 * MIB),
        name="place_attend",
    )(place, landing, in_hbm(old_pool), bias, new_k, new_v, *asked, *arrived)


def combine_kernel(mine, other, out):
    tokens = out.shape[0]
    for j in range(out.shape[1] // HD):
        rows = slice(j * tokens, (j + 1) * tokens)
        a, b = mine[rows, :], other[rows, :]
        top_a, top_b = a[:, HD : 2 * HD], b[:, HD : 2 * HD]
        top = jnp.maximum(top_a, top_b)
        scale_a, scale_b = jnp.exp(top_a - top), jnp.exp(top_b - top)
        total = a[:, 2 * HD :] * scale_a + b[:, 2 * HD :] * scale_b
        value = (a[:, :HD] * scale_a + b[:, :HD] * scale_b) / total
        out[:, j * HD : (j + 1) * HD] = value.astype(out.dtype)


def combine(mine, other, tokens):
    return pl.pallas_call(
        combine_kernel,
        out_shape=jax.ShapeDtypeStruct((tokens, GQ // 2 * HD), jnp.bfloat16),
        in_specs=[VM, VM],
        out_specs=VM,
        compiler_params=pltpu.CompilerParams(vmem_limit_bytes=2 * MIB),
        name="combine",
    )(mine, other)


def project_kernel(groups, place, weight, stream, mine, sibling, res_out):
    half = place[1]
    members, tokens, width = mine.shape
    sums = [stream[g * tokens : (g + 1) * tokens].astype(jnp.float32) for g in range(groups)]
    for h in range(KVH):
        for g in range(groups):
            m = h * groups + g
            first = jnp.where(half == 0, mine[m], sibling[m])
            second = jnp.where(half == 0, sibling[m], mine[m])
            sums[g] = sums[g] + lax.dot_general(
                jnp.concatenate([first, second], axis=1),
                weight[:, 2 * h * width : 2 * (h + 1) * width],
                (((1,), (1,)), ((), ())),
                preferred_element_type=jnp.float32,
            )
    for g in range(groups):
        res_out[g * tokens : (g + 1) * tokens] = sums[g].astype(res_out.dtype)


def project(place, weight, stream, mine, sibling, groups):
    return pl.pallas_call(
        functools.partial(project_kernel, groups),
        out_shape=jax.ShapeDtypeStruct(stream.shape, jnp.bfloat16),
        in_specs=[SM, VM, VM, VM, VM],
        out_specs=VM,
        compiler_params=pltpu.CompilerParams(vmem_limit_bytes=4 * MIB),
        name="out_projection",
    )(place, in_vmem(weight), stream, mine, sibling)


def ffn_kernel(place, landing, mine, sibling, gain, gate, *refs):
    up, refs = refs[:SPLIT], refs[SPLIT:]
    down, late, _, own_out, other_out, kv_out = refs[:6]
    down_buf, normed, hidden, down_sem, late_sem = refs[6:]
    member, half = place[0], place[1]
    members, tokens, width = mine.shape
    per_peer = ARRIVE // members
    resident = kv_out.shape[0] - ARRIVE

    def late_copy(i, k, c):
        source = lax.rem(member - k + members, members)
        spot = i * per_peer + c
        return pltpu.make_async_copy(
            late.at[spot], kv_out.at[resident + landing[source, c]], late_sem.at[spot]
        )

    late_chunks = [(0, 0), (1, 1), (2, members - 1)]

    @pl.when(half == 1)
    def _():
        for i, k in late_chunks:

            @pl.loop(0, per_peer)
            def _(c):
                late_copy(i, k, c).start()

    depth, hidden_count = up[0].shape
    features = depth * SPLIT
    down_copies = []
    for t in range(members):
        cols = pl.ds(t * 2 * width, 2 * width)
        down_copies.append(
            pltpu.make_async_copy(down.at[:, cols], down_buf.at[:, cols], down_sem.at[t])
        )
        down_copies[-1].start()

    square = jnp.zeros((tokens, width), jnp.float32)
    for block in (mine, sibling):
        for t in range(members):
            x = block[t].astype(jnp.float32)
            square = square + x * x
    factor = lax.rsqrt(jnp.sum(square, axis=1, keepdims=True) / features + 1e-05)
    for t in range(members):
        first = jnp.where(half == 0, mine[t], sibling[t])
        second = jnp.where(half == 0, sibling[t], mine[t])
        x = jnp.concatenate([first, second], axis=1).astype(jnp.float32)
        cols = slice(2 * t * width, 2 * (t + 1) * width)
        normed[:, cols] = (x * factor * gain[cols][None, :]).astype(jnp.bfloat16)
    tile = min(1024, hidden_count)
    for f in range(hidden_count // tile):
        cols = slice(f * tile, (f + 1) * tile)
        gate_act = jnp.dot(normed[...], gate[:, cols], preferred_element_type=jnp.float32)
        up_act = 0.0
        for i in range(SPLIT):
            x = normed[:, i * depth : (i + 1) * depth]
            up_act += jnp.dot(x, up[i][:, cols], preferred_element_type=jnp.float32)
        h = gate_act / (1.0 + jnp.exp(-gate_act)) * up_act
        hidden[:, cols] = h.astype(jnp.bfloat16)
    for t in range(members):
        down_copies[t].wait()
        part = jnp.dot(
            hidden[...],
            down_buf[:, 2 * t * width : 2 * (t + 1) * width],
            preferred_element_type=jnp.float32,
        )
        first, second = part[:, :width], part[:, width:]
        own_out[t] = jnp.where(half == 0, first, second)
        other_out[t] = jnp.where(half == 0, second, first).astype(jnp.bfloat16)

    @pl.when(half == 1)
    def _():
        for i, k in late_chunks:

            @pl.loop(0, per_peer)
            def _(c):
                late_copy(i, k, c).wait()


def feed_forward(place, landing, mine, sibling, gain, gate, up, down, late, kv):
    tokens = mine.shape[1]
    hidden_count, features = down.shape
    return pl.pallas_call(
        ffn_kernel,
        out_shape=[
            jax.ShapeDtypeStruct(mine.shape, jnp.float32),
            jax.ShapeDtypeStruct(mine.shape, jnp.bfloat16),
            jax.ShapeDtypeStruct(kv.shape, kv.dtype),
        ],
        in_specs=[SM, SM, VM, VM, VM] + [VM] * (1 + SPLIT) + [HBM, VM, HBM],
        out_specs=[VM, VM, HBM],
        input_output_aliases={5 + 1 + SPLIT + 2: 2},
        scratch_shapes=[
            pltpu.VMEM(down.shape, down.dtype),
            pltpu.VMEM((tokens, features), jnp.bfloat16),
            pltpu.VMEM((tokens, hidden_count), jnp.bfloat16),
            pltpu.SemaphoreType.DMA((mine.shape[0],)),
            pltpu.SemaphoreType.DMA((late.shape[0],)),
        ],
        compiler_params=pltpu.CompilerParams(vmem_limit_bytes=19 * MIB),
        name="feed_forward",
    )(
        place,
        landing,
        mine,
        sibling,
        gain,
        *map(in_vmem, (gate, *up)),
        in_hbm(down),
        late,
        in_hbm(kv),
    )


def local(
    kv_pages,
    page_list,
    block_tables,
    lengths,
    queries,
    fresh_kv,
    stream,
    out_proj,
    norm_gain,
    gate_weight,
    up_weight,
    down_weight,
):
    members = lax.axis_size("tp")
    member = lax.axis_index("tp")
    half = lax.axis_index("pd")
    place = jnp.stack([member, half]).astype(jnp.int32)
    slots = kv_pages.shape[0]
    per_peer = ARRIVE // members
    groups = members // KVH
    rows = block_tables.shape[0]
    steps = queries.shape[1]
    tokens = rows * steps

    def send(x, *hops):
        route = [
            (2 * t + start, 2 * ((t + k) % members) + end)
            for start, k, end in hops
            for t in range(members)
        ]
        return lax.ppermute(x, BOTH, route)

    def swap(x):
        return lax.ppermute(x, "pd", [(0, 1), (1, 0)])

    near, own_chunk, *far = pack(place, page_list, kv_pages)
    far = dict(zip(range(2, members - 1), far))
    crossed = lax.ppermute(near, "pd", [(0, 1)])
    behind, ahead = crossed[:per_peer], crossed[per_peer:]
    hosts = (2, members - 2)
    middle = sorted(set(far) - set(hosts), key=lambda k: abs(k - members // 2))
    arrived = {k: send(far[k], (0, k, 1)) for k in middle}
    for host, k, block in zip(hosts, (1, -1), (ahead, behind)):
        block = jnp.where(half == 0, far[host], block)
        arrived[host] = send(block, (0, host, 1), (1, k, 0))

    *held, bias, landing = prepare(
        place,
        lengths,
        block_tables,
        page_list.reshape(members, slots),
        groups,
        ((out_proj, 1), (up_weight, SPLIT)),
        (near,),
    )

    order = sorted(arrived)
    arrays = [own_chunk] + [arrived[k] for k in order]
    chunks = (
        [(0, 0)] + [(1 + order.index(host), k % members) for host, k in zip(hosts, (1, -1))],
        [(1 + i, k) for i, k in enumerate(order)],
    )
    padding = ((0, -tokens % 128), (0, 0))
    new_k = jnp.pad(fresh_kv[:, :, 0].reshape(tokens, HD), padding)
    new_v = jnp.pad(fresh_kv[:, :, 1].reshape(tokens, HD), padding)
    asked = [queries[:, st] for st in range(steps)]
    kv_part, keep, give, late = place_and_attend(
        place, landing, kv_pages, bias, new_k, new_v, asked, arrays, chunks
    )
    late = lax.ppermute(late, "pd", [(0, 1)])

    def everywhere(x):
        spread = jnp.broadcast_to(x[None], (members, *x.shape))
        mine = lax.all_to_all(spread, "tp", split_axis=0, concat_axis=0)
        return mine, swap(mine)

    att_mine = combine(keep, swap(give), tokens)
    here, there = everywhere(att_mine)

    inner = stream.reshape(steps, groups, rows, -1).transpose(1, 0, 2, 3).reshape(stream.shape)
    residual = project(place, held[0], inner, here, there, groups)

    mine, sibling = everywhere(residual)
    own, other, kv_after = feed_forward(
        place, landing, mine, sibling, norm_gain, gate_weight, held[1:], down_weight, late, kv_part
    )
    summed = (own + swap(other).astype(jnp.float32)).astype(jnp.bfloat16)
    shares = lax.all_to_all(summed, "tp", split_axis=0, concat_axis=0)
    layer = residual.astype(jnp.float32) + jnp.sum(shares.astype(jnp.float32), axis=0)
    layer_out = (
        layer.astype(jnp.bfloat16)
        .reshape(groups, steps, rows, -1)
        .transpose(1, 0, 2, 3)
        .reshape(stream.shape)
    )
    return (kv_after, layer_out)


def solution(mesh):
    return jax.shard_map(
        local,
        mesh=mesh,
        in_specs=(
            P(("grp", "tp", "pd"), None, None, None),
            P("grp"),
            P(("grp", "tp"), None),
            P("grp"),
            P(("grp", "tp"), None, None),
            P(("grp", "tp"), None, None, None),
            P("grp", ("tp", "pd")),
            P(("tp", "pd"), None),
            P(),
            P(None, ("tp", "pd")),
            P(None, ("tp", "pd")),
            P(("tp", "pd"), None),
        ),
        out_specs=(P(("grp", "tp", "pd"), None, None, None), P("grp", ("tp", "pd"))),
        check_vma=False,
    )
```

```python
import functools
import math

import jax
import jax.numpy as jnp
from jax import lax
from jax.experimental import pallas as pl
from jax.experimental.pallas import tpu as pltpu
from jax.sharding import PartitionSpec as P

HD = 128
KVH = 8
GQ = 8
PAGE = 16
REQ_DEV = 2
NEWP = 128
ARRIVE = REQ_DEV * NEWP
MIB = 1024 * 1024
BOTH = ("tp", "pd")
SPLIT = 4

VM = pl.BlockSpec(memory_space=pltpu.VMEM)
SM = pl.BlockSpec(memory_space=pltpu.SMEM)
ANY = pl.BlockSpec(memory_space=pl.ANY)
HBM = pl.BlockSpec(memory_space=pltpu.HBM)


def in_vmem(x):
    return pltpu.with_memory_space_constraint(x, pltpu.VMEM)


def in_hbm(x):
    return pltpu.with_memory_space_constraint(x, pltpu.HBM)


def pack_kernel(members, place, pages, pool, *refs):
    count = members - 1
    outs = refs[:count]
    packed, held, own, counts, sems, load_sems = refs[count:]
    member, half = place[0], place[1]
    slots = pool.shape[0]
    per_peer = ARRIVE // members
    parts = 4
    step = slots // parts

    @pl.when(half == 0)
    def _():
        own_copy = pltpu.make_async_copy(pages, own, load_sems.at[parts])
        own_copy.start()
        loads = []
        for i in range(parts):
            window = pl.ds(i * step, step)
            loads.append(
                pltpu.make_async_copy(pool.at[window], held.at[window], load_sems.at[i])
            )
            loads[-1].start()
        own_copy.wait()
        start = member * slots

        if members in (4, 8):
            carry = (jnp.int32(0), jnp.int32(0))
            for i in range(parts):
                loads[i].wait()

                def body(j, words, base=i * step):
                    low, high = words
                    entry = own[start + base + j]
                    ahead = ((entry >> 8) - member + 1) & (members - 1)
                    leaves = entry >= 0
                    shift = (ahead & 3) * 8
                    is_low = ahead < 4
                    count = (jnp.where(is_low, low, high) >> shift) & 255
                    one = jnp.where(leaves, jnp.int32(1) << shift, 0)
                    packed[jnp.where(leaves, ahead * per_peer + count, ARRIVE)] = held[base + j]
                    return (
                        low + jnp.where(is_low, one, 0),
                        high + jnp.where(is_low, 0, one),
                    )

                carry = lax.fori_loop(0, step, body, carry, unroll=13)
        else:
            for i in range(parts):
                loads[i].wait()

            @pl.loop(0, members + 1)
            def _(i):
                counts[i] = 0

            @pl.loop(0, slots)
            def _(i):
                entry = own[start + i]
                ahead = lax.rem((entry >> 8) - member + members + 1, members)
                row = jnp.where(entry >= 0, ahead, members)
                count = counts[row]
                counts[row] = count + 1
                packed[jnp.where(entry >= 0, row * per_peer + count, ARRIVE)] = held[i]

        copies = []
        near, own_chunk, *far = outs
        moves = [(near, 0, 0), (near, per_peer, 2), (own_chunk, 0, 1)]
        moves += [(out, 0, 3 + i) for i, out in enumerate(far)]
        for i, (out, first, row) in enumerate(moves):
            copies.append(
                pltpu.make_async_copy(
                    packed.at[pl.ds(row * per_peer, per_peer)],
                    out.at[pl.ds(first, per_peer)],
                    sems.at[i],
                )
            )
            copies[-1].start()
        for copy in copies:
            copy.wait()


def pack(place, pages, pool):
    members = lax.axis_size("tp")
    per_peer = ARRIVE // members
    chunk = pool.shape[1:]
    return pl.pallas_call(
        functools.partial(pack_kernel, members),
        out_shape=[pltpu.HBM((2 * per_peer, *chunk), pool.dtype)]
        + [pltpu.HBM((per_peer, *chunk), pool.dtype)] * (members - 2),
        in_specs=[SM, HBM, HBM],
        out_specs=[HBM] * (members - 1),
        scratch_shapes=[
            pltpu.VMEM((ARRIVE + 1, *chunk), pool.dtype),
            pltpu.VMEM(pool.shape, pool.dtype),
            pltpu.SMEM(pages.shape, jnp.int32),
            pltpu.SMEM((members + 1,), jnp.int32),
            pltpu.SemaphoreType.DMA((members,)),
            pltpu.SemaphoreType.DMA((5,)),
        ],
        compiler_params=pltpu.CompilerParams(vmem_limit_bytes=8 * MIB),
        name="pack_pages",
    )(place, in_hbm(pages), in_hbm(pool))


def prepare_kernel(count, parts, groups, place, listed, lengths_hbm, table_hbm, *refs):
    sources = refs[:count]
    held = refs[len(refs) - 8 - parts : -8]
    bias, landing, entries, whole, part, lengths, table, sems = refs[-8:]
    small = [
        pltpu.make_async_copy(lengths_hbm, lengths, sems.at[parts]),
        pltpu.make_async_copy(table_hbm, table, sems.at[parts + 1]),
    ]
    for copy in small:
        copy.start()
    copies = []
    for source in sources:
        done = 0
        while done < source.shape[0]:
            part_out = held[len(copies)]
            window = pl.ds(done, part_out.shape[0])
            copies.append(
                pltpu.make_async_copy(source.at[window], part_out, sems.at[len(copies)])
            )
            copies[-1].start()
            done += part_out.shape[0]

    member = place[0]
    entries[...] = jnp.full(entries.shape, -1, jnp.int32)
    entries[:, : listed.shape[1]] = listed[...]
    entry = entries[...]
    members, lanes = entry.shape
    per_peer = ARRIVE // members
    wanted = (entry >= 0) & ((entry >> 8) == member)
    before = lax.broadcasted_iota(jnp.int32, (lanes, lanes), 0) < lax.broadcasted_iota(
        jnp.int32, (lanes, lanes), 1
    )
    rank = jnp.dot(
        jnp.where(wanted, 1.0, 0.0).astype(jnp.bfloat16),
        jnp.where(before, 1.0, 0.0).astype(jnp.bfloat16),
        preferred_element_type=jnp.float32,
    ).astype(jnp.int32)
    column = lax.broadcasted_iota(jnp.int32, landing.shape, 1)
    found = jnp.zeros(landing.shape, jnp.int32)
    distance = member - lax.broadcasted_iota(jnp.int32, entry.shape, 0)
    distance = jnp.where(distance < 0, distance + members, distance)
    is_near = (distance <= 1) | (distance == members - 1)
    slot_lane = lax.broadcasted_iota(jnp.int32, entry.shape, 1) - (listed.shape[1] - ARRIVE)
    near = jnp.zeros(entry.shape, jnp.float32)
    for c in range(per_peer):
        slot = jnp.sum(jnp.where(wanted & (rank == c), entry & 255, 0), axis=1, keepdims=True)
        found = jnp.where(column == c, slot, found)
        near = jnp.where(is_near & (slot == slot_lane), 1.0, near)
    landing[...] = found
    near = jnp.max(near, axis=0, keepdims=True)
    present = jnp.where(place[1] == 0, near, 1.0 - near)

    for copy in small:
        copy.wait()
    rows, pages = table.shape
    wide = whole.shape[1]
    base = lax.rem(member, groups) * rows
    columns = table[...].T
    page_id = lax.broadcasted_iota(jnp.int32, (pages, wide), 0)
    slot_id = lax.broadcasted_iota(jnp.int32, (pages, wide), 1)
    row_id = lax.broadcasted_iota(jnp.int32, (rows, 128), 0)
    over = jnp.zeros((rows, 128), jnp.int32)
    for r in range(rows):
        length = lengths[base + r]
        full = length // PAGE
        over = jnp.where(row_id == r, length - full * PAGE, over)
        hit = columns[:, r : r + 1] == slot_id
        in_whole = jnp.where(hit & (page_id < full), 1.0, 0.0)
        in_part = jnp.where(hit & (page_id == full), 1.0, 0.0)
        whole[r : r + 1, :] = jnp.sum(in_whole, axis=0, keepdims=True)
        part[r : r + 1, :] = jnp.sum(in_part, axis=0, keepdims=True)
    whole_b = (whole[...] * present).astype(jnp.bfloat16)
    part_b = (part[...] * present).astype(jnp.bfloat16)
    lane = lax.broadcasted_iota(jnp.int32, (rows, 128), 1)
    inside = (lane % PAGE) < over
    per_block = 128 // PAGE
    slot_in = lax.broadcasted_iota(jnp.int32, (wide, 128), 0)
    lane_in = lax.broadcasted_iota(jnp.int32, (wide, 128), 1) // PAGE
    for i in range(bias.shape[1] // 128):
        expand = jnp.where(slot_in == lane_in + i * per_block, 1.0, 0.0).astype(jnp.bfloat16)
        times = jnp.dot(whole_b, expand, preferred_element_type=jnp.float32)
        extra = jnp.dot(part_b, expand, preferred_element_type=jnp.float32)
        bias[:, i * 128 : (i + 1) * 128] = jnp.log(times + jnp.where(inside, extra, 0.0))

    for copy in copies:
        copy.wait()


def prepare(place, lengths, tables, listed, groups, weights, first):
    rows = tables.shape[0]
    members, slots = listed.shape
    wide = -(-slots // 128) * 128
    moved = sum(w.size * w.dtype.itemsize for w, _ in weights)
    pieces = [
        pltpu.VMEM((w.shape[0] // n, w.shape[1]), w.dtype) for w, n in weights for _ in range(n)
    ]
    weights = [w for w, _ in weights]
    count, parts = len(weights), len(pieces)
    return pl.pallas_call(
        functools.partial(prepare_kernel, count, parts, groups),
        out_shape=pieces
        + [
            jax.ShapeDtypeStruct((rows, slots * PAGE), jnp.float32),
            jax.ShapeDtypeStruct((members, 128), jnp.int32),
        ],
        in_specs=[SM, VM] + [HBM] * (2 + count + len(first)),
        out_specs=[VM] * (parts + 2),
        scratch_shapes=[
            pltpu.VMEM((members, wide), jnp.int32),
            pltpu.VMEM((rows, wide), jnp.float32),
            pltpu.VMEM((rows, wide), jnp.float32),
            pltpu.SMEM(lengths.shape, lengths.dtype),
            pltpu.VMEM(tables.shape, tables.dtype),
            pltpu.SemaphoreType.DMA((parts + 2,)),
        ],
        compiler_params=pltpu.CompilerParams(vmem_limit_bytes=13 * MIB),
        cost_estimate=pl.CostEstimate(flops=0, bytes_accessed=moved, transcendentals=0),
        name="prepare",
    )(place, listed, *[in_hbm(x) for x in (lengths, tables, *weights, *first)])


def attend_kernel(members, steps, chunks, place, landing, old_pool, bias, new_k, new_v, *refs):
    asked, refs = refs[:steps], refs[steps:]
    arrived, refs = refs[:-8], refs[-8:]
    kv_out, keep, give, late, pool, spare, scores, sems = refs
    member, half = place[0], place[1]
    slots = pool.shape[0]
    resident = slots - ARRIVE
    per_peer = ARRIVE // members
    rows = bias.shape[0]
    count = rows * steps * GQ
    pool[resident:] = jnp.zeros((ARRIVE, *pool.shape[1:]), pool.dtype)

    def place_pages(which):
        for i, k in chunks[which]:
            source = lax.rem(member - k + members, members)

            @pl.loop(0, per_peer, unroll=math.gcd(per_peer, 8))
            def _(c):
                pool[resident + landing[source, c]] = arrived[i][c]

    spare_in = pltpu.make_async_copy(old_pool, spare, sems.at[0])
    spare_out = pltpu.make_async_copy(spare, kv_out, sems.at[1])

    late_copies = [
        pltpu.make_async_copy(
            arrived[i], late.at[pl.ds(n * per_peer, per_peer)], sems.at[2 + n]
        )
        for n, (i, _) in enumerate(chunks[0])
    ]

    @pl.when(half == 0)
    def _():
        spare_in.start()
        for copy in late_copies:
            copy.start()
        pool[:resident] = jnp.zeros((resident, *pool.shape[1:]), pool.dtype)
        place_pages(0)
        spare_in.wait()
        spare_out.start()

    @pl.when(half == 1)
    def _():
        copy = pltpu.make_async_copy(
            old_pool.at[pl.ds(0, resident)], pool.at[pl.ds(0, resident)], sems.at[0]
        )
        copy.start()
        place_pages(1)
        copy.wait()
        pltpu.make_async_copy(pool, kv_out, sems.at[1]).start()

    scale = 1.0 / math.sqrt(HD)
    q = jnp.concatenate(
        [ask[:, j * HD : (j + 1) * HD] for j in range(GQ) for ask in asked], axis=0
    )
    nt = (((1,), (1,)), ((), ()))
    group = 24
    width = group * PAGE
    lanes = 128
    fresh = lax.dot_general(q, new_k[...], nt, preferred_element_type=jnp.float32) * scale
    q_id = lax.broadcasted_iota(jnp.int32, fresh.shape, 0)
    t_id = lax.broadcasted_iota(jnp.int32, fresh.shape, 1)
    allowed = (q_id % rows == t_id // steps) & (t_id % steps <= (q_id // rows) % steps)
    fresh = jnp.where(allowed & (half == 1), fresh, -jnp.inf)
    peak = fresh
    for c in range(slots // group):
        keys = pool[c * group : (c + 1) * group, 0].reshape(width, HD)
        s = lax.dot_general(q, keys, nt, preferred_element_type=jnp.float32) * scale
        b = bias[:, c * width : (c + 1) * width]
        s = (s.reshape(count // rows, rows, width) + b[None]).reshape(count, width)
        scores[:, c * width : (c + 1) * width] = s
        for i in range(width // lanes):
            peak = jnp.maximum(peak, s[:, i * lanes : (i + 1) * lanes])
    top = jnp.maximum(jnp.max(peak, axis=1, keepdims=True), -1e30)
    p = jnp.exp(fresh - top)
    total = p
    acc = jnp.dot(p.astype(jnp.bfloat16), new_v[...], preferred_element_type=jnp.float32)
    for c in range(slots // group):
        p = jnp.exp(scores[:, c * width : (c + 1) * width] - top)
        for i in range(width // lanes):
            total = total + p[:, i * lanes : (i + 1) * lanes]
        values = pool[c * group : (c + 1) * group, 1].reshape(width, HD)
        acc = acc + jnp.dot(p.astype(jnp.bfloat16), values, preferred_element_type=jnp.float32)
    total = jnp.sum(total, axis=1, keepdims=True)
    middle = count // 2
    for out, first in ((keep, half == 0), (give, half == 1)):
        out[:, :HD] = jnp.where(first, acc[:middle], acc[middle:])
        out[:, HD : 2 * HD] = jnp.broadcast_to(
            jnp.where(first, top[:middle], top[middle:]), (middle, HD)
        )
        out[:, 2 * HD :] = jnp.broadcast_to(
            jnp.where(first, total[:middle], total[middle:]), (middle, HD)
        )

    @pl.when(half == 1)
    def _():
        pltpu.make_async_copy(pool, kv_out, sems.at[1]).wait()

    @pl.when(half == 0)
    def _():
        spare_out.wait()
        for copy in late_copies:
            copy.wait()


def place_and_attend(place, landing, old_pool, bias, new_k, new_v, asked, arrived, chunks):
    members = landing.shape[0]
    slots = old_pool.shape[0]
    steps = len(asked)
    count = bias.shape[0] * steps * GQ
    part = jax.ShapeDtypeStruct((count // 2, 3 * HD), jnp.float32)
    return pl.pallas_call(
        functools.partial(attend_kernel, members, steps, chunks),
        out_shape=[
            jax.ShapeDtypeStruct(old_pool.shape, old_pool.dtype),
            part,
            part,
            jax.ShapeDtypeStruct((3 * ARRIVE // members, *old_pool.shape[1:]), old_pool.dtype),
        ],
        in_specs=[SM, SM, HBM, VM, VM, VM] + [VM] * (steps + len(arrived)),
        out_specs=[HBM, VM, VM, HBM],
        scratch_shapes=[
            pltpu.VMEM(old_pool.shape, old_pool.dtype),
            pltpu.VMEM(old_pool.shape, old_pool.dtype),
            pltpu.VMEM((count, slots * PAGE), jnp.float32),
            pltpu.SemaphoreType.DMA((5,)),
        ],
        compiler_params=pltpu.CompilerParams(vmem_limit_bytes=12 * MIB),
        name="place_attend",
    )(place, landing, in_hbm(old_pool), bias, new_k, new_v, *asked, *arrived)


def combine_kernel(mine, other, out):
    tokens = out.shape[0]
    for j in range(out.shape[1] // HD):
        rows = slice(j * tokens, (j + 1) * tokens)
        a, b = mine[rows, :], other[rows, :]
        top_a, top_b = a[:, HD : 2 * HD], b[:, HD : 2 * HD]
        top = jnp.maximum(top_a, top_b)
        scale_a, scale_b = jnp.exp(top_a - top), jnp.exp(top_b - top)
        total = a[:, 2 * HD :] * scale_a + b[:, 2 * HD :] * scale_b
        value = (a[:, :HD] * scale_a + b[:, :HD] * scale_b) / total
        out[:, j * HD : (j + 1) * HD] = value.astype(out.dtype)


def combine(mine, other, tokens):
    return pl.pallas_call(
        combine_kernel,
        out_shape=jax.ShapeDtypeStruct((tokens, GQ // 2 * HD), jnp.bfloat16),
        in_specs=[VM, VM],
        out_specs=VM,
        compiler_params=pltpu.CompilerParams(vmem_limit_bytes=2 * MIB),
        name="combine",
    )(mine, other)


def project_kernel(groups, place, weight, stream, mine, sibling, res_out):
    half = place[1]
    members, tokens, width = mine.shape
    sums = [stream[g * tokens : (g + 1) * tokens].astype(jnp.float32) for g in range(groups)]
    for h in range(KVH):
        for g in range(groups):
            m = h * groups + g
            first = jnp.where(half == 0, mine[m], sibling[m])
            second = jnp.where(half == 0, sibling[m], mine[m])
            sums[g] = sums[g] + lax.dot_general(
                jnp.concatenate([first, second], axis=1),
                weight[:, 2 * h * width : 2 * (h + 1) * width],
                (((1,), (1,)), ((), ())),
                preferred_element_type=jnp.float32,
            )
    for g in range(groups):
        res_out[g * tokens : (g + 1) * tokens] = sums[g].astype(res_out.dtype)


def project(place, weight, stream, mine, sibling, groups):
    return pl.pallas_call(
        functools.partial(project_kernel, groups),
        out_shape=jax.ShapeDtypeStruct(stream.shape, jnp.bfloat16),
        in_specs=[SM, VM, VM, VM, VM],
        out_specs=VM,
        compiler_params=pltpu.CompilerParams(vmem_limit_bytes=4 * MIB),
        name="out_projection",
    )(place, in_vmem(weight), stream, mine, sibling)


def ffn_kernel(place, mine, sibling, gain, gate, *refs):
    up, refs = refs[:SPLIT], refs[SPLIT:]
    down, own_out, other_out, down_buf, normed, hidden, down_sem = refs
    half = place[1]
    members, tokens, width = mine.shape
    depth, hidden_count = up[0].shape
    features = depth * SPLIT
    down_copies = []
    for t in range(members):
        cols = pl.ds(t * 2 * width, 2 * width)
        down_copies.append(
            pltpu.make_async_copy(down.at[:, cols], down_buf.at[:, cols], down_sem.at[t])
        )
        down_copies[-1].start()

    square = jnp.zeros((tokens, width), jnp.float32)
    for block in (mine, sibling):
        for t in range(members):
            x = block[t].astype(jnp.float32)
            square = square + x * x
    factor = lax.rsqrt(jnp.sum(square, axis=1, keepdims=True) / features + 1e-05)
    for t in range(members):
        first = jnp.where(half == 0, mine[t], sibling[t])
        second = jnp.where(half == 0, sibling[t], mine[t])
        x = jnp.concatenate([first, second], axis=1).astype(jnp.float32)
        cols = slice(2 * t * width, 2 * (t + 1) * width)
        normed[:, cols] = (x * factor * gain[cols][None, :]).astype(jnp.bfloat16)
    tile = min(1024, hidden_count)
    for f in range(hidden_count // tile):
        cols = slice(f * tile, (f + 1) * tile)
        gate_act = jnp.dot(normed[...], gate[:, cols], preferred_element_type=jnp.float32)
        up_act = 0.0
        for i in range(SPLIT):
            x = normed[:, i * depth : (i + 1) * depth]
            up_act += jnp.dot(x, up[i][:, cols], preferred_element_type=jnp.float32)
        h = gate_act / (1.0 + jnp.exp(-gate_act)) * up_act
        hidden[:, cols] = h.astype(jnp.bfloat16)
    for t in range(members):
        down_copies[t].wait()
        part = jnp.dot(
            hidden[...],
            down_buf[:, 2 * t * width : 2 * (t + 1) * width],
            preferred_element_type=jnp.float32,
        )
        first, second = part[:, :width], part[:, width:]
        own_out[t] = jnp.where(half == 0, first, second)
        other_out[t] = jnp.where(half == 0, second, first).astype(jnp.bfloat16)


def feed_forward(place, mine, sibling, gain, gate, up, down):
    tokens = mine.shape[1]
    hidden_count, features = down.shape
    return pl.pallas_call(
        ffn_kernel,
        out_shape=[
            jax.ShapeDtypeStruct(mine.shape, jnp.float32),
            jax.ShapeDtypeStruct(mine.shape, jnp.bfloat16),
        ],
        in_specs=[SM, VM, VM, VM] + [VM] * (1 + SPLIT) + [HBM],
        out_specs=[VM, VM],
        scratch_shapes=[
            pltpu.VMEM(down.shape, down.dtype),
            pltpu.VMEM((tokens, features), jnp.bfloat16),
            pltpu.VMEM((tokens, hidden_count), jnp.bfloat16),
            pltpu.SemaphoreType.DMA((mine.shape[0],)),
        ],
        compiler_params=pltpu.CompilerParams(vmem_limit_bytes=19 * MIB),
        name="feed_forward",
    )(place, mine, sibling, gain, *map(in_vmem, (gate, *up)), in_hbm(down))


def late_kernel(members, place, landing, late, _, __, kv_out, sems):
    member, half = place[0], place[1]
    per_peer = ARRIVE // members
    resident = kv_out.shape[0] - ARRIVE

    def page(i, k, c):
        source = lax.rem(member - k + members, members)
        spot = i * per_peer + c
        return pltpu.make_async_copy(
            late.at[spot], kv_out.at[resident + landing[source, c]], sems.at[spot]
        )

    chunks = [(0, 0), (1, 1), (2, members - 1)]

    @pl.when(half == 1)
    def _():
        for i, k in chunks:

            @pl.loop(0, per_peer, unroll=math.gcd(per_peer, 8))
            def _(c):
                page(i, k, c).start()

        for i, k in chunks:

            @pl.loop(0, per_peer, unroll=math.gcd(per_peer, 8))
            def _(c):
                page(i, k, c).wait()


def place_late(place, landing, late, after, kv):
    return pl.pallas_call(
        functools.partial(late_kernel, landing.shape[0]),
        out_shape=jax.ShapeDtypeStruct(kv.shape, kv.dtype),
        in_specs=[SM, SM, VM, ANY, HBM],
        out_specs=HBM,
        scratch_shapes=[pltpu.SemaphoreType.DMA((late.shape[0],))],
        input_output_aliases={4: 0},
        compiler_params=pltpu.CompilerParams(vmem_limit_bytes=2 * MIB),
        name="place_late",
    )(place, landing, late, after, in_hbm(kv))


def local(
    kv_pages,
    page_list,
    block_tables,
    lengths,
    queries,
    fresh_kv,
    stream,
    out_proj,
    norm_gain,
    gate_weight,
    up_weight,
    down_weight,
):
    members = lax.axis_size("tp")
    member = lax.axis_index("tp")
    half = lax.axis_index("pd")
    place = jnp.stack([member, half]).astype(jnp.int32)
    slots = kv_pages.shape[0]
    per_peer = ARRIVE // members
    groups = members // KVH
    rows = block_tables.shape[0]
    steps = queries.shape[1]
    tokens = rows * steps

    def send(x, *hops):
        route = [
            (2 * t + start, 2 * ((t + k) % members) + end)
            for start, k, end in hops
            for t in range(members)
        ]
        return lax.ppermute(x, BOTH, route)

    def swap(x):
        return lax.ppermute(x, "pd", [(0, 1), (1, 0)])

    near, own_chunk, *far = pack(place, page_list, kv_pages)
    far = dict(zip(range(2, members - 1), far))
    crossed = lax.ppermute(near, "pd", [(0, 1)])
    behind, ahead = crossed[:per_peer], crossed[per_peer:]
    hosts = (2, members - 2)
    middle = sorted(set(far) - set(hosts), key=lambda k: abs(k - members // 2))
    arrived = {k: send(far[k], (0, k, 1)) for k in middle}
    for host, k, block in zip(hosts, (1, -1), (ahead, behind)):
        block = jnp.where(half == 0, far[host], block)
        arrived[host] = send(block, (0, host, 1), (1, k, 0))

    *held, bias, landing = prepare(
        place,
        lengths,
        block_tables,
        page_list.reshape(members, slots),
        groups,
        ((out_proj, 1), (up_weight, SPLIT)),
        (near,),
    )

    order = sorted(arrived)
    arrays = [own_chunk] + [arrived[k] for k in order]
    chunks = (
        [(0, 0)] + [(1 + order.index(host), k % members) for host, k in zip(hosts, (1, -1))],
        [(1 + i, k) for i, k in enumerate(order)],
    )
    padding = ((0, -tokens % 128), (0, 0))
    new_k = jnp.pad(fresh_kv[:, :, 0].reshape(tokens, HD), padding)
    new_v = jnp.pad(fresh_kv[:, :, 1].reshape(tokens, HD), padding)
    asked = [queries[:, st] for st in range(steps)]
    kv_part, keep, give, late = place_and_attend(
        place, landing, kv_pages, bias, new_k, new_v, asked, arrays, chunks
    )
    late = lax.ppermute(late, "pd", [(0, 1)])

    def all_members(x):
        spread = jnp.broadcast_to(x[None], (members, *x.shape))
        return lax.all_to_all(spread, "tp", split_axis=0, concat_axis=0)

    att_mine = combine(keep, swap(give), tokens)
    here = all_members(att_mine)
    there = swap(here)

    inner = stream.reshape(steps, groups, rows, -1).transpose(1, 0, 2, 3).reshape(stream.shape)
    residual = project(place, held[0], inner, here, there, groups)

    mine = all_members(residual)
    kv_after = place_late(place, landing, late, mine, kv_part)
    mine, kv_after = lax.optimization_barrier((mine, kv_after))
    sibling = swap(mine)
    own, other = feed_forward(place, mine, sibling, norm_gain, gate_weight, held[1:], down_weight)
    summed = (own + swap(other).astype(jnp.float32)).astype(jnp.bfloat16)
    shares = lax.all_to_all(summed, "tp", split_axis=0, concat_axis=0)
    layer = residual.astype(jnp.float32) + jnp.sum(shares.astype(jnp.float32), axis=0)
    layer_out = (
        layer.astype(jnp.bfloat16)
        .reshape(groups, steps, rows, -1)
        .transpose(1, 0, 2, 3)
        .reshape(stream.shape)
    )
    return (kv_after, layer_out)


def solution(mesh):
    return jax.shard_map(
        local,
        mesh=mesh,
        in_specs=(
            P(("grp", "tp", "pd"), None, None, None),
            P("grp"),
            P(("grp", "tp"), None),
            P("grp"),
            P(("grp", "tp"), None, None),
            P(("grp", "tp"), None, None, None),
            P("grp", ("tp", "pd")),
            P(("tp", "pd"), None),
            P(),
            P(None, ("tp", "pd")),
            P(None, ("tp", "pd")),
            P(("tp", "pd"), None),
        ),
        out_specs=(P(("grp", "tp", "pd"), None, None, None), P("grp", ("tp", "pd"))),
        check_vma=False,
    )
```

```python
import functools
import math

import jax
import jax.numpy as jnp
from jax import lax
from jax.experimental import pallas as pl
from jax.experimental.pallas import tpu as pltpu
from jax.sharding import PartitionSpec as P

HD = 128
KVH = 8
GQ = 8
PAGE = 16
REQ_DEV = 2
NEWP = 128
ARRIVE = REQ_DEV * NEWP
MIB = 1024 * 1024
BOTH = ("tp", "pd")
SPLIT = 4

VM = pl.BlockSpec(memory_space=pltpu.VMEM)
SM = pl.BlockSpec(memory_space=pltpu.SMEM)
ANY = pl.BlockSpec(memory_space=pl.ANY)
HBM = pl.BlockSpec(memory_space=pltpu.HBM)


def in_vmem(x):
    return pltpu.with_memory_space_constraint(x, pltpu.VMEM)


def in_hbm(x):
    return pltpu.with_memory_space_constraint(x, pltpu.HBM)


def pack_kernel(members, place, pages, pool, *refs):
    count = members - 1
    outs = refs[:count]
    packed, held, own, counts, sems, load_sems = refs[count:]
    member, half = place[0], place[1]
    slots = pool.shape[0]
    per_peer = ARRIVE // members
    parts = 4
    step = slots // parts

    @pl.when(half == 0)
    def _():
        own_copy = pltpu.make_async_copy(pages, own, load_sems.at[parts])
        own_copy.start()
        loads = []
        for i in range(parts):
            window = pl.ds(i * step, step)
            loads.append(
                pltpu.make_async_copy(pool.at[window], held.at[window], load_sems.at[i])
            )
            loads[-1].start()
        own_copy.wait()
        start = member * slots

        if members in (4, 8):
            carry = (jnp.int32(0), jnp.int32(0))
            for i in range(parts):
                loads[i].wait()

                def body(j, words, base=i * step):
                    low, high = words
                    entry = own[start + base + j]
                    ahead = ((entry >> 8) - member + 1) & (members - 1)
                    leaves = entry >= 0
                    shift = (ahead & 3) * 8
                    is_low = ahead < 4
                    count = (jnp.where(is_low, low, high) >> shift) & 255
                    one = jnp.where(leaves, jnp.int32(1) << shift, 0)
                    packed[jnp.where(leaves, ahead * per_peer + count, ARRIVE)] = held[base + j]
                    return (
                        low + jnp.where(is_low, one, 0),
                        high + jnp.where(is_low, 0, one),
                    )

                carry = lax.fori_loop(0, step, body, carry, unroll=13)
        else:
            for i in range(parts):
                loads[i].wait()

            @pl.loop(0, members + 1)
            def _(i):
                counts[i] = 0

            @pl.loop(0, slots)
            def _(i):
                entry = own[start + i]
                ahead = lax.rem((entry >> 8) - member + members + 1, members)
                row = jnp.where(entry >= 0, ahead, members)
                count = counts[row]
                counts[row] = count + 1
                packed[jnp.where(entry >= 0, row * per_peer + count, ARRIVE)] = held[i]

        copies = []
        near, own_chunk, *far = outs
        moves = [(near, 0, 0), (near, per_peer, 2), (own_chunk, 0, 1)]
        moves += [(out, 0, 3 + i) for i, out in enumerate(far)]
        for i, (out, first, row) in enumerate(moves):
            copies.append(
                pltpu.make_async_copy(
                    packed.at[pl.ds(row * per_peer, per_peer)],
                    out.at[pl.ds(first, per_peer)],
                    sems.at[i],
                )
            )
            copies[-1].start()
        for copy in copies:
            copy.wait()


def pack(place, pages, pool):
    members = lax.axis_size("tp")
    per_peer = ARRIVE // members
    chunk = pool.shape[1:]
    return pl.pallas_call(
        functools.partial(pack_kernel, members),
        out_shape=[pltpu.HBM((2 * per_peer, *chunk), pool.dtype)]
        + [pltpu.HBM((per_peer, *chunk), pool.dtype)] * (members - 2),
        in_specs=[SM, HBM, HBM],
        out_specs=[HBM] * (members - 1),
        scratch_shapes=[
            pltpu.VMEM((ARRIVE + 1, *chunk), pool.dtype),
            pltpu.VMEM(pool.shape, pool.dtype),
            pltpu.SMEM(pages.shape, jnp.int32),
            pltpu.SMEM((members + 1,), jnp.int32),
            pltpu.SemaphoreType.DMA((members,)),
            pltpu.SemaphoreType.DMA((5,)),
        ],
        compiler_params=pltpu.CompilerParams(vmem_limit_bytes=8 * MIB),
        name="pack_pages",
    )(place, in_hbm(pages), in_hbm(pool))


def prepare_kernel(count, parts, groups, place, listed, lengths_hbm, table_hbm, *refs):
    sources = refs[:count]
    held = refs[len(refs) - 8 - parts : -8]
    bias, landing, entries, whole, part, lengths, table, sems = refs[-8:]
    small = [
        pltpu.make_async_copy(lengths_hbm, lengths, sems.at[parts]),
        pltpu.make_async_copy(table_hbm, table, sems.at[parts + 1]),
    ]
    for copy in small:
        copy.start()
    copies = []
    for source in sources:
        done = 0
        while done < source.shape[0]:
            part_out = held[len(copies)]
            window = pl.ds(done, part_out.shape[0])
            copies.append(
                pltpu.make_async_copy(source.at[window], part_out, sems.at[len(copies)])
            )
            copies[-1].start()
            done += part_out.shape[0]

    member = place[0]
    entries[...] = jnp.full(entries.shape, -1, jnp.int32)
    entries[:, : listed.shape[1]] = listed[...]
    entry = entries[...]
    members, lanes = entry.shape
    per_peer = ARRIVE // members
    wanted = (entry >= 0) & ((entry >> 8) == member)
    before = lax.broadcasted_iota(jnp.int32, (lanes, lanes), 0) < lax.broadcasted_iota(
        jnp.int32, (lanes, lanes), 1
    )
    rank = jnp.dot(
        jnp.where(wanted, 1.0, 0.0).astype(jnp.bfloat16),
        jnp.where(before, 1.0, 0.0).astype(jnp.bfloat16),
        preferred_element_type=jnp.float32,
    ).astype(jnp.int32)
    column = lax.broadcasted_iota(jnp.int32, landing.shape, 1)
    found = jnp.zeros(landing.shape, jnp.int32)
    distance = member - lax.broadcasted_iota(jnp.int32, entry.shape, 0)
    distance = jnp.where(distance < 0, distance + members, distance)
    is_near = (distance <= 1) | (distance == members - 1)
    slot_lane = lax.broadcasted_iota(jnp.int32, entry.shape, 1) - (listed.shape[1] - ARRIVE)
    near = jnp.zeros(entry.shape, jnp.float32)
    for c in range(per_peer):
        slot = jnp.sum(jnp.where(wanted & (rank == c), entry & 255, 0), axis=1, keepdims=True)
        found = jnp.where(column == c, slot, found)
        near = jnp.where(is_near & (slot == slot_lane), 1.0, near)
    landing[...] = found
    near = jnp.max(near, axis=0, keepdims=True)
    present = jnp.where(place[1] == 0, near, 1.0 - near)

    for copy in small:
        copy.wait()
    rows, pages = table.shape
    wide = whole.shape[1]
    base = lax.rem(member, groups) * rows
    columns = table[...].T
    page_id = lax.broadcasted_iota(jnp.int32, (pages, wide), 0)
    slot_id = lax.broadcasted_iota(jnp.int32, (pages, wide), 1)
    row_id = lax.broadcasted_iota(jnp.int32, (rows, 128), 0)
    over = jnp.zeros((rows, 128), jnp.int32)
    for r in range(rows):
        length = lengths[base + r]
        full = length // PAGE
        over = jnp.where(row_id == r, length - full * PAGE, over)
        hit = columns[:, r : r + 1] == slot_id
        in_whole = jnp.where(hit & (page_id < full), 1.0, 0.0)
        in_part = jnp.where(hit & (page_id == full), 1.0, 0.0)
        whole[r : r + 1, :] = jnp.sum(in_whole, axis=0, keepdims=True)
        part[r : r + 1, :] = jnp.sum(in_part, axis=0, keepdims=True)
    whole_b = (whole[...] * present).astype(jnp.bfloat16)
    part_b = (part[...] * present).astype(jnp.bfloat16)
    lane = lax.broadcasted_iota(jnp.int32, (rows, 128), 1)
    inside = (lane % PAGE) < over
    per_block = 128 // PAGE
    slot_in = lax.broadcasted_iota(jnp.int32, (wide, 128), 0)
    lane_in = lax.broadcasted_iota(jnp.int32, (wide, 128), 1) // PAGE
    for i in range(bias.shape[1] // 128):
        expand = jnp.where(slot_in == lane_in + i * per_block, 1.0, 0.0).astype(jnp.bfloat16)
        times = jnp.dot(whole_b, expand, preferred_element_type=jnp.float32)
        extra = jnp.dot(part_b, expand, preferred_element_type=jnp.float32)
        bias[:, i * 128 : (i + 1) * 128] = jnp.log(times + jnp.where(inside, extra, 0.0))

    for copy in copies:
        copy.wait()


def prepare(place, lengths, tables, listed, groups, weights, first):
    rows = tables.shape[0]
    members, slots = listed.shape
    wide = -(-slots // 128) * 128
    moved = sum(w.size * w.dtype.itemsize for w, _ in weights)
    pieces = [
        pltpu.VMEM((w.shape[0] // n, w.shape[1]), w.dtype) for w, n in weights for _ in range(n)
    ]
    weights = [w for w, _ in weights]
    count, parts = len(weights), len(pieces)
    return pl.pallas_call(
        functools.partial(prepare_kernel, count, parts, groups),
        out_shape=pieces
        + [
            jax.ShapeDtypeStruct((rows, slots * PAGE), jnp.float32),
            jax.ShapeDtypeStruct((members, 128), jnp.int32),
        ],
        in_specs=[SM, VM] + [HBM] * (2 + count + len(first)),
        out_specs=[VM] * (parts + 2),
        scratch_shapes=[
            pltpu.VMEM((members, wide), jnp.int32),
            pltpu.VMEM((rows, wide), jnp.float32),
            pltpu.VMEM((rows, wide), jnp.float32),
            pltpu.SMEM(lengths.shape, lengths.dtype),
            pltpu.VMEM(tables.shape, tables.dtype),
            pltpu.SemaphoreType.DMA((parts + 2,)),
        ],
        compiler_params=pltpu.CompilerParams(vmem_limit_bytes=13 * MIB),
        cost_estimate=pl.CostEstimate(flops=0, bytes_accessed=moved, transcendentals=0),
        name="prepare",
    )(place, listed, *[in_hbm(x) for x in (lengths, tables, *weights, *first)])


def attend_kernel(members, steps, chunks, place, landing, old_pool, bias, new_k, new_v, *refs):
    asked, refs = refs[:steps], refs[steps:]
    arrived, refs = refs[:-8], refs[-8:]
    kv_out, keep, give, late, pool, spare, scores, sems = refs
    member, half = place[0], place[1]
    slots = pool.shape[0]
    resident = slots - ARRIVE
    per_peer = ARRIVE // members
    rows = bias.shape[0]
    count = rows * steps * GQ
    pool[resident:] = jnp.zeros((ARRIVE, *pool.shape[1:]), pool.dtype)

    def place_pages(which):
        for i, k in chunks[which]:
            source = lax.rem(member - k + members, members)

            @pl.loop(0, per_peer, unroll=math.gcd(per_peer, 8))
            def _(c):
                pool[resident + landing[source, c]] = arrived[i][c]

    spare_in = pltpu.make_async_copy(old_pool, spare, sems.at[0])
    spare_out = pltpu.make_async_copy(spare, kv_out, sems.at[1])

    late_copies = [
        pltpu.make_async_copy(
            arrived[i], late.at[pl.ds(n * per_peer, per_peer)], sems.at[2 + n]
        )
        for n, (i, _) in enumerate(chunks[0])
    ]

    @pl.when(half == 0)
    def _():
        spare_in.start()
        for copy in late_copies:
            copy.start()
        pool[:resident] = jnp.zeros((resident, *pool.shape[1:]), pool.dtype)
        place_pages(0)
        spare_in.wait()
        spare_out.start()

    @pl.when(half == 1)
    def _():
        copy = pltpu.make_async_copy(
            old_pool.at[pl.ds(0, resident)], pool.at[pl.ds(0, resident)], sems.at[0]
        )
        copy.start()
        place_pages(1)
        copy.wait()
        pltpu.make_async_copy(pool, kv_out, sems.at[1]).start()

    scale = 1.0 / math.sqrt(HD)
    q = jnp.concatenate(
        [ask[:, j * HD : (j + 1) * HD] for j in range(GQ) for ask in asked], axis=0
    )
    nt = (((1,), (1,)), ((), ()))
    group = 24
    width = group * PAGE
    lanes = 128
    fresh = lax.dot_general(q, new_k[...], nt, preferred_element_type=jnp.float32) * scale
    q_id = lax.broadcasted_iota(jnp.int32, fresh.shape, 0)
    t_id = lax.broadcasted_iota(jnp.int32, fresh.shape, 1)
    allowed = (q_id % rows == t_id // steps) & (t_id % steps <= (q_id // rows) % steps)
    fresh = jnp.where(allowed & (half == 1), fresh, -jnp.inf)
    peak = fresh
    for c in range(slots // group):
        keys = pool[c * group : (c + 1) * group, 0].reshape(width, HD)
        s = lax.dot_general(q, keys, nt, preferred_element_type=jnp.float32) * scale
        b = bias[:, c * width : (c + 1) * width]
        s = (s.reshape(count // rows, rows, width) + b[None]).reshape(count, width)
        scores[:, c * width : (c + 1) * width] = s
        for i in range(width // lanes):
            peak = jnp.maximum(peak, s[:, i * lanes : (i + 1) * lanes])
    top = jnp.maximum(jnp.max(peak, axis=1, keepdims=True), -1e30)
    p = jnp.exp(fresh - top)
    total = p
    acc = jnp.dot(p.astype(jnp.bfloat16), new_v[...], preferred_element_type=jnp.float32)
    for c in range(slots // group):
        p = jnp.exp(scores[:, c * width : (c + 1) * width] - top)
        for i in range(width // lanes):
            total = total + p[:, i * lanes : (i + 1) * lanes]
        values = pool[c * group : (c + 1) * group, 1].reshape(width, HD)
        acc = acc + jnp.dot(p.astype(jnp.bfloat16), values, preferred_element_type=jnp.float32)
    total = jnp.sum(total, axis=1, keepdims=True)
    middle = count // 2
    for out, first in ((keep, half == 0), (give, half == 1)):
        out[:, :HD] = jnp.where(first, acc[:middle], acc[middle:])
        out[:, HD : 2 * HD] = jnp.broadcast_to(
            jnp.where(first, top[:middle], top[middle:]), (middle, HD)
        )
        out[:, 2 * HD :] = jnp.broadcast_to(
            jnp.where(first, total[:middle], total[middle:]), (middle, HD)
        )

    @pl.when(half == 1)
    def _():
        pltpu.make_async_copy(pool, kv_out, sems.at[1]).wait()

    @pl.when(half == 0)
    def _():
        spare_out.wait()
        for copy in late_copies:
            copy.wait()


def place_and_attend(place, landing, old_pool, bias, new_k, new_v, asked, arrived, chunks):
    members = landing.shape[0]
    slots = old_pool.shape[0]
    steps = len(asked)
    count = bias.shape[0] * steps * GQ
    part = jax.ShapeDtypeStruct((count // 2, 3 * HD), jnp.float32)
    return pl.pallas_call(
        functools.partial(attend_kernel, members, steps, chunks),
        out_shape=[
            jax.ShapeDtypeStruct(old_pool.shape, old_pool.dtype),
            part,
            part,
            jax.ShapeDtypeStruct((3 * ARRIVE // members, *old_pool.shape[1:]), old_pool.dtype),
        ],
        in_specs=[SM, SM, HBM, VM, VM, VM] + [VM] * (steps + len(arrived)),
        out_specs=[HBM, VM, VM, HBM],
        scratch_shapes=[
            pltpu.VMEM(old_pool.shape, old_pool.dtype),
            pltpu.VMEM(old_pool.shape, old_pool.dtype),
            pltpu.VMEM((count, slots * PAGE), jnp.float32),
            pltpu.SemaphoreType.DMA((5,)),
        ],
        compiler_params=pltpu.CompilerParams(vmem_limit_bytes=12 * MIB),
        name="place_attend",
    )(place, landing, in_hbm(old_pool), bias, new_k, new_v, *asked, *arrived)


def combine_kernel(mine, other, out):
    tokens = out.shape[0]
    for j in range(out.shape[1] // HD):
        rows = slice(j * tokens, (j + 1) * tokens)
        a, b = mine[rows, :], other[rows, :]
        top_a, top_b = a[:, HD : 2 * HD], b[:, HD : 2 * HD]
        top = jnp.maximum(top_a, top_b)
        scale_a, scale_b = jnp.exp(top_a - top), jnp.exp(top_b - top)
        total = a[:, 2 * HD :] * scale_a + b[:, 2 * HD :] * scale_b
        value = (a[:, :HD] * scale_a + b[:, :HD] * scale_b) / total
        out[:, j * HD : (j + 1) * HD] = value.astype(out.dtype)


def combine(mine, other, tokens):
    return pl.pallas_call(
        combine_kernel,
        out_shape=jax.ShapeDtypeStruct((tokens, GQ // 2 * HD), jnp.bfloat16),
        in_specs=[VM, VM],
        out_specs=VM,
        compiler_params=pltpu.CompilerParams(vmem_limit_bytes=2 * MIB),
        name="combine",
    )(mine, other)


def project_kernel(groups, place, weight, stream, mine, sibling, res_out):
    half = place[1]
    members, tokens, width = mine.shape
    sums = [stream[g * tokens : (g + 1) * tokens].astype(jnp.float32) for g in range(groups)]
    for h in range(KVH):
        for g in range(groups):
            m = h * groups + g
            first = jnp.where(half == 0, mine[m], sibling[m])
            second = jnp.where(half == 0, sibling[m], mine[m])
            sums[g] = sums[g] + lax.dot_general(
                jnp.concatenate([first, second], axis=1),
                weight[:, 2 * h * width : 2 * (h + 1) * width],
                (((1,), (1,)), ((), ())),
                preferred_element_type=jnp.float32,
            )
    for g in range(groups):
        res_out[g * tokens : (g + 1) * tokens] = sums[g].astype(res_out.dtype)


def project(place, weight, stream, mine, sibling, groups):
    return pl.pallas_call(
        functools.partial(project_kernel, groups),
        out_shape=jax.ShapeDtypeStruct(stream.shape, jnp.bfloat16),
        in_specs=[SM, VM, VM, VM, VM],
        out_specs=VM,
        compiler_params=pltpu.CompilerParams(vmem_limit_bytes=4 * MIB),
        name="out_projection",
    )(place, in_vmem(weight), stream, mine, sibling)


def ffn_kernel(place, landing, mine, sibling, gain, gate, *refs):
    up, refs = refs[:SPLIT], refs[SPLIT:]
    down, late, _, own_out, other_out, kv_out = refs[:6]
    down_buf, normed, hidden, down_sem, late_sem = refs[6:]
    member, half = place[0], place[1]
    members, tokens, width = mine.shape
    per_peer = ARRIVE // members
    resident = kv_out.shape[0] - ARRIVE

    def late_copy(i, k, c):
        source = lax.rem(member - k + members, members)
        spot = i * per_peer + c
        return pltpu.make_async_copy(
            late.at[spot], kv_out.at[resident + landing[source, c]], late_sem.at[spot]
        )

    late_chunks = [(0, 0), (1, 1), (2, members - 1)]

    @pl.when(half == 1)
    def _():
        for i, k in late_chunks:

            @pl.loop(0, per_peer, unroll=math.gcd(per_peer, 16))
            def _(c):
                late_copy(i, k, c).start()

    depth, hidden_count = up[0].shape
    features = depth * SPLIT
    down_copies = []
    for t in range(members):
        cols = pl.ds(t * 2 * width, 2 * width)
        down_copies.append(
            pltpu.make_async_copy(down.at[:, cols], down_buf.at[:, cols], down_sem.at[t])
        )
        down_copies[-1].start()

    square = jnp.zeros((tokens, width), jnp.float32)
    for block in (mine, sibling):
        for t in range(members):
            x = block[t].astype(jnp.float32)
            square = square + x * x
    factor = lax.rsqrt(jnp.sum(square, axis=1, keepdims=True) / features + 1e-05)
    for t in range(members):
        first = jnp.where(half == 0, mine[t], sibling[t])
        second = jnp.where(half == 0, sibling[t], mine[t])
        x = jnp.concatenate([first, second], axis=1).astype(jnp.float32)
        cols = slice(2 * t * width, 2 * (t + 1) * width)
        normed[:, cols] = (x * factor * gain[cols][None, :]).astype(jnp.bfloat16)
    tile = min(1024, hidden_count)
    for f in range(hidden_count // tile):
        cols = slice(f * tile, (f + 1) * tile)
        gate_act = jnp.dot(normed[...], gate[:, cols], preferred_element_type=jnp.float32)
        up_act = 0.0
        for i in range(SPLIT):
            x = normed[:, i * depth : (i + 1) * depth]
            up_act += jnp.dot(x, up[i][:, cols], preferred_element_type=jnp.float32)
        h = gate_act / (1.0 + jnp.exp(-gate_act)) * up_act
        hidden[:, cols] = h.astype(jnp.bfloat16)
    for t in range(members):
        down_copies[t].wait()
        part = jnp.dot(
            hidden[...],
            down_buf[:, 2 * t * width : 2 * (t + 1) * width],
            preferred_element_type=jnp.float32,
        )
        first, second = part[:, :width], part[:, width:]
        own_out[t] = jnp.where(half == 0, first, second)
        other_out[t] = jnp.where(half == 0, second, first).astype(jnp.bfloat16)

    @pl.when(half == 1)
    def _():
        for i, k in late_chunks:

            @pl.loop(0, per_peer, unroll=math.gcd(per_peer, 16))
            def _(c):
                late_copy(i, k, c).wait()


def feed_forward(place, landing, mine, sibling, gain, gate, up, down, late, kv):
    tokens = mine.shape[1]
    hidden_count, features = down.shape
    return pl.pallas_call(
        ffn_kernel,
        out_shape=[
            jax.ShapeDtypeStruct(mine.shape, jnp.float32),
            jax.ShapeDtypeStruct(mine.shape, jnp.bfloat16),
            jax.ShapeDtypeStruct(kv.shape, kv.dtype),
        ],
        in_specs=[SM, SM, VM, VM, VM] + [VM] * (1 + SPLIT) + [HBM, VM, HBM],
        out_specs=[VM, VM, HBM],
        input_output_aliases={5 + 1 + SPLIT + 2: 2},
        scratch_shapes=[
            pltpu.VMEM(down.shape, down.dtype),
            pltpu.VMEM((tokens, features), jnp.bfloat16),
            pltpu.VMEM((tokens, hidden_count), jnp.bfloat16),
            pltpu.SemaphoreType.DMA((mine.shape[0],)),
            pltpu.SemaphoreType.DMA((late.shape[0],)),
        ],
        compiler_params=pltpu.CompilerParams(vmem_limit_bytes=19 * MIB),
        name="feed_forward",
    )(
        place,
        landing,
        mine,
        sibling,
        gain,
        *map(in_vmem, (gate, *up)),
        in_hbm(down),
        late,
        in_hbm(kv),
    )


def local(
    kv_pages,
    page_list,
    block_tables,
    lengths,
    queries,
    fresh_kv,
    stream,
    out_proj,
    norm_gain,
    gate_weight,
    up_weight,
    down_weight,
):
    members = lax.axis_size("tp")
    member = lax.axis_index("tp")
    half = lax.axis_index("pd")
    place = jnp.stack([member, half]).astype(jnp.int32)
    slots = kv_pages.shape[0]
    per_peer = ARRIVE // members
    groups = members // KVH
    rows = block_tables.shape[0]
    steps = queries.shape[1]
    tokens = rows * steps

    def send(x, *hops):
        route = [
            (2 * t + start, 2 * ((t + k) % members) + end)
            for start, k, end in hops
            for t in range(members)
        ]
        return lax.ppermute(x, BOTH, route)

    def swap(x):
        return lax.ppermute(x, "pd", [(0, 1), (1, 0)])

    near, own_chunk, *far = pack(place, page_list, kv_pages)
    far = dict(zip(range(2, members - 1), far))
    crossed = lax.ppermute(near, "pd", [(0, 1)])
    behind, ahead = crossed[:per_peer], crossed[per_peer:]
    hosts = (2, members - 2)
    middle = sorted(set(far) - set(hosts), key=lambda k: abs(k - members // 2))
    arrived = {k: send(far[k], (0, k, 1)) for k in middle}
    for host, k, block in zip(hosts, (1, -1), (ahead, behind)):
        block = jnp.where(half == 0, far[host], block)
        arrived[host] = send(block, (0, host, 1), (1, k, 0))

    *held, bias, landing = prepare(
        place,
        lengths,
        block_tables,
        page_list.reshape(members, slots),
        groups,
        ((out_proj, 1), (up_weight, SPLIT)),
        (near,),
    )

    order = sorted(arrived)
    arrays = [own_chunk] + [arrived[k] for k in order]
    chunks = (
        [(0, 0)] + [(1 + order.index(host), k % members) for host, k in zip(hosts, (1, -1))],
        [(1 + i, k) for i, k in enumerate(order)],
    )
    padding = ((0, -tokens % 128), (0, 0))
    new_k = jnp.pad(fresh_kv[:, :, 0].reshape(tokens, HD), padding)
    new_v = jnp.pad(fresh_kv[:, :, 1].reshape(tokens, HD), padding)
    asked = [queries[:, st] for st in range(steps)]
    kv_part, keep, give, late = place_and_attend(
        place, landing, kv_pages, bias, new_k, new_v, asked, arrays, chunks
    )
    late = lax.ppermute(late, "pd", [(0, 1)])

    def everywhere(x):
        spread = jnp.broadcast_to(x[None], (members, *x.shape))
        mine = lax.all_to_all(spread, "tp", split_axis=0, concat_axis=0)
        return mine, swap(mine)

    att_mine = combine(keep, swap(give), tokens)
    here, there = everywhere(att_mine)

    inner = stream.reshape(steps, groups, rows, -1).transpose(1, 0, 2, 3).reshape(stream.shape)
    residual = project(place, held[0], inner, here, there, groups)

    mine, sibling = everywhere(residual)
    own, other, kv_after = feed_forward(
        place, landing, mine, sibling, norm_gain, gate_weight, held[1:], down_weight, late, kv_part
    )
    summed = (own + swap(other).astype(jnp.float32)).astype(jnp.bfloat16)
    shares = lax.all_to_all(summed, "tp", split_axis=0, concat_axis=0)
    layer = residual.astype(jnp.float32) + jnp.sum(shares.astype(jnp.float32), axis=0)
    layer_out = (
        layer.astype(jnp.bfloat16)
        .reshape(groups, steps, rows, -1)
        .transpose(1, 0, 2, 3)
        .reshape(stream.shape)
    )
    return (kv_after, layer_out)


def solution(mesh):
    return jax.shard_map(
        local,
        mesh=mesh,
        in_specs=(
            P(("grp", "tp", "pd"), None, None, None),
            P("grp"),
            P(("grp", "tp"), None),
            P("grp"),
            P(("grp", "tp"), None, None),
            P(("grp", "tp"), None, None, None),
            P("grp", ("tp", "pd")),
            P(("tp", "pd"), None),
            P(),
            P(None, ("tp", "pd")),
            P(None, ("tp", "pd")),
            P(("tp", "pd"), None),
        ),
        out_specs=(P(("grp", "tp", "pd"), None, None, None), P("grp", ("tp", "pd"))),
        check_vma=False,
    )
```
